32 devices in a mesh: seq: 4 (over y, core), ctx: 8 (over z, x).
Axes of the slice: x: 2, y: 2, z: 4, core: 2. Of those that a mesh axis runs over, the one named last changes fastest.
Arguments:
- hidden: bfloat16 [4, 2048, 2048], P('seq', 'ctx'), may hold values from -6 to 6
- out_grad: bfloat16 [4, 2048, 2048], P('seq', 'ctx'), may hold values from -6 to 6
- norm_first: float32 [2048], replicated, may hold values from 0.5 to 1.5
- norm_second: float32 [2048], replicated, may hold values from 0.5 to 1.5
- joint_weight: bfloat16 [2048, 4096], P(('seq', 'ctx')), may hold values from -0.125 to 0.125
- out_weight: bfloat16 [2048, 2048], P(('seq', 'ctx')), may hold values from -0.5 to 0.5
- gate_weight: bfloat16 [2048, 8192], P(('seq', 'ctx')), may hold values from -0.125 to 0.125
- up_weight: bfloat16 [2048, 8192], P(('seq', 'ctx')), may hold values from -0.125 to 0.125
- down_weight: bfloat16 [8192, 2048], P(('seq', 'ctx')), may hold values from -0.0625 to 0.0625
- joint_left: bfloat16 [8, 2048, 16], replicated, may hold values from -0.125 to 0.125
- joint_right: bfloat16 [8, 16, 4096], replicated, may hold values from -1.5 to 1.5
- out_left: bfloat16 [8, 2048, 16], replicated, may hold values from -0.5 to 0.5
- out_right: bfloat16 [8, 16, 2048], replicated, may hold values from -1.5 to 1.5
- gate_left: bfloat16 [8, 2048, 16], replicated, may hold values from -0.125 to 0.125
- gate_right: bfloat16 [8, 16, 8192], replicated, may hold values from -1.5 to 1.5
- up_left: bfloat16 [8, 2048, 16], replicated, may hold values from -0.125 to 0.125
- up_right: bfloat16 [8, 16, 8192], replicated, may hold values from -1.5 to 1.5
- down_left: bfloat16 [8, 8192, 16], replicated, may hold values from -0.0625 to 0.0625
- down_right: bfloat16 [8, 16, 2048], replicated, may hold values from -1.5 to 1.5
- doc_lengths: int32 [4, 6], P('seq'), may hold values from 1 to 1536, as said below
- adapter_ids: int32 [4], P('seq'), may hold values from 0 to 7
Outputs:
- layer_output: bfloat16 [4, 2048, 2048], P('seq', 'ctx')
- input_delta: bfloat16 [4, 2048, 2048], P('seq', 'ctx')
- delta_joint_left: float32 [8, 2048, 16], replicated
- delta_joint_right: float32 [8, 16, 4096], replicated
- delta_out_left: float32 [8, 2048, 16], replicated
- delta_out_right: float32 [8, 16, 2048], replicated
- delta_gate_left: float32 [8, 2048, 16], replicated
- delta_gate_right: float32 [8, 16, 8192], replicated
- delta_up_left: float32 [8, 2048, 16], replicated
- delta_up_right: float32 [8, 16, 8192], replicated
- delta_down_left: float32 [8, 8192, 16], replicated
- delta_down_right: float32 [8, 16, 2048], replicated
The draws below stay inside these ranges and needn't reach their ends.
Inputs may be any that keep to these rules, and one draw needn't show every extreme that they name: `doc_lengths`: the lengths of each sequence sum to 2048; its first document holds 1536 tokens.
All inputs are finite; a program needn't handle non-finite values.
Results may differ from the reference program's by a relative error of at most 0.02.
Values may be sent and summed in bfloat16 or wider, within the bound.
No kernel may reach another device: no remote copies, remote signals or barrier semaphores. Data moves between devices by JAX's collectives and lax.ppermute only.
A program may use at most 320 MiB of HBM per device.

```python
import jax
import jax.numpy as jnp
from jax import lax

D = 2048
HEADS = 16
KV_HEADS = 8
HEAD_DIM = 128
FF = 8192
RANK = 16
ADAPTERS = 8
WINDOW = 1024
DOCS = 6
SEQ_LEN = 2048
SEQS = 4
QKV = 4096
N_CTX = 8


def draw_doc_lengths(key, part):
    key = jax.random.fold_in(key, 11)
    first_length = SEQ_LEN - SEQ_LEN // 4
    remain = SEQ_LEN - first_length
    shares = jax.random.randint(key, (SEQS, DOCS - 1), 1, 5, dtype=jnp.int32)
    share_total = jnp.sum(shares, axis=1, keepdims=True)
    pieces = remain * shares // share_total
    pieces = pieces.at[:, -1].add(remain - jnp.sum(pieces, axis=1))
    leading = jnp.full((SEQS, 1), first_length, jnp.int32)
    return jnp.concatenate([leading, pieces], axis=1).astype(jnp.int32)


def place_ends(values, own_key, smallest, top_value):
    shape = values.shape
    index_at = [jax.random.randint(jax.random.fold_in(own_key, axis), (), 0, shape[axis]) for axis in range(len(shape))]
    values = values.at[tuple(index_at)].set(smallest)
    longest = shape.index(max(shape))
    index_at[longest] = (index_at[longest] + 1) % shape[longest]
    return values.at[tuple(index_at)].set(top_value)


def block_scale(stream_key, extent, shards, least, largest):
    loudness = 1.0
    for position, blocks in shards:
        heights = jax.random.uniform(jax.random.fold_in(jax.random.fold_in(stream_key, 6), position), (blocks,), jnp.float32, least / len(shards), largest / len(shards))
        loudness = loudness * jnp.repeat(jnp.exp(heights), extent[position] // blocks).reshape((-1,) + (1,) * (len(extent) - 1 - position))
    return loudness


def gaussian(key, extent, spread, reach, shards=(), held_as=jnp.bfloat16):
    values = spread * jax.random.normal(key, extent, jnp.float32)
    if shards:
        values = values * block_scale(key, extent, shards, -0.22, 0.18)
    return jnp.clip(values, -reach, reach).astype(held_as)


def setup_inputs(seed: int = 0) -> dict:
    splits = jax.random.split(jax.random.key(seed), 22)
    hidden = gaussian(splits[0], (SEQS, SEQ_LEN, D), 1.0, 6.0, ((0, 4), (1, 8)))
    out_grad = gaussian(splits[1], (SEQS, SEQ_LEN, D), 1.0, 6.0, ((0, 4), (1, 8)))
    norm_first = jnp.clip(1.0 + 0.1 * jax.random.normal(splits[2], (D,), jnp.float32), 0.5, 1.5)
    norm_second = jnp.clip(1.0 + 0.1 * jax.random.normal(splits[3], (D,), jnp.float32), 0.5, 1.5)
    joint_weight = gaussian(splits[4], (D, QKV), D ** -0.5, 0.125, ((0, 32),))
    out_weight = gaussian(splits[5], (D, D), (D // 16) ** -0.5, 0.5, ((0, 32),))
    gate_weight = gaussian(splits[6], (D, FF), D ** -0.5, 0.125, ((0, 32),))
    up_weight = gaussian(splits[7], (D, FF), D ** -0.5, 0.125, ((0, 32),))
    down_weight = gaussian(splits[8], (FF, D), FF ** -0.5, 0.0625, ((0, 32),))
    joint_left = gaussian(splits[9], (ADAPTERS, D, RANK), D ** -0.5, 0.125)
    joint_right = gaussian(splits[10], (ADAPTERS, RANK, QKV), RANK ** -0.5, 1.5)
    out_left = gaussian(splits[11], (ADAPTERS, D, RANK), (D // 16) ** -0.5, 0.5)
    out_right = gaussian(splits[12], (ADAPTERS, RANK, D), RANK ** -0.5, 1.5)
    gate_left = gaussian(splits[13], (ADAPTERS, D, RANK), D ** -0.5, 0.125)
    gate_right = gaussian(splits[14], (ADAPTERS, RANK, FF), RANK ** -0.5, 1.5)
    up_left = gaussian(splits[15], (ADAPTERS, D, RANK), D ** -0.5, 0.125)
    up_right = gaussian(splits[16], (ADAPTERS, RANK, FF), RANK ** -0.5, 1.5)
    down_left = gaussian(splits[17], (ADAPTERS, FF, RANK), FF ** -0.5, 0.0625)
    down_right = gaussian(splits[18], (ADAPTERS, RANK, D), RANK ** -0.5, 1.5)
    doc_lengths = draw_doc_lengths(jax.random.fold_in(splits[21], 71), 0)
    adapter_ids = place_ends(jax.random.randint(splits[20], (SEQS,), 0, ADAPTERS), jax.random.fold_in(splits[20], 1), 0, ADAPTERS - 1).astype(jnp.int32)
    return dict(hidden=hidden, out_grad=out_grad, norm_first=norm_first, norm_second=norm_second, joint_weight=joint_weight, out_weight=out_weight, gate_weight=gate_weight, up_weight=up_weight, down_weight=down_weight, joint_left=joint_left, joint_right=joint_right, out_left=out_left, out_right=out_right, gate_left=gate_left, gate_right=gate_right, up_left=up_left, up_right=up_right, down_left=down_left, down_right=down_right, doc_lengths=doc_lengths, adapter_ids=adapter_ids)


@jax.custom_vjp
def low(v):
    return lax.optimization_barrier(v.astype(jnp.bfloat16)).astype(jnp.float32)

@jax.custom_vjp
def low_back(v):
    return v

def low_keep(v):
    return (low(v), None)

def low_pass(kept, grad):
    return (grad,)

def back_keep(v):
    return (v, None)

def back_low(kept, grad):
    return (low(grad),)
low.defvjp(low_keep, low_pass)
low_back.defvjp(back_keep, back_low)
epsilon = 1e-06
rotary_base = 1000000.0
masked_score = -1e+30
precise = lax.Precision.HIGHEST

def product(left, right):
    return jnp.dot(left, right, precision=precise, preferred_element_type=jnp.float32)

def normed(values, gain):
    return values * lax.rsqrt(lax.optimization_barrier(jnp.mean(values * values, axis=-1, keepdims=True)) + epsilon) * gain

def dealt_places(length, parts):
    row_count = length // parts
    half = row_count // 2
    index = jnp.arange(length, dtype=jnp.int32)
    owner = index // row_count
    within = index % row_count
    return jnp.where(within < half, owner * half + within, length - (owner + 1) * half + within - half).astype(jnp.int32)

def document_of(places, lengths):
    ends = jnp.cumsum(lengths)
    return lax.optimization_barrier(jnp.sum((places[:, None] >= ends[None, :]).astype(jnp.int32), axis=1)).astype(jnp.int32)

def rotary(places):
    inverse = rotary_base ** (-jnp.arange(HEAD_DIM // 2, dtype=jnp.float32) * 2.0 / HEAD_DIM)
    angles = places.astype(jnp.float32)[:, None] * inverse[None, :]
    return (jnp.concatenate([jnp.cos(angles)] * 2, axis=1), jnp.concatenate([jnp.sin(angles)] * 2, axis=1))

def rotate(flat, cosine, sine, heads):
    shaped = flat.reshape(flat.shape[0], heads, HEAD_DIM)
    half = HEAD_DIM // 2
    turned = jnp.concatenate([-shaped[..., half:], shaped[..., :half]], axis=-1)
    return (shaped * cosine[:, None, :] + turned * sine[:, None, :]).reshape(flat.shape[0], heads * HEAD_DIM)

def adapted(inputs, weight, left, right):
    inner = low_back(low(product(inputs, left)))
    return product(inputs, weight) + product(inner, right)

def attend(queries, keys, values, places, documents):
    length = queries.shape[0]
    block = 512 if length % 512 == 0 else length
    count = length // block
    group = HEADS // KV_HEADS
    shaped_keys = keys.reshape(length, KV_HEADS, HEAD_DIM)
    shaped_values = values.reshape(length, KV_HEADS, HEAD_DIM)
    query_blocks = queries.reshape(count, block, KV_HEADS, group, HEAD_DIM)
    place_blocks = places.reshape(count, block)
    document_blocks = documents.reshape(count, block)

    def one_block(key_rows, value_rows, query_rows, query_places, query_documents):
        raw = low_back(jnp.einsum('qkgd,skd->kgqs', query_rows, key_rows, precision=precise))
        scores = raw * HEAD_DIM ** (-0.5)
        distance = query_places[:, None] - places[None, :]
        visible = (query_documents[:, None] == documents[None, :]) & (distance >= 0) & (distance < WINDOW)
        scores = jnp.where(visible[None, None], scores, masked_score)
        weights = low(jax.nn.softmax(scores, axis=-1))
        mixed = jnp.einsum('kgqs,skd->qkgd', weights, value_rows, precision=precise)
        return mixed.reshape(block, HEADS * HEAD_DIM)
    checked = jax.checkpoint(one_block)
    outputs = lax.map(lambda item: checked(shaped_keys, shaped_values, item[0], item[1], item[2]), (query_blocks, place_blocks, document_blocks))
    return outputs.reshape(length, HEADS * HEAD_DIM)

def layer(tokens, factors, weights, places, documents, adapter):
    norm_first, norm_second, joint_weight, out_weight, gate_weight, up_weight, down_weight = weights
    picked = [lax.dynamic_index_in_dim(factor, adapter, 0, keepdims=False) for factor in factors]
    query_width = HEADS * HEAD_DIM
    key_width = KV_HEADS * HEAD_DIM
    first = low(normed(tokens, norm_first))
    joined = low_back(adapted(first, joint_weight, picked[0], picked[1]))
    cosine, sine = rotary(places)
    queries = low(rotate(joined[:, :query_width], cosine, sine, HEADS))
    keys = low(rotate(joined[:, query_width:query_width + key_width], cosine, sine, KV_HEADS))
    values = low(joined[:, query_width + key_width:])
    mixed = low_back(low(attend(queries, keys, values, places, documents)))
    residual = tokens + low_back(adapted(mixed, out_weight, picked[2], picked[3]))
    second = low(normed(residual, norm_second))
    gate = low_back(adapted(second, gate_weight, picked[4], picked[5]))
    up = low_back(adapted(second, up_weight, picked[6], picked[7]))
    activated = low(jax.nn.silu(gate) * up)
    return residual + low_back(adapted(activated, down_weight, picked[8], picked[9]))

def reference(hidden, out_grad, norm_first, norm_second, joint_weight, out_weight, gate_weight, up_weight, down_weight, joint_left, joint_right, out_left, out_right, gate_left, gate_right, up_left, up_right, down_left, down_right, doc_lengths, adapter_ids):
    weights = tuple((weight.astype(jnp.float32) for weight in (norm_first, norm_second, joint_weight, out_weight, gate_weight, up_weight, down_weight)))
    factors = tuple((factor.astype(jnp.float32) for factor in (joint_left, joint_right, out_left, out_right, gate_left, gate_right, up_left, up_right, down_left, down_right)))
    places = dealt_places(SEQ_LEN, N_CTX)

    def one_sequence(totals, item):
        tokens, cotangent, lengths, adapter = item
        documents = document_of(places, lengths)

        def forward(tokens_in, factors_in):
            return layer(tokens_in, factors_in, weights, places, documents, adapter)
        result, pullback = jax.vjp(forward, tokens.astype(jnp.float32), factors)
        token_delta, factor_delta = pullback(cotangent.astype(jnp.float32))
        totals = tuple((total + delta for total, delta in zip(totals, factor_delta)))
        return (totals, (result.astype(jnp.bfloat16), token_delta.astype(jnp.bfloat16)))
    start = tuple((jnp.zeros(factor.shape, jnp.float32) for factor in factors))
    totals, outputs = lax.scan(one_sequence, start, (hidden, out_grad, doc_lengths, adapter_ids))
    return (outputs[0], outputs[1], totals[0], totals[1], totals[2], totals[3], totals[4], totals[5], totals[6], totals[7], totals[8], totals[9])
```

```python
import functools

import jax
import jax.numpy as jnp
from jax import lax
from jax.experimental import pallas as pl
from jax.experimental.pallas import tpu as pltpu
from jax.sharding import Mesh, PartitionSpec as P

HEADS = 16
KV_HEADS = 8
HEAD_DIM = 128
WINDOW = 1024
FIRST_DOC = 1536
RANK = 16
PAD = 128
TP = 4

epsilon = 1e-06
rotary_base = 1000000.0
masked_score = -1e30

BF = jnp.bfloat16
F32 = jnp.float32
MIB = 1024 * 1024


def dot(left, right):
    return jnp.dot(left, right, preferred_element_type=F32)


def dot_t(left, right):
    return lax.dot_general(left, right, (((1,), (1,)), ((), ())), preferred_element_type=F32)


def t_dot(left, right):
    return lax.dot_general(left, right, (((0,), (0,)), ((), ())), preferred_element_type=F32)


def params(mib, grid=0):
    extra = {"dimension_semantics": ("arbitrary",) * grid} if grid else {}
    return pltpu.CompilerParams(vmem_limit_bytes=mib * MIB, **extra)


def cost(flops, nbytes, trans=0):
    return pl.CostEstimate(flops=int(flops), bytes_accessed=int(nbytes), transcendentals=int(trans))


VM = pl.BlockSpec(memory_space=pltpu.VMEM)
SM = pl.BlockSpec(memory_space=pltpu.SMEM)
ANY = pl.BlockSpec(memory_space=pl.ANY)


def half_range(side, h, span, length):
    start = span * h if side == 0 else length - span * (h + 1)
    return (start, start + span)


def may_see(q, k):
    grain = 64
    for q0 in range(q[0], q[1], grain):
        for k0 in range(k[0], k[1], grain):
            same = (q0 >= FIRST_DOC) == (k0 >= FIRST_DOC)
            if same and k0 < q0 + grain and q0 - (k0 + grain - 1) < WINDOW:
                return True
    return False


def key_plan(halves, span, length):
    slots = []
    for shift in list(range(halves - 1, 0, -1)) + list(range(-1, -halves, -1)):
        for side in (0, 1):
            pairs = []
            for h in range(halves):
                source = h - shift
                if not 0 <= source < halves:
                    continue
                wanted = half_range(side, source, span, length)
                if any(may_see(half_range(s, h, span, length), wanted) for s in (0, 1)):
                    pairs.append((source, h))
            if pairs:
                slots.append((shift, side, tuple(pairs)))
    tile = min(256, span)
    step = 128
    ranges = []
    for i in range(2 * span // tile):
        low, high = (1 << 30, 0)
        for h in range(halves):
            side, inside = divmod(i * tile, span)
            base = half_range(side, h, span, length)[0] + inside
            held = []
            for shift, key_side, pairs in slots:
                held.append(
                    half_range(key_side, h - shift, span, length) if (h - shift, h) in pairs else None
                )
            held += [half_range(s, h, span, length) for s in (0, 1)]
            for index, region in enumerate(held):
                if region is None:
                    continue
                for offset in range(0, span, step):
                    block = (region[0] + offset, region[0] + min(offset + step, span))
                    if may_see((base, base + tile), block):
                        low = min(low, index * span + offset)
                        high = max(high, index * span + offset + step)
        ranges.append((low, min(high, (len(slots) + 2) * span)))
    return (slots, tile, ranges)


def place_rows(me, r, rows):
    half = rows // 2
    other = me ^ r
    first = pl.multiple_of(other * half, half)
    second = pl.multiple_of(TP * half + (TP - 1 - other) * half, half)
    return ((0, first), (half, second))


def qkv_kernel(me_ref, x0, x1, x2, x3, w_ref, jr_ref, cos_ref, sin_ref, q_ref, kv_ref):
    me = me_ref[0]
    rows, wide = x0.shape
    d = wide - PAD
    half = rows // 2
    nq = q_ref.shape[1] // HEAD_DIM
    nk = kv_ref.shape[1] // HEAD_DIM // 2
    for r, x_ref in enumerate((x0, x1, x2, x3)):
        joined = dot(x_ref[:, :d], w_ref[...]) + dot(x_ref[:, d:], jr_ref[...])
        for source, target in place_rows(me, r, rows):
            part = joined[source : source + half]
            cosine = cos_ref[pl.ds(target, half), :]
            sine = sin_ref[pl.ds(target, half), :]
            for head in range(nq + nk):
                u = part[:, head * HEAD_DIM : (head + 1) * HEAD_DIM]
                turned = (u * cosine + pltpu.roll(u, HEAD_DIM // 2, 1) * sine).astype(BF)
                if head < nq:
                    q_ref[pl.ds(target, half), head * HEAD_DIM : (head + 1) * HEAD_DIM] = turned
                else:
                    at = head - nq
                    kv_ref[pl.ds(target, half), at * HEAD_DIM : (at + 1) * HEAD_DIM] = turned
            kv_ref[pl.ds(target, half), nk * HEAD_DIM :] = part[:, (nq + nk) * HEAD_DIM :].astype(BF)


def head_columns(ref, rows, first, count):
    return jnp.concatenate(
        [ref[rows, (first + i) * HEAD_DIM : (first + i + 1) * HEAD_DIM] for i in range(count)], axis=0
    )


def bias_of(qpos_ref, kpos_ref, rows, low, high, group):
    distance = qpos_ref[rows, :] - kpos_ref[:, low:high]
    bias = jnp.where((distance >= 0) & (distance < WINDOW), 0.0, masked_score).astype(F32)
    return jnp.concatenate([bias] * group, axis=0)


def attend_kernel(tile, ranges, me_ref, q_ref, kv_ref, qpos_ref, kpos_ref, mixed_ref, lse_ref, held):
    me = me_ref[0]
    rows = mixed_ref.shape[1]
    half = rows // 2
    nk = kv_ref.shape[1] // HEAD_DIM // 2
    group = q_ref.shape[1] // HEAD_DIM // nk
    scale = HEAD_DIM ** (-0.5)
    for i, (low, high) in enumerate(ranges):
        here = slice(i * tile, (i + 1) * tile)
        bias = bias_of(qpos_ref, kpos_ref, here, low, high, group)
        for head in range(nk):
            q = head_columns(q_ref, here, head * group, group)
            k = kv_ref[low:high, head * HEAD_DIM : (head + 1) * HEAD_DIM]
            v = kv_ref[low:high, (nk + head) * HEAD_DIM : (nk + head + 1) * HEAD_DIM]
            scores = dot_t(q, k) * scale + bias
            largest = jnp.max(scores, axis=-1, keepdims=True)
            raised = jnp.exp(scores - largest)
            total = jnp.sum(raised, axis=-1, keepdims=True)
            out = dot((raised * (1.0 / total)).astype(BF), v).astype(BF)
            lse = largest + jnp.log(total)
            for g in range(group):
                at = head * group + g
                held[here, at * HEAD_DIM : (at + 1) * HEAD_DIM] = out[g * tile : (g + 1) * tile]
                lse_ref[here, at : at + 1] = lse[g * tile : (g + 1) * tile]
    for r in range(TP):
        for source, target in place_rows(me, r, rows):
            mixed_ref[r, source : source + half, :] = held[pl.ds(target, half), :]


def attend_back_kernel(
    tile,
    ranges,
    me_ref,
    q_ref,
    kv_ref,
    qpos_ref,
    kpos_ref,
    lse_ref,
    mixed_ref,
    d0,
    d1,
    d2,
    d3,
    cos_ref,
    sin_ref,
    dq_ref,
    dkv_ref,
    dslot_ref,
    held,
    given,
    total_ref,
):
    me = me_ref[0]
    rows = mixed_ref.shape[1]
    half = rows // 2
    nk = kv_ref.shape[1] // HEAD_DIM // 2
    group = q_ref.shape[1] // HEAD_DIM // nk
    scale = HEAD_DIM ** (-0.5)
    for r, d_ref in enumerate((d0, d1, d2, d3)):
        for source, target in place_rows(me, r, rows):
            held[pl.ds(target, half), :] = mixed_ref[r, source : source + half, :]
            given[pl.ds(target, half), :] = d_ref[source : source + half, :]
    total_ref[...] = jnp.zeros_like(total_ref)
    for i, (low, high) in enumerate(ranges):
        here = slice(i * tile, (i + 1) * tile)
        bias = bias_of(qpos_ref, kpos_ref, here, low, high, group)
        cosine = cos_ref[here, :]
        sine = sin_ref[here, :]
        for head in range(nk):
            key_columns = slice(head * HEAD_DIM, (head + 1) * HEAD_DIM)
            value_columns = slice((nk + head) * HEAD_DIM, (nk + head + 1) * HEAD_DIM)
            q = head_columns(q_ref, here, head * group, group)
            out = head_columns(held, here, head * group, group)
            delta = head_columns(given, here, head * group, group)
            lse = jnp.concatenate(
                [lse_ref[here, head * group + g : head * group + g + 1] for g in range(group)], axis=0
            )
            k = kv_ref[low:high, key_columns]
            v = kv_ref[low:high, value_columns]
            chances = jnp.exp(dot_t(q, k) * scale + bias - lse)
            inner = jnp.sum(out.astype(F32) * delta.astype(F32), axis=-1, keepdims=True)
            raw = (chances * (dot_t(delta, v) - inner) * scale).astype(BF)
            dq = dot(raw, k)
            for g in range(group):
                at = head * group + g
                e = dq[g * tile : (g + 1) * tile]
                back = e * cosine - pltpu.roll(e, HEAD_DIM // 2, 1) * sine
                dq_ref[here, at * HEAD_DIM : (at + 1) * HEAD_DIM] = back.astype(BF)
            total_ref[low:high, key_columns] += t_dot(raw, q)
            total_ref[low:high, value_columns] += t_dot(chances.astype(BF), delta)
    extra = dslot_ref.shape[0]
    dslot_ref[...] = total_ref[:extra, :].astype(BF)
    dkv_ref[...] = total_ref[extra:, :]


def out_kernel(
    me_ref, m_ref, w_ref, olt_ref, or_ref, x_ref, gain_ref, lgu_ref, aug_ref, res_ref, oi_ref, acc, inner
):
    r = pl.program_id(0)
    d = x_ref.shape[1]

    @pl.when(r == 0)
    def _():
        acc[...] = x_ref[...].astype(F32)
        inner[...] = jnp.zeros_like(inner)

    m = m_ref[0]
    acc[...] += dot(m, w_ref[...])
    inner[...] += dot_t(m, olt_ref[...])

    @pl.when(r == TP - 1)
    def _():
        low = inner[...].astype(BF)
        oi_ref[...] = low
        residual = acc[...] + dot(low, or_ref[...])
        res_ref[...] = residual
        factor = lax.rsqrt(jnp.mean(residual * residual, axis=-1, keepdims=True) + epsilon)
        second = (residual * factor * gain_ref[...]).astype(BF)
        aug_ref[:, :d] = second
        aug_ref[:, d:] = dot_t(second, lgu_ref[...]).astype(BF)


def out_back_kernel(
    me_ref,
    p0,
    p1,
    p2,
    p3,
    dy_ref,
    res_ref,
    gain_ref,
    or_ref,
    olt_ref,
    oi_ref,
    w_ref,
    m_ref,
    dmix_ref,
    dres_ref,
    tor_ref,
    tol_ref,
    branch,
    inner,
):
    r = pl.program_id(0)

    @pl.when(r == 0)
    def _():
        gain = gain_ref[...]
        incoming = (
            p0[...].astype(F32) + p1[...].astype(F32) + p2[...].astype(F32) + p3[...].astype(F32)
        )
        v = res_ref[...]
        factor = lax.rsqrt(jnp.mean(v * v, axis=-1, keepdims=True) + epsilon)
        scaled = incoming * gain
        back = factor * scaled - v * (factor * factor * factor) * jnp.mean(
            scaled * v, axis=-1, keepdims=True
        )
        delta = dy_ref[...].astype(F32) + back
        dres_ref[...] = delta
        low = delta.astype(BF)
        branch[...] = low
        inner[...] = dot_t(low, or_ref[...]).astype(BF)
        tor_ref[...] = t_dot(oi_ref[...], low)

    dmix_ref[0] = (dot_t(branch[...], w_ref[...]) + dot(inner[...], olt_ref[...])).astype(BF)
    tol_ref[...] = t_dot(inner[...], m_ref[0])


def feed_kernel(
    x0,
    x1,
    x2,
    x3,
    y0,
    y1,
    y2,
    y3,
    gate_ref,
    up_ref,
    down_ref,
    dlt_ref,
    rg_ref,
    ru_ref,
    dr_ref,
    lgu_ref,
    o0,
    o1,
    o2,
    o3,
    s0,
    s1,
    s2,
    s3,
    tdl_ref,
    tgr_ref,
    tur_ref,
    tlast_ref,
    x_all,
    y_all,
    acc_out,
    acc_second,
    acc_inner,
    tails,
    sem,
):
    j = pl.program_id(0)
    rows = x0.shape[0]
    d = acc_out.shape[1]

    @pl.when(j == 0)
    def _():
        copies = []
        for r, ref in enumerate((x0, x1, x2, x3)):
            copies.append(pltpu.make_async_copy(ref, x_all.at[pl.ds(r * rows, rows), :], sem.at[r]))
        for r, ref in enumerate((y0, y1, y2, y3)):
            copies.append(
                pltpu.make_async_copy(ref, y_all.at[pl.ds(r * rows, rows), :], sem.at[TP + r])
            )
        for copy in copies:
            copy.start()
        acc_out[...] = jnp.zeros_like(acc_out)
        acc_second[...] = jnp.zeros_like(acc_second)
        acc_inner[...] = jnp.zeros_like(acc_inner)
        for copy in copies:
            copy.wait()
        tails[...] = x_all[:, d:] + y_all[:, d:]

    block = gate_ref.shape[-1]
    gate_w = gate_ref[...].reshape(d, block)
    up_w = up_ref[...].reshape(d, block)
    down_w = down_ref[...].reshape(block, d)
    dlt, rg, ru = (dlt_ref[...], rg_ref[...], ru_ref[...])
    term_dl = jnp.zeros((PAD, block), F32)
    term_g = jnp.zeros((PAD, block), F32)
    term_u = jnp.zeros((PAD, block), F32)
    take = min(512, TP * rows)
    for start in range(0, TP * rows, take):
        here = slice(start, start + take)
        x = x_all[here, :d]
        y = y_all[here, :d]
        xi = x_all[here, d:]
        yi = y_all[here, d:]
        gate = dot(x, gate_w) + dot(xi, rg)
        up = dot(x, up_w) + dot(xi, ru)
        delta = dot_t(y, down_w) + dot(yi, dlt)
        sigmoid = jax.nn.sigmoid(gate)
        silu = gate * sigmoid
        act = (silu * up).astype(BF)
        delta_gate = (delta * up * sigmoid * (1.0 + gate * (1.0 - sigmoid))).astype(BF)
        delta_up = (delta * silu).astype(BF)
        acc_out[here, :] += dot(act, down_w)
        acc_second[here, :] += dot_t(delta_gate, gate_w) + dot_t(delta_up, up_w)
        acc_inner[here, :] += dot_t(act, dlt) + dot_t(delta_gate, rg) + dot_t(delta_up, ru)
        tail = tails[here, :]
        term_dl += t_dot(tail, act)
        term_g += t_dot(tail, delta_gate)
        term_u += t_dot(tail, delta_up)
    tdl_ref[...] = term_dl[:RANK]
    tgr_ref[...] = term_g[RANK : 2 * RANK]
    tur_ref[...] = term_u[2 * RANK : 3 * RANK]

    @pl.when(j == pl.num_programs(0) - 1)
    def _():
        inner = acc_inner[...].astype(BF)
        term_y = t_dot(inner, y_all[:, :d])
        tlast_ref[0] = term_y[:RANK]
        term_x = t_dot(inner, x_all[:, :d])
        tlast_ref[1] = term_x[RANK : 2 * RANK]
        tlast_ref[2] = term_x[2 * RANK : 3 * RANK]
        for r, (o_ref, s_ref) in enumerate(zip((o0, o1, o2, o3), (s0, s1, s2, s3))):
            here = slice(r * rows, (r + 1) * rows)
            part = inner[here]
            s_ref[...] = (acc_second[here, :] + dot(part, lgu_ref[...])).astype(BF)
            o_ref[...] = (acc_out[here, :] + dot(part, dr_ref[...])).astype(BF)


def joint_back_kernel(
    sides,
    me_ref,
    dq_ref,
    dkv_ref,
    *rest,
):
    extra = rest[: len(sides)]
    (cos_ref, sin_ref, w_ref, jr_ref, jlt_ref, x0, x1, x2, x3) = rest[len(sides) : len(sides) + 9]
    (f0, f1, f2, f3, tjr_ref, tjl_ref, keys, dj) = rest[len(sides) + 9 :]
    me = me_ref[0]
    rows, wide = x0.shape
    d = wide - PAD
    half = rows // 2
    span = TP * half
    nk = dkv_ref.shape[1] // HEAD_DIM // 2
    query_width = dq_ref.shape[1]
    for side in (0, 1):
        here = slice(side * span, (side + 1) * span)
        total = dkv_ref[here, :]
        for ref, owner in zip(extra, sides):
            if owner == side:
                total = total + ref[...].astype(F32)
        for head in range(nk):
            e = total[:, head * HEAD_DIM : (head + 1) * HEAD_DIM]
            back = e * cos_ref[here, :] - pltpu.roll(e, HEAD_DIM // 2, 1) * sin_ref[here, :]
            keys[here, head * HEAD_DIM : (head + 1) * HEAD_DIM] = back.astype(BF)
        keys[here, nk * HEAD_DIM :] = total[:, nk * HEAD_DIM :].astype(BF)
    for r in range(TP):
        for source, target in place_rows(me, r, rows):
            to = slice(r * rows + source, r * rows + source + half)
            dj[to, :query_width] = dq_ref[pl.ds(target, half), :]
            dj[to, query_width:] = keys[pl.ds(target, half), :]
    term_r = jnp.zeros((PAD, dj.shape[1]), F32)
    term_l = jnp.zeros((PAD, d), F32)
    for r, (x_ref, f_ref) in enumerate(zip((x0, x1, x2, x3), (f0, f1, f2, f3))):
        part = dj[r * rows : (r + 1) * rows, :]
        inner = dot_t(part, jr_ref[...]).astype(BF)
        f_ref[...] = (dot_t(part, w_ref[...]) + dot(inner, jlt_ref[...])).astype(BF)
        term_r += t_dot(x_ref[:, d:], part)
        term_l += t_dot(inner, x_ref[:, :d])
    tjr_ref[...] = term_r[:RANK]
    tjl_ref[...] = term_l[:RANK]


def shape(dims, dtype=BF):
    return jax.ShapeDtypeStruct(dims, dtype)


def swap(value, r):
    return lax.ppermute(value, "t", [(i, i ^ r) for i in range(TP)])


def norm_back(values, gain, incoming):
    factor = lax.rsqrt(jnp.mean(values * values, axis=-1, keepdims=True) + epsilon)
    scaled = incoming * gain
    return factor * scaled - values * (factor * factor * factor) * jnp.mean(
        scaled * values, axis=-1, keepdims=True
    )


def per_device(
    hidden,
    out_grad,
    norm_first,
    norm_second,
    joint_weight,
    out_weight,
    gate_weight,
    up_weight,
    down_weight,
    joint_left,
    joint_right,
    out_left,
    out_right,
    gate_left,
    gate_right,
    up_left,
    up_right,
    down_left,
    down_right,
    doc_lengths,
    adapter_ids,
):
    seqs = lax.axis_size("s")
    halves = lax.axis_size("h")
    groups = seqs * halves
    rows, d = hidden.shape[1:]
    half = rows // 2
    span = TP * half
    tokens = TP * rows
    length = rows * TP * halves
    strip = joint_weight.shape[0]
    ff = gate_weight.shape[1]
    own_ff = down_weight.shape[0]
    slice_ff = groups * own_ff
    wide = d + PAD
    nq = HEADS // TP
    nk = KV_HEADS // TP
    qw = nq * HEAD_DIM
    kw = nk * HEAD_DIM
    cols = qw + 2 * kw
    me = lax.axis_index("t")
    h = lax.axis_index("h")
    me_ref = me.reshape(1).astype(jnp.int32)
    slots, tile, ranges = key_plan(halves, span, length)

    q_end = HEADS * HEAD_DIM
    k_end = q_end + KV_HEADS * HEAD_DIM
    joint_cut = jnp.concatenate(
        [
            joint_weight[:, :q_end].reshape(strip, TP, qw),
            joint_weight[:, q_end:k_end].reshape(strip, TP, kw),
            joint_weight[:, k_end:].reshape(strip, TP, kw),
        ],
        axis=2,
    ).transpose(1, 0, 2)
    joint_cut = lax.all_to_all(joint_cut, "t", 0, 0, tiled=True).reshape(TP * strip, cols)
    joint_w = lax.all_gather(joint_cut, ("s", "h"), axis=0, tiled=True)

    adapter = adapter_ids[0]

    def pick(factor):
        return lax.dynamic_index_in_dim(factor, adapter, 0, keepdims=False)

    def pick_left(factor):
        return pick(jnp.swapaxes(factor, 1, 2))

    def padded(value, first):
        return jnp.pad(value, ((first, PAD - first - value.shape[0]), (0, 0)))

    def ff_slice(value):
        return lax.dynamic_index_in_dim(
            value.reshape(RANK, groups, TP, own_ff), me, 2, keepdims=False
        ).reshape(RANK, slice_ff)

    jr = pick(joint_right)
    jr_own = jnp.concatenate(
        [
            lax.dynamic_slice_in_dim(jr[:, :q_end], me * qw, qw, 1),
            lax.dynamic_slice_in_dim(jr[:, q_end:k_end], me * kw, kw, 1),
            lax.dynamic_slice_in_dim(jr[:, k_end:], me * kw, kw, 1),
        ],
        axis=1,
    )
    jr_pad = padded(jr_own, 0)
    jlt_pad = padded(pick_left(joint_left), 0)
    olt = pick_left(out_left)
    orr = pick(out_right)
    lgu = jnp.pad(
        jnp.concatenate([pick_left(gate_left), pick_left(up_left)], axis=0),
        ((RANK, PAD - 3 * RANK), (0, 0)),
    )
    rg = padded(ff_slice(pick(gate_right)), RANK)
    ru = padded(ff_slice(pick(up_right)), 2 * RANK)
    dlt = padded(ff_slice(pick_left(down_left)), 0)
    dr_pad = padded(pick(down_right), 0)

    index = jnp.arange(span, dtype=jnp.int32)

    def side_places(side, at):
        return (span * at if side == 0 else length - span * (at + 1)) + index

    ends = jnp.cumsum(doc_lengths[0])

    def marked(places):
        documents = jnp.sum((places[:, None] >= ends[None, :]).astype(jnp.int32), axis=1)
        return places + documents * (4 * length)

    own_places = jnp.concatenate([side_places(0, h), side_places(1, h)])
    own_marks = marked(own_places)
    slot_marks = []
    for shift, side, pairs in slots:
        valid = functools.reduce(jnp.logical_or, [h == target for _, target in pairs])
        slot_marks.append(jnp.where(valid, marked(side_places(side, h - shift)), 1 << 29))
    key_marks = jnp.concatenate(slot_marks + [own_marks])[None, :]
    query_marks = own_marks[:, None]
    inverse = rotary_base ** (-jnp.arange(HEAD_DIM // 2, dtype=F32) * 2.0 / HEAD_DIM)
    angles = own_places.astype(F32)[:, None] * inverse[None, :]
    cosine = jnp.concatenate([jnp.cos(angles)] * 2, axis=1)
    sine = jnp.sin(angles)
    sine = jnp.concatenate([-sine, sine], axis=1)

    x_own = hidden[0]
    x32 = x_own.astype(F32)
    first = (
        x32 * lax.rsqrt(jnp.mean(x32 * x32, axis=-1, keepdims=True) + epsilon) * norm_first
    ).astype(BF)
    first_aug = jnp.concatenate([first, dot_t(first, jlt_pad).astype(BF)], axis=1)
    firsts = [first_aug] + [swap(first_aug, r) for r in (1, 2, 3)]

    feed_cut = jnp.stack([gate_weight, up_weight]).reshape(2, strip, groups, TP, own_ff)
    feed_cut = feed_cut.transpose(3, 0, 1, 2, 4).reshape(TP, 2, strip, slice_ff)
    feed_cut = lax.all_to_all(feed_cut, "t", 0, 0, tiled=True)
    feed_cut = feed_cut.transpose(1, 0, 2, 3).reshape(2, TP * strip, slice_ff)

    q, kv = pl.pallas_call(
        qkv_kernel,
        out_shape=(shape((tokens, qw)), shape((tokens, 2 * kw))),
        in_specs=[SM] + [VM] * 8,
        out_specs=(VM, VM),
        compiler_params=params(48),
        cost_estimate=cost(2 * tokens * wide * cols, 10 * MIB),
        name="qkv",
    )(me_ref, *firsts, joint_w, jr_pad, cosine, sine)

    pieces = [
        lax.ppermute(kv[side * span : (side + 1) * span], "h", pairs) for shift, side, pairs in slots
    ]
    kv_all = jnp.concatenate(pieces + [kv], axis=0)
    key_rows = kv_all.shape[0]
    pairs_done = sum((high - low) * tile for low, high in ranges) * nq

    out_w = lax.all_gather(out_weight, ("s", "h", "t"), axis=0, tiled=True)
    feed_w = lax.all_gather(feed_cut[None], ("s", "h"), axis=0, tiled=True)
    down_w = lax.all_gather(down_weight[None], ("s", "h"), axis=0, tiled=True)

    mixed, lse = pl.pallas_call(
        functools.partial(attend_kernel, tile, ranges),
        out_shape=(shape((TP, rows, qw)), shape((tokens, nq), F32)),
        in_specs=[SM] + [VM] * 4,
        out_specs=(VM, VM),
        scratch_shapes=[pltpu.VMEM((tokens, qw), BF)],
        compiler_params=params(48),
        cost_estimate=cost(4 * pairs_done * HEAD_DIM, 6 * MIB, pairs_done),
        name="attend",
    )(me_ref, q, kv_all, query_marks, key_marks)

    mine = jnp.stack([mixed[0]] + [swap(mixed[r], r) for r in (1, 2, 3)])

    second_aug, residual, out_inner = pl.pallas_call(
        out_kernel,
        grid_spec=pltpu.PrefetchScalarGridSpec(
            num_scalar_prefetch=1,
            grid=(TP,),
            in_specs=[
                pl.BlockSpec((1, rows, qw), lambda r, m: (r, 0, 0)),
                pl.BlockSpec((qw, d), lambda r, m: (m[0] ^ r, 0)),
                pl.BlockSpec((RANK, qw), lambda r, m: (0, m[0] ^ r)),
                pl.BlockSpec((RANK, d), lambda r, m: (0, 0)),
                pl.BlockSpec((rows, d), lambda r, m: (0, 0)),
                pl.BlockSpec((1, d), lambda r, m: (0, 0)),
                pl.BlockSpec((PAD, d), lambda r, m: (0, 0)),
            ],
            out_specs=[
                pl.BlockSpec((rows, wide), lambda r, m: (0, 0)),
                pl.BlockSpec((rows, d), lambda r, m: (0, 0)),
                pl.BlockSpec((rows, RANK), lambda r, m: (0, 0)),
            ],
            scratch_shapes=[pltpu.VMEM((rows, d), F32), pltpu.VMEM((rows, RANK), F32)],
        ),
        out_shape=(shape((rows, wide)), shape((rows, d), F32), shape((rows, RANK))),
        compiler_params=params(48, 1),
        cost_estimate=cost(2 * rows * d * d, 12 * MIB),
        name="out",
    )(me_ref, mine, out_w, olt, orr, x_own, norm_second[None], lgu)

    dy = out_grad[0]
    dy_aug = jnp.concatenate([dy, dot_t(dy, dr_pad).astype(BF)], axis=1)
    dys = [dy_aug] + [swap(dy_aug, r) for r in (1, 2, 3)]
    seconds = [second_aug] + [swap(second_aug, r) for r in (1, 2, 3)]

    block = max(256, own_ff)
    per = block // own_ff
    steps = slice_ff // block
    fixed2 = lambda j: (0, 0)
    term_spec = pl.BlockSpec((RANK, block), lambda j: (0, j))
    low_spec = pl.BlockSpec((PAD, block), lambda j: (0, j))
    whole = pl.BlockSpec((rows, d), fixed2, pipeline_mode=pl.Buffered(1))
    fed = pl.pallas_call(
        feed_kernel,
        grid=(steps,),
        in_specs=[ANY] * 8
        + [
            pl.BlockSpec((groups, 1, TP * strip, block), lambda j: (0, 0, 0, j)),
            pl.BlockSpec((groups, 1, TP * strip, block), lambda j: (0, 1, 0, j)),
            pl.BlockSpec((per, own_ff, d), lambda j: (j, 0, 0)),
            low_spec,
            low_spec,
            low_spec,
            pl.BlockSpec((PAD, d), fixed2, pipeline_mode=pl.Buffered(1)),
            pl.BlockSpec((PAD, d), fixed2, pipeline_mode=pl.Buffered(1)),
        ],
        out_specs=[whole] * 8
        + [term_spec] * 3
        + [pl.BlockSpec((3, RANK, d), lambda j: (0, 0, 0), pipeline_mode=pl.Buffered(1))],
        out_shape=[shape((rows, d))] * 8
        + [shape((RANK, slice_ff), F32)] * 3
        + [shape((3, RANK, d), F32)],
        scratch_shapes=[
            pltpu.VMEM((tokens, wide), BF),
            pltpu.VMEM((tokens, wide), BF),
            pltpu.VMEM((tokens, d), F32),
            pltpu.VMEM((tokens, d), F32),
            pltpu.VMEM((tokens, PAD), F32),
            pltpu.VMEM((tokens, PAD), BF),
            pltpu.SemaphoreType.DMA((2 * TP,)),
        ],
        compiler_params=params(60, 1),
        cost_estimate=cost(2 * tokens * d * slice_ff * 6, 50 * MIB),
        name="feed",
    )(*seconds, *dys, feed_w, feed_w, down_w, dlt, rg, ru, dr_pad, lgu)
    out_parts, second_parts = (fed[:4], fed[4:8])
    term_dl, term_gr, term_ur, term_last = fed[8:]

    second_got = [second_parts[0]] + [swap(second_parts[r], r) for r in (1, 2, 3)]

    dmix, delta_residual, term_or, term_ol = pl.pallas_call(
        out_back_kernel,
        grid_spec=pltpu.PrefetchScalarGridSpec(
            num_scalar_prefetch=1,
            grid=(TP,),
            in_specs=[pl.BlockSpec((rows, d), lambda r, m: (0, 0))] * 6
            + [
                pl.BlockSpec((1, d), lambda r, m: (0, 0)),
                pl.BlockSpec((RANK, d), lambda r, m: (0, 0)),
                pl.BlockSpec((RANK, qw), lambda r, m: (0, m[0] ^ r)),
                pl.BlockSpec((rows, RANK), lambda r, m: (0, 0)),
                pl.BlockSpec((qw, d), lambda r, m: (m[0] ^ r, 0)),
                pl.BlockSpec((1, rows, qw), lambda r, m: (r, 0, 0)),
            ],
            out_specs=[
                pl.BlockSpec((1, rows, qw), lambda r, m: (r, 0, 0)),
                pl.BlockSpec((rows, d), lambda r, m: (0, 0)),
                pl.BlockSpec((RANK, d), lambda r, m: (0, 0)),
                pl.BlockSpec((RANK, qw), lambda r, m: (0, m[0] ^ r)),
            ],
            scratch_shapes=[pltpu.VMEM((rows, d), BF), pltpu.VMEM((rows, RANK), BF)],
        ),
        out_shape=(
            shape((TP, rows, qw)),
            shape((rows, d), F32),
            shape((RANK, d), F32),
            shape((RANK, d), F32),
        ),
        compiler_params=params(48, 1),
        cost_estimate=cost(2 * rows * d * d, 16 * MIB),
        name="out_back",
    )(me_ref, *second_got, dy, residual, norm_second[None], orr, olt, out_inner, out_w, mine)

    deltas = [dmix[0]] + [swap(dmix[r], r) for r in (1, 2, 3)]

    out_got = [out_parts[0]] + [swap(out_parts[r], r) for r in (1, 2, 3)]
    layer_output = (
        residual
        + (out_got[0].astype(F32) + out_got[1].astype(F32))
        + (out_got[2].astype(F32) + out_got[3].astype(F32))
    ).astype(BF)[None]

    by_slice = jnp.concatenate([term_gr, term_ur, term_dl], axis=0).astype(BF)
    by_slice = lax.psum_scatter(by_slice, "h", scatter_dimension=0, tiled=True)
    by_rows = jnp.concatenate([term_last.reshape(3 * RANK, d), term_or, term_ol], axis=0).astype(BF)
    by_rows = lax.psum_scatter(by_rows, ("h", "t"), scatter_dimension=0, tiled=True)
    early = lax.all_gather(jnp.concatenate([by_slice, by_rows], axis=0), ("s", "h", "t"))
    ids = lax.all_gather(adapter_ids, "s", axis=0, tiled=True)

    dq, dkv, dslot = pl.pallas_call(
        functools.partial(attend_back_kernel, tile, ranges),
        out_shape=(
            shape((tokens, qw)),
            shape((tokens, 2 * kw), F32),
            shape((key_rows - tokens, 2 * kw)),
        ),
        in_specs=[SM] + [VM] * 12,
        out_specs=(VM, VM, VM),
        scratch_shapes=[
            pltpu.VMEM((tokens, qw), BF),
            pltpu.VMEM((tokens, qw), BF),
            pltpu.VMEM((key_rows, 2 * kw), F32),
        ],
        compiler_params=params(56),
        cost_estimate=cost(10 * pairs_done * HEAD_DIM, 12 * MIB, pairs_done),
        name="attend_back",
    )(me_ref, q, kv_all, query_marks, key_marks, lse, mixed, *deltas, cosine, sine)

    returned = [
        lax.ppermute(dslot[i * span : (i + 1) * span], "h", [(b, a) for a, b in pairs])
        for i, (shift, side, pairs) in enumerate(slots)
    ]
    sides = tuple(side for _, side, _ in slots)
    back = pl.pallas_call(
        functools.partial(joint_back_kernel, sides),
        out_shape=[shape((rows, d))] * 4 + [shape((RANK, cols), F32), shape((RANK, d), F32)],
        in_specs=[SM] + [VM] * (2 + len(sides) + 9),
        out_specs=[VM] * 6,
        scratch_shapes=[pltpu.VMEM((tokens, 2 * kw), BF), pltpu.VMEM((tokens, cols), BF)],
        compiler_params=params(56),
        cost_estimate=cost(2 * tokens * d * cols, 16 * MIB),
        name="joint_back",
    )(me_ref, dq, dkv, *returned, cosine, sine, joint_w, jr_pad, jlt_pad, *firsts)
    first_parts, term_jr, term_jl = (back[:4], back[4], back[5])

    got = [first_parts[0]] + [swap(first_parts[r], r) for r in (1, 2, 3)]
    delta_first = (got[0].astype(F32) + got[1].astype(F32)) + (
        got[2].astype(F32) + got[3].astype(F32)
    )
    input_delta = (delta_residual + norm_back(x32, norm_first, delta_first)).astype(BF)[None]

    late = lax.all_gather(
        jnp.concatenate([term_jl, term_jr], axis=1).astype(BF), ("s", "h", "t")
    ).reshape(seqs, halves, TP, RANK, d + cols)

    chosen = (ids[None, :] == jnp.arange(joint_left.shape[0], dtype=jnp.int32)[:, None]).astype(F32)

    def slotted(value):
        value = value.astype(F32)
        return sum(chosen[:, i, None, None] * value[i][None] for i in range(seqs))

    early = early.reshape(seqs, halves, TP, -1, d)
    cut = 3 * RANK // halves
    by_slice = early[:, :, :, :cut].transpose(0, 2, 1, 3, 4).reshape(seqs, TP, 3, RANK, groups, own_ff)
    by_slice = by_slice.transpose(0, 2, 3, 4, 1, 5).reshape(seqs, 3, RANK, ff)
    by_rows = early[:, :, :, cut:].reshape(seqs, 5, RANK, d)
    d_gr, d_ur, d_dl = [slotted(by_slice[:, i]) for i in range(3)]
    d_dr, d_gl, d_ul, d_or, d_ol = [slotted(by_rows[:, i]) for i in range(5)]
    late = late.astype(F32)
    d_jl = slotted(jnp.sum(late[..., :d], axis=(1, 2)))
    late_r = jnp.sum(late[..., d:], axis=1).transpose(0, 2, 1, 3)
    d_jr = slotted(
        jnp.concatenate(
            [
                late_r[..., :qw].reshape(seqs, RANK, q_end),
                late_r[..., qw : qw + kw].reshape(seqs, RANK, k_end - q_end),
                late_r[..., qw + kw :].reshape(seqs, RANK, k_end - q_end),
            ],
            axis=2,
        )
    )

    def left(value):
        return jnp.swapaxes(value, 1, 2)

    return (
        layer_output,
        input_delta,
        left(d_jl),
        d_jr,
        left(d_ol),
        d_or,
        left(d_gl),
        d_gr,
        left(d_ul),
        d_ur,
        left(d_dl),
        d_dr,
    )


def solution(mesh):
    seqs, ctx = (mesh.shape["seq"], mesh.shape["ctx"])
    inner = Mesh(mesh.devices.reshape(seqs, ctx // TP, TP), ("s", "h", "t"))
    acts = P("s", ("h", "t"), None)
    weight = P(("s", "h", "t"), None)
    placed = (
        (acts, acts, P(), P())
        + (weight,) * 5
        + (P(),) * 10
        + (P("s", None), P("s"))
    )
    return jax.shard_map(
        per_device,
        mesh=inner,
        in_specs=placed,
        out_specs=(acts, acts) + (P(),) * 10,
        check_vma=False,
    )
```

```python
import functools

import jax
import jax.numpy as jnp
from jax import lax
from jax.experimental import pallas as pl
from jax.experimental.pallas import tpu as pltpu
from jax.sharding import Mesh, PartitionSpec as P

HEADS = 16
KV_HEADS = 8
HEAD_DIM = 128
WINDOW = 1024
FIRST_DOC = 1536
RANK = 16
PAD = 128
TP = 4

epsilon = 1e-06
rotary_base = 1000000.0
masked_score = -1e30

BF = jnp.bfloat16
F32 = jnp.float32
MIB = 1024 * 1024


def dot(left, right):
    return jnp.dot(left, right, preferred_element_type=F32)


def dot_t(left, right):
    return lax.dot_general(left, right, (((1,), (1,)), ((), ())), preferred_element_type=F32)


def t_dot(left, right):
    return lax.dot_general(left, right, (((0,), (0,)), ((), ())), preferred_element_type=F32)


def params(mib, grid=0):
    extra = {"dimension_semantics": ("arbitrary",) * grid} if grid else {}
    return pltpu.CompilerParams(vmem_limit_bytes=mib * MIB, **extra)


def cost(flops, nbytes, trans=0):
    return pl.CostEstimate(flops=int(flops), bytes_accessed=int(nbytes), transcendentals=int(trans))


VM = pl.BlockSpec(memory_space=pltpu.VMEM)
SM = pl.BlockSpec(memory_space=pltpu.SMEM)
ANY = pl.BlockSpec(memory_space=pl.ANY)


def half_range(side, h, span, length):
    start = span * h if side == 0 else length - span * (h + 1)
    return (start, start + span)


def may_see(q, k):
    grain = 64
    for q0 in range(q[0], q[1], grain):
        for k0 in range(k[0], k[1], grain):
            same = (q0 >= FIRST_DOC) == (k0 >= FIRST_DOC)
            if same and k0 < q0 + grain and q0 - (k0 + grain - 1) < WINDOW:
                return True
    return False


def key_plan(halves, span, length):
    slots = []
    for shift in list(range(halves - 1, 0, -1)) + list(range(-1, -halves, -1)):
        for side in (0, 1):
            pairs = []
            for h in range(halves):
                source = h - shift
                if not 0 <= source < halves:
                    continue
                wanted = half_range(side, source, span, length)
                if any(may_see(half_range(s, h, span, length), wanted) for s in (0, 1)):
                    pairs.append((source, h))
            if pairs:
                slots.append((shift, side, tuple(pairs)))
    tile = min(256, span)
    step = 128
    ranges = []
    for i in range(2 * span // tile):
        low, high = (1 << 30, 0)
        for h in range(halves):
            side, inside = divmod(i * tile, span)
            base = half_range(side, h, span, length)[0] + inside
            held = []
            for shift, key_side, pairs in slots:
                held.append(
                    half_range(key_side, h - shift, span, length) if (h - shift, h) in pairs else None
                )
            held += [half_range(s, h, span, length) for s in (0, 1)]
            for index, region in enumerate(held):
                if region is None:
                    continue
                for offset in range(0, span, step):
                    block = (region[0] + offset, region[0] + min(offset + step, span))
                    if may_see((base, base + tile), block):
                        low = min(low, index * span + offset)
                        high = max(high, index * span + offset + step)
        ranges.append((low, min(high, (len(slots) + 2) * span)))
    return (slots, tile, ranges)


def place_rows(me, r, rows):
    half = rows // 2
    other = me ^ r
    first = pl.multiple_of(other * half, half)
    second = pl.multiple_of(TP * half + (TP - 1 - other) * half, half)
    return ((0, first), (half, second))


def cut_kernel(wide, me_ref, joint_ref, gate_ref, up_ref, *outs):
    me = me_ref[0]
    joints, feeds = (outs[:TP], outs[TP:])
    cols = joints[0].shape[1]
    kw = KV_HEADS // TP * HEAD_DIM
    qw = cols - 2 * kw
    for r in range(TP):
        other = me ^ r
        start = 0
        base = 0
        for width, count in ((qw, TP), (kw, TP), (kw, TP)):
            joints[r][:, start : start + width] = joint_ref[
                :, pl.ds(pl.multiple_of(base + other * width, HEAD_DIM), width)
            ]
            start += width
            base += width * count
        for g in range(feeds[r].shape[2] // wide if feeds else 0):
            at = pl.ds(pl.multiple_of((g * TP + other) * wide, wide), wide)
            feeds[r][0, :, g * wide : (g + 1) * wide] = gate_ref[:, at]
            feeds[r][1, :, g * wide : (g + 1) * wide] = up_ref[:, at]


def natural_kernel(count, me_ref, *refs):
    parts, (out_ref, sem) = (refs[:count], refs[-2:])
    me = me_ref[0]
    strip = parts[0].shape[-2]
    copies = []
    for r, ref in enumerate(parts):
        rows = pl.ds(pl.multiple_of((me ^ r) * strip, strip), strip)
        to = out_ref.at[rows, :] if len(ref.shape) == 2 else out_ref.at[:, rows, :]
        copies.append(pltpu.make_async_copy(ref, to, sem.at[r]))
    for copy in copies:
        copy.start()
    for copy in copies:
        copy.wait()


def strips_kernel(layout, strip, me_ref, *refs):
    out_ref, sem = refs[-2:]
    me, place = (me_ref[0], me_ref[1])
    copies = []
    for ref, (r, groups) in zip(refs, layout):
        for i, group in enumerate(groups):
            row = pl.multiple_of(((place ^ group) * TP + (me ^ r)) * strip, strip)
            copies.append(
                pltpu.make_async_copy(
                    ref.at[pl.ds(i * strip, strip), :],
                    out_ref.at[pl.ds(row, strip), :],
                    sem.at[len(copies)],
                )
            )
    for copy in copies:
        copy.start()
    for copy in copies:
        copy.wait()


def load_pieces(place, pieces, target, sem):
    strip = pieces[0].shape[0]
    if len(pieces) == 1:
        copies = [pltpu.make_async_copy(pieces[0], target, sem.at[0])]
        copies[0].start()
        return copies
    copies = []
    for r, ref in enumerate(pieces):
        rows = pl.ds(pl.multiple_of((place ^ r) * strip, strip), strip)
        copies.append(pltpu.make_async_copy(ref, target.at[rows, :], sem.at[r]))
    for copy in copies:
        copy.start()
    return copies


def qkv_kernel(count, me_ref, *refs):
    pieces = refs[:count]
    (x0, x1, x2, x3a, x3b, jr_ref, cos_ref, sin_ref) = refs[count : count + 8]
    (q_ref, kv_ref, w_ref, sem) = refs[-4:]
    me = me_ref[0]
    copies = load_pieces(me_ref[1], pieces, w_ref, sem)
    rows, wide = x0.shape
    d = wide - PAD
    half = rows // 2
    nq = q_ref.shape[1] // HEAD_DIM
    nk = kv_ref.shape[1] // HEAD_DIM // 2
    for copy in copies:
        copy.wait()
    for r, x_refs in enumerate(((x0,), (x1,), (x2,), (x3a, x3b))):
        x = jnp.concatenate([ref[...] for ref in x_refs], axis=0)
        joined = dot(x[:, :d], w_ref[...]) + dot(x[:, d:], jr_ref[...])
        for source, target in place_rows(me, r, rows):
            part = joined[source : source + half]
            cosine = cos_ref[pl.ds(target, half), :]
            sine = sin_ref[pl.ds(target, half), :]
            for head in range(nq + nk):
                u = part[:, head * HEAD_DIM : (head + 1) * HEAD_DIM]
                turned = (u * cosine + pltpu.roll(u, HEAD_DIM // 2, 1) * sine).astype(BF)
                if head < nq:
                    q_ref[pl.ds(target, half), head * HEAD_DIM : (head + 1) * HEAD_DIM] = turned
                else:
                    at = head - nq
                    kv_ref[pl.ds(target, half), at * HEAD_DIM : (at + 1) * HEAD_DIM] = turned
            kv_ref[pl.ds(target, half), nk * HEAD_DIM :] = part[:, (nq + nk) * HEAD_DIM :].astype(BF)


def head_columns(ref, rows, first, count):
    return jnp.concatenate(
        [ref[rows, (first + i) * HEAD_DIM : (first + i + 1) * HEAD_DIM] for i in range(count)], axis=0
    )


def bias_of(qpos_ref, kpos_ref, rows, low, high, group):
    distance = qpos_ref[rows, :] - kpos_ref[:, low:high]
    bias = jnp.where((distance >= 0) & (distance < WINDOW), 0.0, masked_score).astype(F32)
    return jnp.concatenate([bias] * group, axis=0)


def attend_kernel(tile, ranges, me_ref, q_ref, kv_ref, qpos_ref, kpos_ref, mixed_ref, lse_ref, held):
    me = me_ref[0]
    rows = mixed_ref.shape[1]
    half = rows // 2
    nk = kv_ref.shape[1] // HEAD_DIM // 2
    group = q_ref.shape[1] // HEAD_DIM // nk
    scale = HEAD_DIM ** (-0.5)
    for i, (low, high) in enumerate(ranges):
        here = slice(i * tile, (i + 1) * tile)
        bias = bias_of(qpos_ref, kpos_ref, here, low, high, group)
        for head in range(nk):
            q = head_columns(q_ref, here, head * group, group)
            k = kv_ref[low:high, head * HEAD_DIM : (head + 1) * HEAD_DIM]
            v = kv_ref[low:high, (nk + head) * HEAD_DIM : (nk + head + 1) * HEAD_DIM]
            scores = dot_t(q, k) * scale + bias
            largest = jnp.max(scores, axis=-1, keepdims=True)
            raised = jnp.exp(scores - largest)
            total = jnp.sum(raised, axis=-1, keepdims=True)
            out = dot((raised * (1.0 / total)).astype(BF), v).astype(BF)
            lse = largest + jnp.log(total)
            for g in range(group):
                at = head * group + g
                held[here, at * HEAD_DIM : (at + 1) * HEAD_DIM] = out[g * tile : (g + 1) * tile]
                lse_ref[here, at : at + 1] = lse[g * tile : (g + 1) * tile]
    for r in range(TP):
        for source, target in place_rows(me, r, rows):
            mixed_ref[r, source : source + half, :] = held[pl.ds(target, half), :]


def attend_back_kernel(
    tile,
    ranges,
    me_ref,
    q_ref,
    kv_ref,
    qpos_ref,
    kpos_ref,
    lse_ref,
    mixed_ref,
    d0,
    d1,
    d2,
    d3,
    cos_ref,
    sin_ref,
    dq_ref,
    dkv_ref,
    dslot_ref,
    held,
    given,
    total_ref,
):
    me = me_ref[0]
    rows = mixed_ref.shape[1]
    half = rows // 2
    nk = kv_ref.shape[1] // HEAD_DIM // 2
    group = q_ref.shape[1] // HEAD_DIM // nk
    scale = HEAD_DIM ** (-0.5)
    for r, d_ref in enumerate((d0, d1, d2, d3)):
        for source, target in place_rows(me, r, rows):
            held[pl.ds(target, half), :] = mixed_ref[r, source : source + half, :]
            given[pl.ds(target, half), :] = d_ref[source : source + half, :]
    total_ref[...] = jnp.zeros_like(total_ref)
    for i, (low, high) in enumerate(ranges):
        here = slice(i * tile, (i + 1) * tile)
        bias = bias_of(qpos_ref, kpos_ref, here, low, high, group)
        cosine = cos_ref[here, :]
        sine = sin_ref[here, :]
        for head in range(nk):
            key_columns = slice(head * HEAD_DIM, (head + 1) * HEAD_DIM)
            value_columns = slice((nk + head) * HEAD_DIM, (nk + head + 1) * HEAD_DIM)
            q = head_columns(q_ref, here, head * group, group)
            out = head_columns(held, here, head * group, group)
            delta = head_columns(given, here, head * group, group)
            lse = jnp.concatenate(
                [lse_ref[here, head * group + g : head * group + g + 1] for g in range(group)], axis=0
            )
            k = kv_ref[low:high, key_columns]
            v = kv_ref[low:high, value_columns]
            chances = jnp.exp(dot_t(q, k) * scale + bias - lse)
            inner = jnp.sum(out.astype(F32) * delta.astype(F32), axis=-1, keepdims=True)
            raw = (chances * (dot_t(delta, v) - inner) * scale).astype(BF)
            dq = dot(raw, k)
            for g in range(group):
                at = head * group + g
                e = dq[g * tile : (g + 1) * tile]
                back = e * cosine - pltpu.roll(e, HEAD_DIM // 2, 1) * sine
                dq_ref[here, at * HEAD_DIM : (at + 1) * HEAD_DIM] = back.astype(BF)
            total_ref[low:high, key_columns] += t_dot(raw, q)
            total_ref[low:high, value_columns] += t_dot(chances.astype(BF), delta)
    extra = dslot_ref.shape[0]
    dslot_ref[...] = total_ref[:extra, :].astype(BF)
    dkv_ref[...] = total_ref[extra:, :]


def out_kernel(
    me_ref, m_ref, w_ref, olt_ref, or_ref, x_ref, gain_ref, lgu_ref, aug_ref, res_ref, oi_ref, acc, inner
):
    r = pl.program_id(0)
    d = x_ref.shape[1]

    @pl.when(r == 0)
    def _():
        acc[...] = x_ref[...].astype(F32)
        inner[...] = jnp.zeros_like(inner)

    m = m_ref[0]
    acc[...] += dot(m, w_ref[...])
    inner[...] += dot_t(m, olt_ref[...])

    @pl.when(r == TP - 1)
    def _():
        low = inner[...].astype(BF)
        oi_ref[...] = low
        residual = acc[...] + dot(low, or_ref[...])
        res_ref[...] = residual
        factor = lax.rsqrt(jnp.mean(residual * residual, axis=-1, keepdims=True) + epsilon)
        second = (residual * factor * gain_ref[...]).astype(BF)
        aug_ref[:, :d] = second
        aug_ref[:, d:] = dot_t(second, lgu_ref[...]).astype(BF)


def out_back_kernel(
    me_ref,
    p0,
    p1,
    p2,
    p3,
    dy_ref,
    res_ref,
    gain_ref,
    or_ref,
    olt_ref,
    oi_ref,
    w_ref,
    m_ref,
    tdr_ref,
    dmix_ref,
    dres_ref,
    branch,
    inner,
    terms,
):
    r = pl.program_id(0)
    rows, d = dy_ref.shape
    width = d // TP

    @pl.when(r == 0)
    def _():
        gain = gain_ref[...]
        incoming = (p0[:rows].astype(F32) + p1[:rows].astype(F32)) + (
            p2[:rows].astype(F32) + p3[:rows].astype(F32)
        )
        v = res_ref[...]
        factor = lax.rsqrt(jnp.mean(v * v, axis=-1, keepdims=True) + epsilon)
        scaled = incoming * gain
        back = factor * scaled - v * (factor * factor * factor) * jnp.mean(
            scaled * v, axis=-1, keepdims=True
        )
        delta = dy_ref[...].astype(F32) + back
        dres_ref[...] = delta
        low = delta.astype(BF)
        branch[...] = low
        inner[...] = dot_t(low, or_ref[...]).astype(BF)
        terms[:RANK] = tdr_ref[...]
        terms[RANK:] = t_dot(oi_ref[...], low)

    dmix_ref[0, :rows] = (dot_t(branch[...], w_ref[...]) + dot(inner[...], olt_ref[...])).astype(BF)
    at = pl.ds(pl.multiple_of((me_ref[0] ^ r) * width, width), width)
    dmix_ref[0, rows : rows + 2 * RANK] = terms[:, at].astype(BF)
    dmix_ref[0, rows + 2 * RANK :] = t_dot(inner[...], m_ref[0]).astype(BF)


def load_rows(refs, stores, sem):
    copies = []
    stores = stores if isinstance(stores, tuple) else (stores,)
    for index, store in enumerate(stores):
        at = 0
        for ref in refs[5 * index : 5 * index + 5]:
            copies.append(
                pltpu.make_async_copy(
                    ref, store.at[pl.ds(at, ref.shape[0]), :], sem.at[len(copies)]
                )
            )
            at += ref.shape[0]
    for copy in copies:
        copy.start()
    for copy in copies:
        copy.wait()


def gate_kernel(*refs):
    xs, refs = (refs[:5], refs[5:])
    (gate_ref, up_ref, rg_ref, ru_ref, act_ref, silu_ref, slope_ref, x_all, sem) = refs
    d = x_all.shape[1] - PAD

    @pl.when(pl.program_id(0) == 0)
    def _():
        load_rows(xs, x_all, sem)

    block = gate_ref.shape[-1]
    gate_w = gate_ref[...].reshape(d, block)
    up_w = up_ref[...].reshape(d, block)
    count = x_all.shape[0]
    take = min(512, count)
    for start in range(0, count, take):
        here = slice(start, start + take)
        x = x_all[here, :d]
        xi = x_all[here, d:]
        gate = dot(x, gate_w) + dot(xi, rg_ref[...])
        up = dot(x, up_w) + dot(xi, ru_ref[...])
        sigmoid = jax.nn.sigmoid(gate)
        silu = gate * sigmoid
        act_ref[here, :] = (silu * up).astype(BF)
        silu_ref[here, :] = silu.astype(BF)
        slope_ref[here, :] = (up * sigmoid * (1.0 + gate * (1.0 - sigmoid))).astype(BF)


def feed_back_kernel(me_ref, *refs):
    xs, ys, refs = (refs[:5], refs[5:10], refs[10:])
    (gate_ref, up_ref, down_ref, silu_ref, slope_ref, dlt_ref, rg_ref, ru_ref, lgu_ref, *refs) = refs
    (s0, s1, s2, s3, tgr_ref, tur_ref, x_all, y_all, acc_second, acc_inner, sem) = refs
    me = me_ref[0]
    j = pl.program_id(0)
    d = acc_second.shape[1]
    rows = x_all.shape[0] // TP

    @pl.when(j == 0)
    def _():
        load_rows(list(xs) + list(ys), (x_all, y_all), sem)
        acc_second[...] = jnp.zeros_like(acc_second)
        acc_inner[...] = jnp.zeros_like(acc_inner)

    block = gate_ref.shape[-1]
    gate_w = gate_ref[...].reshape(d, block)
    up_w = up_ref[...].reshape(d, block)
    down_w = down_ref[...]
    dlt, rg, ru = (dlt_ref[...], rg_ref[...], ru_ref[...])
    term_g = jnp.zeros((PAD, block), F32)
    term_u = jnp.zeros((PAD, block), F32)
    take = min(512, TP * rows)
    for start in range(0, TP * rows, take):
        here = slice(start, start + take)
        delta = dot_t(y_all[here, :d], down_w) + dot(y_all[here, d:], dlt)
        delta_gate = (delta * slope_ref[here, :].astype(F32)).astype(BF)
        delta_up = (delta * silu_ref[here, :].astype(F32)).astype(BF)
        acc_second[here, :] += dot_t(delta_gate, gate_w) + dot_t(delta_up, up_w)
        acc_inner[here, :] += dot_t(delta_gate, rg) + dot_t(delta_up, ru)
        tail = x_all[here, d:]
        term_g += t_dot(tail, delta_gate)
        term_u += t_dot(tail, delta_up)
    tgr_ref[...] = term_g[RANK : 2 * RANK]
    tur_ref[...] = term_u[2 * RANK : 3 * RANK]

    @pl.when(j == pl.num_programs(0) - 1)
    def _():
        inner = acc_inner[...].astype(BF)
        width = d // TP
        for r, s_ref in enumerate((s0, s1, s2, s3)):
            here = slice(r * rows, (r + 1) * rows)
            s_ref[:rows, :] = (acc_second[here, :] + dot(inner[here], lgu_ref[...])).astype(BF)
            at = pl.ds(pl.multiple_of((me ^ r) * width, width), width)
            term = t_dot(inner, x_all[:, at]).astype(BF)
            s_ref[rows:, :width] = term[RANK : 2 * RANK]
            s_ref[rows:, width : 2 * width] = term[2 * RANK : 3 * RANK]
            s_ref[rows:, 2 * width :] = jnp.zeros((RANK, d - 2 * width), BF)


def down_kernel(*refs):
    ys, refs = (refs[:5], refs[5:])
    (down_ref, act_ref, dlt_ref, dr_ref, o0, o1, o2, o3, tdl_ref, tdr_ref, *refs) = refs
    (y_all, acc, acc_inner, sem) = refs
    j = pl.program_id(0)
    rows = o0.shape[0]
    d = acc.shape[1]

    @pl.when(j == 0)
    def _():
        load_rows(ys, y_all, sem)
        acc[...] = jnp.zeros_like(acc)
        acc_inner[...] = jnp.zeros_like(acc_inner)

    acc[...] += dot(act_ref[...], down_ref[...])
    acc_inner[...] += dot_t(act_ref[...], dlt_ref[...])
    tdl_ref[...] = t_dot(y_all[:, d:], act_ref[...])[:RANK]

    @pl.when(j == pl.num_programs(0) - 1)
    def _():
        inner = acc_inner[...].astype(BF)
        tdr_ref[...] = t_dot(inner, y_all[:, :d])[:RANK]
        for r, o_ref in enumerate((o0, o1, o2, o3)):
            here = slice(r * rows, (r + 1) * rows)
            o_ref[...] = (acc[here, :] + dot(inner[here], dr_ref[...])).astype(BF)


def slot_kernel(plan, adapters, got_ref, *outs):
    seqs, halves = got_ref.shape[:2]
    marks = []
    for i in range(seqs):
        ids = got_ref[i, 0, 0, :, -PAD:].astype(F32)
        marks.append(
            [
                jnp.max(jnp.where(ids == float(e), 1.0, 0.0), axis=1, keepdims=True)
                for e in range(adapters)
            ]
        )
    for out_ref, parts in zip(outs, plan):
        for to, width, sources in parts:
            values = []
            for i in range(seqs):
                total = None
                for h, t, at in sources:
                    part = got_ref[i, h, t, :, at : at + width].astype(F32)
                    total = part if total is None else total + part
                values.append(total)
            for e in range(adapters):
                out_ref[e, :, to : to + width] = sum(
                    marks[i][e] * values[i] for i in range(seqs)
                )


def joint_terms_kernel(sides, me_ref, dq_ref, dkv_ref, *refs):
    extra, refs = (refs[: len(sides)], refs[len(sides) :])
    (cos_ref, sin_ref, jr_ref, x0, x1, x2, x3a, x3b, dj, inner_ref, tjr_ref, tjl_ref, keys) = refs
    me = me_ref[0]
    rows, wide = x0.shape
    d = wide - PAD
    half = rows // 2
    span = TP * half
    nk = dkv_ref.shape[1] // HEAD_DIM // 2
    query_width = dq_ref.shape[1]
    for side in (0, 1):
        here = slice(side * span, (side + 1) * span)
        total = dkv_ref[here, :]
        for ref, owner in zip(extra, sides):
            if owner == side:
                total = total + ref[...].astype(F32)
        for head in range(nk):
            e = total[:, head * HEAD_DIM : (head + 1) * HEAD_DIM]
            back = e * cos_ref[here, :] - pltpu.roll(e, HEAD_DIM // 2, 1) * sin_ref[here, :]
            keys[here, head * HEAD_DIM : (head + 1) * HEAD_DIM] = back.astype(BF)
        keys[here, nk * HEAD_DIM :] = total[:, nk * HEAD_DIM :].astype(BF)
    for r in range(TP):
        for source, target in place_rows(me, r, rows):
            to = slice(r * rows + source, r * rows + source + half)
            dj[to, :query_width] = dq_ref[pl.ds(target, half), :]
            dj[to, query_width:] = keys[pl.ds(target, half), :]
    term_r = jnp.zeros((PAD, dj.shape[1]), F32)
    term_l = jnp.zeros((PAD, d), F32)
    for r, x_refs in enumerate(((x0,), (x1,), (x2,), (x3a, x3b))):
        x = jnp.concatenate([ref[...] for ref in x_refs], axis=0)
        here = slice(r * rows, (r + 1) * rows)
        inner = dot_t(dj[here, :], jr_ref[...]).astype(BF)
        inner_ref[here, :] = inner
        term_r += t_dot(x[:, d:], dj[here, :])
        term_l += t_dot(inner, x[:, :d])
    tjr_ref[...] = term_r[:RANK]
    tjl_ref[...] = term_l[:RANK]


def joint_back_kernel(me_ref, *refs):
    pieces = refs[:-9]
    (dj, inner, jlt_ref, f0, f1, f2, f3, w_ref, sem) = refs[-9:]
    for copy in load_pieces(me_ref[1], pieces, w_ref, sem):
        copy.wait()
    rows = f0.shape[0]
    for r, f_ref in enumerate((f0, f1, f2, f3)):
        here = slice(r * rows, (r + 1) * rows)
        f_ref[...] = (dot_t(dj[here, :], w_ref[...]) + dot(inner[here, :], jlt_ref[...])).astype(BF)


def shape(dims, dtype=BF):
    return jax.ShapeDtypeStruct(dims, dtype)


def swap(value, r):
    return lax.ppermute(value, "t", [(i, i ^ r) for i in range(TP)])


def near_far(value):
    return (swap(value, 1), swap(value, 2))


def corners(near, far):
    half = near.shape[0] // 2
    return (swap(near[:half], 2), swap(far[half:], 1))


def sent(parts):
    return [parts[0]] + [swap(parts[r], r) for r in range(1, TP)]


def after(value, *others):
    return lax.optimization_barrier((value, others))[0]


def together(*values):
    return lax.optimization_barrier(values)


def flip(value, axis, bit):
    size = lax.axis_size(axis)
    return lax.ppermute(value, axis, [(i, i ^ bit) for i in range(size)])


def collect_first(value, seqs, halves):
    held = {0: value}
    for i in range(halves.bit_length() - 1):
        held[1 << i] = flip(value, "h", 1 << i)
    for i in range(1, seqs.bit_length() - 1):
        held[halves << i] = flip(value, "s", 1 << i)
    return held


def collect_rest(held, seqs, halves):
    held = dict(held)
    bits = [("h", 1 << i, 1 << i) for i in range(halves.bit_length() - 1)]
    bits += [("s", 1 << i, halves << i) for i in range(1, seqs.bit_length() - 1)]
    for axis, bit, offset in bits:
        for index in sorted(held):
            if index < offset and index | offset not in held:
                held[index | offset] = flip(held[index], axis, bit)
    return held


def norm_back(values, gain, incoming):
    factor = lax.rsqrt(jnp.mean(values * values, axis=-1, keepdims=True) + epsilon)
    scaled = incoming * gain
    return factor * scaled - values * (factor * factor * factor) * jnp.mean(
        scaled * values, axis=-1, keepdims=True
    )


def per_device(
    hidden,
    out_grad,
    norm_first,
    norm_second,
    joint_weight,
    out_weight,
    gate_weight,
    up_weight,
    down_weight,
    joint_left,
    joint_right,
    out_left,
    out_right,
    gate_left,
    gate_right,
    up_left,
    up_right,
    down_left,
    down_right,
    doc_lengths,
    adapter_ids,
):
    seqs = lax.axis_size("s")
    halves = lax.axis_size("h")
    groups = seqs * halves
    rows, d = hidden.shape[1:]
    half = rows // 2
    span = TP * half
    tokens = TP * rows
    length = rows * TP * halves
    strip = joint_weight.shape[0]
    ff = gate_weight.shape[1]
    own_ff = down_weight.shape[0]
    slice_ff = groups * own_ff
    wide = d + PAD
    nq = HEADS // TP
    nk = KV_HEADS // TP
    qw = nq * HEAD_DIM
    kw = nk * HEAD_DIM
    cols = qw + 2 * kw
    me = lax.axis_index("t")
    h = lax.axis_index("h")
    s_at = lax.axis_index("s")
    place = s_at * halves + h
    me_ref = jnp.stack([me, place]).astype(jnp.int32)
    slots, tile, ranges = key_plan(halves, span, length)

    adapter = adapter_ids[0]

    def pick(factor):
        return lax.dynamic_index_in_dim(factor, adapter, 0, keepdims=False)

    def pick_left(factor):
        return pick(jnp.swapaxes(factor, 1, 2))

    def padded(value, first):
        return jnp.pad(value, ((first, PAD - first - value.shape[0]), (0, 0)))

    q_end = HEADS * HEAD_DIM
    k_end = q_end + KV_HEADS * HEAD_DIM
    x_own = hidden[0]
    x32 = x_own.astype(F32)
    first = (
        x32 * lax.rsqrt(jnp.mean(x32 * x32, axis=-1, keepdims=True) + epsilon) * norm_first
    ).astype(BF)
    jlt_pad = padded(pick_left(joint_left), 0)
    first_aug = jnp.concatenate([first, dot_t(first, jlt_pad).astype(BF)], axis=1)

    whole_lanes = own_ff % HEAD_DIM == 0
    feed_shapes = [shape((2, strip, slice_ff))] * (TP if whole_lanes else 0)
    cut = pl.pallas_call(
        functools.partial(cut_kernel, own_ff),
        out_shape=[shape((strip, cols))] * TP + feed_shapes,
        in_specs=[SM] + [VM] * 3,
        out_specs=[VM] * (TP + len(feed_shapes)),
        compiler_params=params(24),
        cost_estimate=cost(0, 6 * MIB),
        name="cut",
    )(me_ref, joint_weight, gate_weight, up_weight)
    feed_parts = cut[TP:]
    if not whole_lanes:
        both = jnp.stack([gate_weight, up_weight]).reshape(2, strip, groups, TP, own_ff)
        feed_parts = [
            lax.dynamic_index_in_dim(both, me ^ r, 3, keepdims=False).reshape(2, strip, slice_ff)
            for r in range(TP)
        ]

    def natural(parts, out, *others):
        return pl.pallas_call(
            functools.partial(natural_kernel, TP),
            out_shape=out,
            in_specs=[SM] + [ANY] * (TP + len(others)),
            out_specs=ANY,
            scratch_shapes=[pltpu.SemaphoreType.DMA((TP,))],
            compiler_params=params(8),
            cost_estimate=cost(0, 4 * MIB),
            name="natural",
        )(me_ref, *parts, *others)

    def ff_slice(value):
        return lax.dynamic_index_in_dim(
            value.reshape(RANK, groups, TP, own_ff), me, 2, keepdims=False
        ).reshape(RANK, slice_ff)

    jr = pick(joint_right)
    jr_own = jnp.concatenate(
        [
            lax.dynamic_slice_in_dim(jr[:, :q_end], me * qw, qw, 1),
            lax.dynamic_slice_in_dim(jr[:, q_end:k_end], me * kw, kw, 1),
            lax.dynamic_slice_in_dim(jr[:, k_end:], me * kw, kw, 1),
        ],
        axis=1,
    )
    jr_pad = padded(jr_own, 0)
    olt = pick_left(out_left)
    orr = pick(out_right)
    lgu = jnp.pad(
        jnp.concatenate([pick_left(gate_left), pick_left(up_left)], axis=0),
        ((RANK, PAD - 3 * RANK), (0, 0)),
    )
    rg = padded(ff_slice(pick(gate_right)), RANK)
    ru = padded(ff_slice(pick(up_right)), 2 * RANK)
    dlt = padded(ff_slice(pick_left(down_left)), 0)

    index = jnp.arange(span, dtype=jnp.int32)

    def side_places(side, at):
        return (span * at if side == 0 else length - span * (at + 1)) + index

    ends = jnp.cumsum(doc_lengths[0])

    def marked(places):
        documents = jnp.sum((places[:, None] >= ends[None, :]).astype(jnp.int32), axis=1)
        return places + documents * (4 * length)

    own_places = jnp.concatenate([side_places(0, h), side_places(1, h)])
    own_marks = marked(own_places)
    slot_marks = []
    for shift, side, pairs in slots:
        valid = functools.reduce(jnp.logical_or, [h == target for _, target in pairs])
        slot_marks.append(jnp.where(valid, marked(side_places(side, h - shift)), 1 << 29))
    key_marks = jnp.concatenate(slot_marks + [own_marks])[None, :]
    query_marks = own_marks[:, None]
    inverse = rotary_base ** (-jnp.arange(HEAD_DIM // 2, dtype=F32) * 2.0 / HEAD_DIM)
    angles = own_places.astype(F32)[:, None] * inverse[None, :]
    cosine = jnp.concatenate([jnp.cos(angles)] * 2, axis=1)
    sine = jnp.sin(angles)
    sine = jnp.concatenate([-sine, sine], axis=1)

    dy = out_grad[0]
    dr_pad = padded(pick(down_right), 0)
    dy_aug = jnp.concatenate([dy, dot_t(dy, dr_pad).astype(BF)], axis=1)

    joint_sent, out_held = together(sent(cut[:TP]), collect_first(out_weight, seqs, halves))
    joint_cut = natural(joint_sent, shape((TP * strip, cols)))
    joint_w = lax.all_gather(joint_cut, ("s", "h"), axis=0, tiled=True)

    feed_parts, first_aug, out_held, _ = together(feed_parts, first_aug, out_held, joint_cut)
    feed_sent, first_got, (rg, ru, dlt, lgu, olt, orr, dr_pad, dy_aug) = together(
        sent(feed_parts), near_far(first_aug), (rg, ru, dlt, lgu, olt, orr, dr_pad, dy_aug)
    )
    out_held = collect_rest(after(out_held, first_got), seqs, halves)
    feed_cut = natural(feed_sent, shape((2, TP * strip, slice_ff)))
    feed_w = lax.all_gather(feed_cut[None], ("s", "h"), axis=0, tiled=True)

    first_ends, out_held = together(corners(*first_got), out_held)
    held_groups = tuple(sorted(out_held))
    out_mine = jnp.concatenate([out_held[i] for i in held_groups], axis=0)
    firsts = [first_aug, *first_got, *first_ends]

    q, kv = pl.pallas_call(
        functools.partial(qkv_kernel, 1),
        out_shape=(shape((tokens, qw)), shape((tokens, 2 * kw))),
        in_specs=[SM] + [ANY] + [VM] * 8,
        out_specs=(VM, VM),
        scratch_shapes=[pltpu.VMEM((d, cols), BF), pltpu.SemaphoreType.DMA((1,))],
        compiler_params=params(48),
        cost_estimate=cost(2 * tokens * wide * cols, 10 * MIB),
        name="qkv",
    )(me_ref, joint_w, *firsts, jr_pad, cosine, sine)

    out_mine = after(out_mine, q)
    pieces, out_got, own_core = together(
        [
            lax.ppermute(kv[side * span : (side + 1) * span], "h", pairs)
            for shift, side, pairs in slots
        ],
        near_far(out_mine),
        flip(out_mine, "s", 1),
    )
    kv_all = jnp.concatenate(pieces + [kv], axis=0)
    key_rows = kv_all.shape[0]
    pairs_done = sum((high - low) * tile for low, high in ranges) * nq

    mixed, lse = pl.pallas_call(
        functools.partial(attend_kernel, tile, ranges),
        out_shape=(shape((TP, rows, qw)), shape((tokens, nq), F32)),
        in_specs=[SM] + [VM] * 4,
        out_specs=(VM, VM),
        scratch_shapes=[pltpu.VMEM((tokens, qw), BF)],
        compiler_params=params(48),
        cost_estimate=cost(4 * pairs_done * HEAD_DIM, 6 * MIB, pairs_done),
        name="attend",
    )(me_ref, q, kv_all, query_marks, key_marks)

    out_got = after(out_got, mixed)
    mine, out_ends, out_cores = together(
        sent(mixed), corners(*out_got), [flip(block, "s", 1) for block in out_got]
    )
    down_w = lax.all_gather(after(down_weight, mixed), ("s", "h"), axis=0, tiled=True)
    mine = jnp.stack(mine)
    end_cores = together(*[flip(block, "s", 1) for block in out_ends])
    out_blocks = [out_mine, *out_got, *out_ends, own_core, *out_cores, *end_cores]
    cut_at = len(held_groups) // 2
    layout = [(0, held_groups), (1, held_groups), (2, held_groups)]
    layout += [(3, held_groups[:cut_at]), (3, held_groups[cut_at:])]
    layout += [(r, tuple(i | halves for i in some)) for r, some in layout]
    out_w = pl.pallas_call(
        functools.partial(strips_kernel, tuple(layout), strip),
        out_shape=shape((d, d)),
        in_specs=[SM] + [ANY] * len(layout),
        out_specs=ANY,
        scratch_shapes=[pltpu.SemaphoreType.DMA((groups * TP,))],
        compiler_params=params(8),
        cost_estimate=cost(0, 16 * MIB),
        name="strips",
    )(me_ref, *out_blocks)

    second_aug, residual, out_inner = pl.pallas_call(
        out_kernel,
        grid_spec=pltpu.PrefetchScalarGridSpec(
            num_scalar_prefetch=1,
            grid=(TP,),
            in_specs=[
                pl.BlockSpec((1, rows, qw), lambda r, m: (r, 0, 0)),
                pl.BlockSpec((qw, d), lambda r, m: (m[0] ^ r, 0)),
                pl.BlockSpec((RANK, qw), lambda r, m: (0, m[0] ^ r)),
                pl.BlockSpec((RANK, d), lambda r, m: (0, 0)),
                pl.BlockSpec((rows, d), lambda r, m: (0, 0)),
                pl.BlockSpec((1, d), lambda r, m: (0, 0)),
                pl.BlockSpec((PAD, d), lambda r, m: (0, 0)),
            ],
            out_specs=[
                pl.BlockSpec((rows, wide), lambda r, m: (0, 0)),
                pl.BlockSpec((rows, d), lambda r, m: (0, 0)),
                pl.BlockSpec((rows, RANK), lambda r, m: (0, 0)),
            ],
            scratch_shapes=[pltpu.VMEM((rows, d), F32), pltpu.VMEM((rows, RANK), F32)],
        ),
        out_shape=(shape((rows, wide)), shape((rows, d), F32), shape((rows, RANK))),
        compiler_params=params(48, 1),
        cost_estimate=cost(2 * rows * d * d, 12 * MIB),
        name="out",
    )(me_ref, mine, out_w, olt, orr, x_own, norm_second[None], lgu)

    second_got = together(*near_far(second_aug))
    second_ends = corners(*second_got)
    second_ends = together(*second_ends)
    dy_aug = after(dy_aug, second_ends)
    dy_far = swap(dy_aug, 3)
    dy_ends = (dy_far[: rows // 2], dy_far[rows // 2 :])
    dy_got = near_far(dy_aug)
    dys = [dy_aug, *dy_got, *dy_ends]
    seconds = [second_aug, *second_got, *second_ends]

    block = max(256, own_ff)
    steps = slice_ff // block
    fixed = lambda j: (0, 0)
    column = lambda j: (0, j)
    term_spec = pl.BlockSpec((RANK, block), column)
    low_spec = pl.BlockSpec((PAD, block), column)
    wide_spec = pl.BlockSpec((tokens, block), column)
    down_spec = pl.BlockSpec((block, d), lambda j: (j, 0))
    once = dict(pipeline_mode=pl.Buffered(1))
    kept = pl.BlockSpec((PAD, d), fixed, **once)
    weight_specs = [
        pl.BlockSpec((groups, 1, TP * strip, block), lambda j: (0, 0, 0, j)),
        pl.BlockSpec((groups, 1, TP * strip, block), lambda j: (0, 1, 0, j)),
    ]
    act, silu, slope = pl.pallas_call(
        gate_kernel,
        grid=(steps,),
        in_specs=[ANY] * 5 + weight_specs + [low_spec] * 2,
        out_specs=[wide_spec] * 3,
        scratch_shapes=[pltpu.VMEM((tokens, wide), BF), pltpu.SemaphoreType.DMA((5,))],
        out_shape=[shape((tokens, slice_ff))] * 3,
        compiler_params=params(56, 1),
        cost_estimate=cost(2 * tokens * d * slice_ff * 2, 32 * MIB),
        name="gate",
    )(*seconds, feed_w, feed_w, rg, ru)

    tall = rows + RANK
    back = pl.pallas_call(
        feed_back_kernel,
        grid=(steps,),
        in_specs=[SM]
        + [ANY] * 10
        + weight_specs
        + [down_spec]
        + [wide_spec] * 2
        + [low_spec] * 3
        + [kept],
        out_specs=[pl.BlockSpec((tall, d), fixed, **once)] * 4 + [term_spec] * 2,
        scratch_shapes=[
            pltpu.VMEM((tokens, wide), BF),
            pltpu.VMEM((tokens, wide), BF),
            pltpu.VMEM((tokens, d), F32),
            pltpu.VMEM((tokens, PAD), F32),
            pltpu.SemaphoreType.DMA((10,)),
        ],
        out_shape=[shape((tall, d))] * 4 + [shape((RANK, slice_ff), F32)] * 2,
        compiler_params=params(60, 1),
        cost_estimate=cost(2 * tokens * d * slice_ff * 3, 50 * MIB),
        name="feed_back",
    )(me_ref, *seconds, *dys, feed_w, feed_w, down_w, silu, slope, dlt, rg, ru, lgu)
    second_parts, (term_gr, term_ur) = (back[:4], back[4:])

    down = pl.pallas_call(
        down_kernel,
        grid=(steps,),
        in_specs=[ANY] * 5 + [down_spec, wide_spec, low_spec, kept],
        out_specs=[pl.BlockSpec((rows, d), fixed, **once)] * 4
        + [term_spec, pl.BlockSpec((RANK, d), fixed)],
        scratch_shapes=[
            pltpu.VMEM((tokens, wide), BF),
            pltpu.VMEM((tokens, d), F32),
            pltpu.VMEM((tokens, PAD), F32),
            pltpu.SemaphoreType.DMA((5,)),
        ],
        out_shape=[shape((rows, d))] * 4 + [shape((RANK, slice_ff), F32), shape((RANK, d), F32)],
        compiler_params=params(56, 1),
        cost_estimate=cost(2 * tokens * d * slice_ff, 24 * MIB),
        name="down",
    )(*dys, down_w, after(act, second_parts), dlt, dr_pad)
    out_parts, (term_dl, term_dr) = (down[:4], down[4:])

    adapters = joint_left.shape[0]
    bits = halves.bit_length() - 1
    turned = [sum(((i >> b) & 1) << (bits - 1 - b) for b in range(bits)) for i in range(halves)]
    share = slice_ff // halves

    def by_slice(at):
        parts = []
        for source in range(halves):
            first_column = turned[source] * share
            for t in range(TP):
                for g in range(share // own_ff):
                    group = first_column // own_ff + g
                    to = (group * TP + t) * own_ff
                    parts.append((to, own_ff, ((source, t, at + g * own_ff),)))
        return tuple(parts)

    def by_t(at, size, base=0, count=halves):
        return tuple(
            (base + t * size, size, tuple((i, t, at) for i in range(count))) for t in range(TP)
        )

    def slotted(got, plan, widths, name):
        return pl.pallas_call(
            functools.partial(slot_kernel, plan, adapters),
            out_shape=[shape((adapters, RANK, size), F32) for size in widths],
            in_specs=[VM],
            out_specs=[VM] * len(widths),
            compiler_params=params(48),
            cost_estimate=cost(adapters * seqs * RANK * sum(widths), 64 * adapters * sum(widths)),
            name=name,
        )(got)

    def over_h(value):
        at = 1
        while at < halves:
            count = value.shape[1] // 2
            upper = (h // at) % 2
            keep = lax.dynamic_slice_in_dim(value, upper * count, count, 1)
            give = lax.dynamic_slice_in_dim(value, (1 - upper) * count, count, 1)
            value = keep + flip(give.astype(BF), "h", at).astype(F32)
            at *= 2
        return value

    id_columns = jnp.full((RANK, PAD), adapter_ids[0], F32)
    width = d // TP

    second_got, out_parts = together(sent(second_parts), out_parts)
    second_terms = sum(part[rows:, : 2 * width].astype(F32) for part in second_got)

    dmix, delta_residual = pl.pallas_call(
        out_back_kernel,
        grid_spec=pltpu.PrefetchScalarGridSpec(
            num_scalar_prefetch=1,
            grid=(TP,),
            in_specs=[pl.BlockSpec((tall, d), lambda r, m: (0, 0))] * 4
            + [pl.BlockSpec((rows, d), lambda r, m: (0, 0))] * 2
            + [
                pl.BlockSpec((1, d), lambda r, m: (0, 0)),
                pl.BlockSpec((RANK, d), lambda r, m: (0, 0)),
                pl.BlockSpec((RANK, qw), lambda r, m: (0, m[0] ^ r)),
                pl.BlockSpec((rows, RANK), lambda r, m: (0, 0)),
                pl.BlockSpec((qw, d), lambda r, m: (m[0] ^ r, 0)),
                pl.BlockSpec((1, rows, qw), lambda r, m: (r, 0, 0)),
                pl.BlockSpec((RANK, d), lambda r, m: (0, 0)),
            ],
            out_specs=[
                pl.BlockSpec((1, rows + 3 * RANK, qw), lambda r, m: (r, 0, 0)),
                pl.BlockSpec((rows, d), lambda r, m: (0, 0)),
            ],
            scratch_shapes=[
                pltpu.VMEM((rows, d), BF),
                pltpu.VMEM((rows, RANK), BF),
                pltpu.VMEM((2 * RANK, d), F32),
            ],
        ),
        out_shape=(shape((TP, rows + 3 * RANK, qw)), shape((rows, d), F32)),
        compiler_params=params(48, 1),
        cost_estimate=cost(2 * rows * d * d, 16 * MIB),
        name="out_back",
    )(me_ref, *second_got, dy, residual, norm_second[None], orr, olt, out_inner, out_w, mine, term_dr)

    slice_terms = after(jnp.concatenate([term_gr, term_ur, term_dl], axis=0), dmix)
    deltas, slice_terms = together(sent(dmix), over_h(slice_terms))
    mixed_terms = sum(part[rows:].astype(F32) for part in deltas)
    early_in = jnp.concatenate(
        [slice_terms[i * RANK : (i + 1) * RANK] for i in range(3)]
        + [second_terms]
        + [mixed_terms[i * RANK : (i + 1) * RANK] for i in range(3)]
        + [id_columns],
        axis=1,
    ).astype(BF)
    deltas, early_in = together(deltas, early_in)
    early = lax.all_gather(early_in, ("s", "h", "t")).reshape(seqs, halves, TP, RANK, -1)

    dq, dkv, dslot = pl.pallas_call(
        functools.partial(attend_back_kernel, tile, ranges),
        out_shape=(
            shape((tokens, qw)),
            shape((tokens, 2 * kw), F32),
            shape((key_rows - tokens, 2 * kw)),
        ),
        in_specs=[SM] + [VM] * 12,
        out_specs=(VM, VM, VM),
        scratch_shapes=[
            pltpu.VMEM((tokens, qw), BF),
            pltpu.VMEM((tokens, qw), BF),
            pltpu.VMEM((key_rows, 2 * kw), F32),
        ],
        compiler_params=params(56),
        cost_estimate=cost(10 * pairs_done * HEAD_DIM, 12 * MIB, pairs_done),
        name="attend_back",
    )(me_ref, q, kv_all, query_marks, key_marks, lse, mixed, *deltas, cosine, sine)

    out_got = sent(after(out_parts, deltas))
    dslot = after(dslot, out_got[1:3])
    returned = [
        lax.ppermute(dslot[i * span : (i + 1) * span], "h", [(b, a) for a, b in pairs])
        for i, (shift, side, pairs) in enumerate(slots)
    ]
    layer_output = (
        residual
        + (out_got[0].astype(F32) + out_got[1].astype(F32))
        + (out_got[2].astype(F32) + out_got[3].astype(F32))
    ).astype(BF)[None]
    sides = tuple(side for _, side, _ in slots)
    dj, joint_deltas, term_jr, term_jl = pl.pallas_call(
        functools.partial(joint_terms_kernel, sides),
        out_shape=[
            shape((tokens, cols)),
            shape((tokens, PAD)),
            shape((RANK, cols), F32),
            shape((RANK, d), F32),
        ],
        in_specs=[SM] + [VM] * (2 + len(sides) + 8),
        out_specs=[VM] * 4,
        scratch_shapes=[pltpu.VMEM((tokens, 2 * kw), BF)],
        compiler_params=params(56),
        cost_estimate=cost(tokens * d * cols // 4, 12 * MIB),
        name="joint_terms",
    )(me_ref, dq, dkv, *returned, cosine, sine, jr_pad, *firsts)
    left_parts = [
        lax.dynamic_slice_in_dim(term_jl, (me ^ r) * width, width, 1).astype(BF) for r in range(TP)
    ]
    left_sent = sent(left_parts)
    first_parts = pl.pallas_call(
        joint_back_kernel,
        out_shape=[shape((rows, d))] * 4,
        in_specs=[SM] + [ANY] + [VM] * 3,
        out_specs=[VM] * 4,
        scratch_shapes=[pltpu.VMEM((d, cols), BF), pltpu.SemaphoreType.DMA((1,))],
        compiler_params=params(56),
        cost_estimate=cost(2 * tokens * d * cols, 16 * MIB),
        name="joint_back",
    )(me_ref, joint_w, dj, after(joint_deltas, out_got), jlt_pad)

    got = sent(first_parts)
    early = after(early, got[1:3])
    d_gr, d_ur, d_dl, d_gl, d_ul, d_dr, d_or, d_ol = slotted(
        early,
        tuple(by_slice(i * share) for i in range(3))
        + tuple(by_t(3 * share + i * width, width) for i in range(5)),
        (ff, ff, ff, d, d, d, d, d),
        "slots_early",
    )
    late = jnp.concatenate([sum(part.astype(F32) for part in left_sent), term_jr], axis=1)
    late = after(late, (got[1:3], d_gr))
    at = 1
    while at < halves:
        late = late + flip(late.astype(BF), "h", at).astype(F32)
        at *= 2
    late = jnp.concatenate([late, id_columns], axis=1).astype(BF)[None]
    at = 1
    while at < seqs:
        other = flip(late, "s", at)
        upper = (s_at // at) % 2 == 1
        late = jnp.concatenate(
            [jnp.where(upper, other, late), jnp.where(upper, late, other)], axis=0
        )
        at *= 2
    late_got = [late, swap(late, 1), swap(late, 2), swap(late, 3)]
    low = [jnp.where(me % 2 == 1, late_got[i ^ 1], late_got[i]) for i in range(TP)]
    late = jnp.stack([jnp.where(me >= 2, low[i ^ 2], low[i]) for i in range(TP)], axis=1)[:, None]
    delta_first = (got[0].astype(F32) + got[1].astype(F32)) + (
        got[2].astype(F32) + got[3].astype(F32)
    )
    input_delta = (delta_residual + norm_back(x32, norm_first, delta_first)).astype(BF)[None]
    d_jl, d_jr = slotted(
        late,
        (
            by_t(0, width, 0, 1),
            by_t(width, qw, 0, 1)
            + by_t(width + qw, kw, q_end, 1)
            + by_t(width + qw + kw, kw, k_end, 1),
        ),
        (d, HEADS * HEAD_DIM + 2 * KV_HEADS * HEAD_DIM),
        "slots_late",
    )

    def left(value):
        return jnp.swapaxes(value, 1, 2)

    return (
        layer_output,
        input_delta,
        left(d_jl),
        d_jr,
        left(d_ol),
        d_or,
        left(d_gl),
        d_gr,
        left(d_ul),
        d_ur,
        left(d_dl),
        d_dr,
    )


def solution(mesh):
    seqs, ctx = (mesh.shape["seq"], mesh.shape["ctx"])
    inner = Mesh(mesh.devices.reshape(seqs, ctx // TP, TP), ("s", "h", "t"))
    acts = P("s", ("h", "t"), None)
    weight = P(("s", "h", "t"), None)
    placed = (
        (acts, acts, P(), P())
        + (weight,) * 5
        + (P(),) * 10
        + (P("s", None), P("s"))
    )
    return jax.shard_map(
        per_device,
        mesh=inner,
        in_specs=placed,
        out_specs=(acts, acts) + (P(),) * 10,
        check_vma=False,
    )
```

```python
import functools

import jax
import jax.numpy as jnp
from jax import lax
from jax.experimental import pallas as pl
from jax.experimental.pallas import tpu as pltpu
from jax.sharding import Mesh, PartitionSpec as P

HEADS = 16
KV_HEADS = 8
HEAD_DIM = 128
WINDOW = 1024
FIRST_DOC = 1536
RANK = 16
PAD = 128
TP = 4

epsilon = 1e-06
rotary_base = 1000000.0
masked_score = -1e30

BF = jnp.bfloat16
F32 = jnp.float32
MIB = 1024 * 1024


def dot(left, right):
    return jnp.dot(left, right, preferred_element_type=F32)


def dot_t(left, right):
    return lax.dot_general(left, right, (((1,), (1,)), ((), ())), preferred_element_type=F32)


def t_dot(left, right):
    return lax.dot_general(left, right, (((0,), (0,)), ((), ())), preferred_element_type=F32)


def params(mib, grid=0):
    extra = {"dimension_semantics": ("arbitrary",) * grid} if grid else {}
    return pltpu.CompilerParams(vmem_limit_bytes=mib * MIB, **extra)


def cost(flops, nbytes, trans=0):
    return pl.CostEstimate(flops=int(flops), bytes_accessed=int(nbytes), transcendentals=int(trans))


VM = pl.BlockSpec(memory_space=pltpu.VMEM)
SM = pl.BlockSpec(memory_space=pltpu.SMEM)
ANY = pl.BlockSpec(memory_space=pl.ANY)


def half_range(side, h, span, length):
    start = span * h if side == 0 else length - span * (h + 1)
    return (start, start + span)


def may_see(q, k):
    grain = 64
    for q0 in range(q[0], q[1], grain):
        for k0 in range(k[0], k[1], grain):
            same = (q0 >= FIRST_DOC) == (k0 >= FIRST_DOC)
            if same and k0 < q0 + grain and q0 - (k0 + grain - 1) < WINDOW:
                return True
    return False


def key_plan(halves, span, length):
    slots = []
    for shift in list(range(halves - 1, 0, -1)) + list(range(-1, -halves, -1)):
        for side in (0, 1):
            pairs = []
            for h in range(halves):
                source = h - shift
                if not 0 <= source < halves:
                    continue
                wanted = half_range(side, source, span, length)
                if any(may_see(half_range(s, h, span, length), wanted) for s in (0, 1)):
                    pairs.append((source, h))
            if pairs:
                slots.append((shift, side, tuple(pairs)))
    tile = min(256, span)
    step = 128
    ranges = []
    for i in range(2 * span // tile):
        low, high = (1 << 30, 0)
        for h in range(halves):
            side, inside = divmod(i * tile, span)
            base = half_range(side, h, span, length)[0] + inside
            held = []
            for shift, key_side, pairs in slots:
                held.append(
                    half_range(key_side, h - shift, span, length) if (h - shift, h) in pairs else None
                )
            held += [half_range(s, h, span, length) for s in (0, 1)]
            for index, region in enumerate(held):
                if region is None:
                    continue
                for offset in range(0, span, step):
                    block = (region[0] + offset, region[0] + min(offset + step, span))
                    if may_see((base, base + tile), block):
                        low = min(low, index * span + offset)
                        high = max(high, index * span + offset + step)
        ranges.append((low, min(high, (len(slots) + 2) * span)))
    return (slots, tile, ranges)


def place_rows(me, r, rows):
    half = rows // 2
    other = me ^ r
    first = pl.multiple_of(other * half, half)
    second = pl.multiple_of(TP * half + (TP - 1 - other) * half, half)
    return ((0, first), (half, second))


def cut_kernel(wide, me_ref, joint_ref, gate_ref, up_ref, *outs):
    me = me_ref[0]
    joints, feeds = (outs[:TP], outs[TP:])
    cols = joints[0].shape[1]
    kw = KV_HEADS // TP * HEAD_DIM
    qw = cols - 2 * kw
    for r in range(TP):
        other = me ^ r
        start = 0
        base = 0
        for width, count in ((qw, TP), (kw, TP), (kw, TP)):
            joints[r][:, start : start + width] = joint_ref[
                :, pl.ds(pl.multiple_of(base + other * width, HEAD_DIM), width)
            ]
            start += width
            base += width * count
        for g in range(feeds[r].shape[2] // wide if feeds else 0):
            at = pl.ds(pl.multiple_of((g * TP + other) * wide, wide), wide)
            feeds[r][0, :, g * wide : (g + 1) * wide] = gate_ref[:, at]
            feeds[r][1, :, g * wide : (g + 1) * wide] = up_ref[:, at]


def natural_kernel(count, me_ref, *refs):
    parts, (out_ref, sem) = (refs[:count], refs[-2:])
    me = me_ref[0]
    strip = parts[0].shape[-2]
    copies = []
    for r, ref in enumerate(parts):
        rows = pl.ds(pl.multiple_of((me ^ r) * strip, strip), strip)
        to = out_ref.at[rows, :] if len(ref.shape) == 2 else out_ref.at[:, rows, :]
        copies.append(pltpu.make_async_copy(ref, to, sem.at[r]))
    for copy in copies:
        copy.start()
    for copy in copies:
        copy.wait()


def strips_kernel(layout, strip, me_ref, *refs):
    out_ref, sem = refs[-2:]
    me, place = (me_ref[0], me_ref[1])
    copies = []
    for ref, (r, groups) in zip(refs, layout):
        for i, group in enumerate(groups):
            row = pl.multiple_of(((place ^ group) * TP + (me ^ r)) * strip, strip)
            copies.append(
                pltpu.make_async_copy(
                    ref.at[pl.ds(i * strip, strip), :],
                    out_ref.at[pl.ds(row, strip), :],
                    sem.at[len(copies)],
                )
            )
    for copy in copies:
        copy.start()
    for copy in copies:
        copy.wait()


def load_pieces(place, pieces, target, sem):
    strip = pieces[0].shape[0]
    if len(pieces) == 1:
        copies = [pltpu.make_async_copy(pieces[0], target, sem.at[0])]
        copies[0].start()
        return copies
    copies = []
    for r, ref in enumerate(pieces):
        rows = pl.ds(pl.multiple_of((place ^ r) * strip, strip), strip)
        copies.append(pltpu.make_async_copy(ref, target.at[rows, :], sem.at[r]))
    for copy in copies:
        copy.start()
    return copies


def qkv_kernel(count, me_ref, *refs):
    pieces = refs[:count]
    (x0, x1, x2, x3a, x3b, jr_ref, cos_ref, sin_ref) = refs[count : count + 8]
    (q_ref, kv_ref, w_ref, sem) = refs[-4:]
    me = me_ref[0]
    copies = load_pieces(me_ref[1], pieces, w_ref, sem)
    rows, wide = x0.shape
    d = wide - PAD
    half = rows // 2
    nq = q_ref.shape[1] // HEAD_DIM
    nk = kv_ref.shape[1] // HEAD_DIM // 2
    for copy in copies:
        copy.wait()
    for r, x_refs in enumerate(((x0,), (x1,), (x2,), (x3a, x3b))):
        x = jnp.concatenate([ref[...] for ref in x_refs], axis=0)
        joined = dot(x[:, :d], w_ref[...]) + dot(x[:, d:], jr_ref[...])
        for source, target in place_rows(me, r, rows):
            part = joined[source : source + half]
            cosine = cos_ref[pl.ds(target, half), :]
            sine = sin_ref[pl.ds(target, half), :]
            for head in range(nq + nk):
                u = part[:, head * HEAD_DIM : (head + 1) * HEAD_DIM]
                turned = (u * cosine + pltpu.roll(u, HEAD_DIM // 2, 1) * sine).astype(BF)
                if head < nq:
                    q_ref[pl.ds(target, half), head * HEAD_DIM : (head + 1) * HEAD_DIM] = turned
                else:
                    at = head - nq
                    kv_ref[pl.ds(target, half), at * HEAD_DIM : (at + 1) * HEAD_DIM] = turned
            kv_ref[pl.ds(target, half), nk * HEAD_DIM :] = part[:, (nq + nk) * HEAD_DIM :].astype(BF)


def head_columns(ref, rows, first, count):
    return jnp.concatenate(
        [ref[rows, (first + i) * HEAD_DIM : (first + i + 1) * HEAD_DIM] for i in range(count)], axis=0
    )


def bias_of(qpos_ref, kpos_ref, rows, low, high, group):
    distance = qpos_ref[rows, :] - kpos_ref[:, low:high]
    bias = jnp.where((distance >= 0) & (distance < WINDOW), 0.0, masked_score).astype(F32)
    return jnp.concatenate([bias] * group, axis=0)


def attend_kernel(tile, ranges, me_ref, q_ref, kv_ref, qpos_ref, kpos_ref, mixed_ref, lse_ref, held):
    me = me_ref[0]
    rows = mixed_ref.shape[1]
    half = rows // 2
    nk = kv_ref.shape[1] // HEAD_DIM // 2
    group = q_ref.shape[1] // HEAD_DIM // nk
    scale = HEAD_DIM ** (-0.5)
    for i, (low, high) in enumerate(ranges):
        here = slice(i * tile, (i + 1) * tile)
        bias = bias_of(qpos_ref, kpos_ref, here, low, high, group)
        for head in range(nk):
            q = head_columns(q_ref, here, head * group, group)
            k = kv_ref[low:high, head * HEAD_DIM : (head + 1) * HEAD_DIM]
            v = kv_ref[low:high, (nk + head) * HEAD_DIM : (nk + head + 1) * HEAD_DIM]
            scores = dot_t(q, k) * scale + bias
            largest = jnp.max(scores, axis=-1, keepdims=True)
            raised = jnp.exp(scores - largest)
            total = jnp.sum(raised, axis=-1, keepdims=True)
            out = dot((raised * (1.0 / total)).astype(BF), v).astype(BF)
            lse = largest + jnp.log(total)
            for g in range(group):
                at = head * group + g
                held[here, at * HEAD_DIM : (at + 1) * HEAD_DIM] = out[g * tile : (g + 1) * tile]
                lse_ref[here, at : at + 1] = lse[g * tile : (g + 1) * tile]
    for r in range(TP):
        for source, target in place_rows(me, r, rows):
            mixed_ref[r, source : source + half, :] = held[pl.ds(target, half), :]


def attend_back_kernel(
    tile,
    ranges,
    me_ref,
    q_ref,
    kv_ref,
    qpos_ref,
    kpos_ref,
    lse_ref,
    mixed_ref,
    d0,
    d1,
    d2,
    d3,
    cos_ref,
    sin_ref,
    dq_ref,
    dkv_ref,
    dslot_ref,
    held,
    given,
    total_ref,
):
    me = me_ref[0]
    rows = mixed_ref.shape[1]
    half = rows // 2
    nk = kv_ref.shape[1] // HEAD_DIM // 2
    group = q_ref.shape[1] // HEAD_DIM // nk
    scale = HEAD_DIM ** (-0.5)
    for r, d_ref in enumerate((d0, d1, d2, d3)):
        for source, target in place_rows(me, r, rows):
            held[pl.ds(target, half), :] = mixed_ref[r, source : source + half, :]
            given[pl.ds(target, half), :] = d_ref[source : source + half, :]
    total_ref[...] = jnp.zeros_like(total_ref)
    for i, (low, high) in enumerate(ranges):
        here = slice(i * tile, (i + 1) * tile)
        bias = bias_of(qpos_ref, kpos_ref, here, low, high, group)
        cosine = cos_ref[here, :]
        sine = sin_ref[here, :]
        for head in range(nk):
            key_columns = slice(head * HEAD_DIM, (head + 1) * HEAD_DIM)
            value_columns = slice((nk + head) * HEAD_DIM, (nk + head + 1) * HEAD_DIM)
            q = head_columns(q_ref, here, head * group, group)
            out = head_columns(held, here, head * group, group)
            delta = head_columns(given, here, head * group, group)
            lse = jnp.concatenate(
                [lse_ref[here, head * group + g : head * group + g + 1] for g in range(group)], axis=0
            )
            k = kv_ref[low:high, key_columns]
            v = kv_ref[low:high, value_columns]
            chances = jnp.exp(dot_t(q, k) * scale + bias - lse)
            inner = jnp.sum(out.astype(F32) * delta.astype(F32), axis=-1, keepdims=True)
            raw = (chances * (dot_t(delta, v) - inner) * scale).astype(BF)
            dq = dot(raw, k)
            for g in range(group):
                at = head * group + g
                e = dq[g * tile : (g + 1) * tile]
                back = e * cosine - pltpu.roll(e, HEAD_DIM // 2, 1) * sine
                dq_ref[here, at * HEAD_DIM : (at + 1) * HEAD_DIM] = back.astype(BF)
            total_ref[low:high, key_columns] += t_dot(raw, q)
            total_ref[low:high, value_columns] += t_dot(chances.astype(BF), delta)
    extra = dslot_ref.shape[0]
    dslot_ref[...] = total_ref[:extra, :].astype(BF)
    dkv_ref[...] = total_ref[extra:, :]


def out_kernel(
    me_ref, m_ref, w_ref, olt_ref, or_ref, x_ref, gain_ref, lgu_ref, aug_ref, res_ref, oi_ref, acc, inner
):
    r = pl.program_id(0)
    d = x_ref.shape[1]

    @pl.when(r == 0)
    def _():
        acc[...] = x_ref[...].astype(F32)
        inner[...] = jnp.zeros_like(inner)

    m = m_ref[0]
    acc[...] += dot(m, w_ref[...])
    inner[...] += dot_t(m, olt_ref[...])

    @pl.when(r == TP - 1)
    def _():
        low = inner[...].astype(BF)
        oi_ref[...] = low
        residual = acc[...] + dot(low, or_ref[...])
        res_ref[...] = residual
        factor = lax.rsqrt(jnp.mean(residual * residual, axis=-1, keepdims=True) + epsilon)
        second = (residual * factor * gain_ref[...]).astype(BF)
        aug_ref[:, :d] = second
        aug_ref[:, d:] = dot_t(second, lgu_ref[...]).astype(BF)


def out_back_kernel(
    me_ref,
    p0,
    p1,
    p2,
    p3,
    dy_ref,
    res_ref,
    gain_ref,
    or_ref,
    olt_ref,
    oi_ref,
    w_ref,
    m_ref,
    tdr_ref,
    dmix_ref,
    dres_ref,
    branch,
    inner,
    terms,
):
    r = pl.program_id(0)
    rows, d = dy_ref.shape
    width = d // TP

    @pl.when(r == 0)
    def _():
        gain = gain_ref[...]
        incoming = (p0[:rows].astype(F32) + p1[:rows].astype(F32)) + (
            p2[:rows].astype(F32) + p3[:rows].astype(F32)
        )
        v = res_ref[...]
        factor = lax.rsqrt(jnp.mean(v * v, axis=-1, keepdims=True) + epsilon)
        scaled = incoming * gain
        back = factor * scaled - v * (factor * factor * factor) * jnp.mean(
            scaled * v, axis=-1, keepdims=True
        )
        delta = dy_ref[...].astype(F32) + back
        dres_ref[...] = delta
        low = delta.astype(BF)
        branch[...] = low
        inner[...] = dot_t(low, or_ref[...]).astype(BF)
        terms[:RANK] = tdr_ref[...]
        terms[RANK:] = t_dot(oi_ref[...], low)

    dmix_ref[0, :rows] = (dot_t(branch[...], w_ref[...]) + dot(inner[...], olt_ref[...])).astype(BF)
    at = pl.ds(pl.multiple_of((me_ref[0] ^ r) * width, width), width)
    dmix_ref[0, rows : rows + 2 * RANK] = terms[:, at].astype(BF)
    dmix_ref[0, rows + 2 * RANK :] = t_dot(inner[...], m_ref[0]).astype(BF)


def load_rows(refs, stores, sem):
    copies = []
    for some, store in zip(refs, stores):
        at = 0
        for ref in some:
            copies.append(
                pltpu.make_async_copy(
                    ref, store.at[pl.ds(at, ref.shape[0]), :], sem.at[len(copies)]
                )
            )
            at += ref.shape[0]
    for copy in copies:
        copy.start()
    for copy in copies:
        copy.wait()


def gate_kernel(*refs):
    xs, refs = (refs[:5], refs[5:])
    (gate_ref, up_ref, rg_ref, ru_ref, act_ref, silu_ref, slope_ref, x_all, sem) = refs
    d = x_all.shape[1] - PAD

    @pl.when(pl.program_id(0) == 0)
    def _():
        load_rows((xs,), (x_all,), sem)

    block = gate_ref.shape[-1]
    gate_w = gate_ref[...].reshape(d, block)
    up_w = up_ref[...].reshape(d, block)
    count = x_all.shape[0]
    take = min(512, count)
    for start in range(0, count, take):
        here = slice(start, start + take)
        x = x_all[here, :d]
        xi = x_all[here, d:]
        gate = dot(x, gate_w) + dot(xi, rg_ref[...])
        up = dot(x, up_w) + dot(xi, ru_ref[...])
        sigmoid = jax.nn.sigmoid(gate)
        silu = gate * sigmoid
        act_ref[here, :] = (silu * up).astype(BF)
        silu_ref[here, :] = silu.astype(BF)
        slope_ref[here, :] = (up * sigmoid * (1.0 + gate * (1.0 - sigmoid))).astype(BF)


def feed_back_kernel(me_ref, *refs):
    xs, ys, refs = (refs[:5], refs[5:9], refs[9:])
    (gate_ref, up_ref, down_ref, silu_ref, slope_ref, dlt_ref, rg_ref, ru_ref, lgu_ref, *refs) = refs
    (s0, s1, s2, s3, tgr_ref, tur_ref, x_all, y_all, acc_second, acc_inner, sem) = refs
    me = me_ref[0]
    j = pl.program_id(0)
    d = acc_second.shape[1]
    rows = x_all.shape[0] // TP

    @pl.when(j == 0)
    def _():
        load_rows((xs, ys), (x_all, y_all), sem)
        acc_second[...] = jnp.zeros_like(acc_second)
        acc_inner[...] = jnp.zeros_like(acc_inner)

    block = gate_ref.shape[-1]
    gate_w = gate_ref[...].reshape(d, block)
    up_w = up_ref[...].reshape(d, block)
    down_w = down_ref[...]
    dlt, rg, ru = (dlt_ref[...], rg_ref[...], ru_ref[...])
    term_g = jnp.zeros((PAD, block), F32)
    term_u = jnp.zeros((PAD, block), F32)
    take = min(512, TP * rows)
    for start in range(0, TP * rows, take):
        here = slice(start, start + take)
        delta = dot_t(y_all[here, :d], down_w) + dot(y_all[here, d:], dlt)
        delta_gate = (delta * slope_ref[here, :].astype(F32)).astype(BF)
        delta_up = (delta * silu_ref[here, :].astype(F32)).astype(BF)
        acc_second[here, :] += dot_t(delta_gate, gate_w) + dot_t(delta_up, up_w)
        acc_inner[here, :] += dot_t(delta_gate, rg) + dot_t(delta_up, ru)
        tail = x_all[here, d:]
        term_g += t_dot(tail, delta_gate)
        term_u += t_dot(tail, delta_up)
    tgr_ref[...] = term_g[RANK : 2 * RANK]
    tur_ref[...] = term_u[2 * RANK : 3 * RANK]

    @pl.when(j == pl.num_programs(0) - 1)
    def _():
        inner = acc_inner[...].astype(BF)
        width = d // TP
        for r, s_ref in enumerate((s0, s1, s2, s3)):
            here = slice(r * rows, (r + 1) * rows)
            s_ref[:rows, :] = (acc_second[here, :] + dot(inner[here], lgu_ref[...])).astype(BF)
            at = pl.ds(pl.multiple_of((me ^ r) * width, width), width)
            term = t_dot(inner, x_all[:, at]).astype(BF)
            s_ref[rows:, :width] = term[RANK : 2 * RANK]
            s_ref[rows:, width : 2 * width] = term[2 * RANK : 3 * RANK]
            s_ref[rows:, 2 * width :] = jnp.zeros((RANK, d - 2 * width), BF)


def down_kernel(*refs):
    ys, refs = (refs[:4], refs[4:])
    (down_ref, act_ref, dlt_ref, dr_ref, o0, o1, o2, o3, tdl_ref, tdr_ref, *refs) = refs
    (y_all, acc, acc_inner, sem) = refs
    j = pl.program_id(0)
    rows = o0.shape[0]
    d = acc.shape[1]

    @pl.when(j == 0)
    def _():
        load_rows((ys,), (y_all,), sem)
        acc[...] = jnp.zeros_like(acc)
        acc_inner[...] = jnp.zeros_like(acc_inner)

    acc[...] += dot(act_ref[...], down_ref[...])
    acc_inner[...] += dot_t(act_ref[...], dlt_ref[...])
    tdl_ref[...] = t_dot(y_all[:, d:], act_ref[...])[:RANK]

    @pl.when(j == pl.num_programs(0) - 1)
    def _():
        inner = acc_inner[...].astype(BF)
        tdr_ref[...] = t_dot(inner, y_all[:, :d])[:RANK]
        for r, o_ref in enumerate((o0, o1, o2, o3)):
            here = slice(r * rows, (r + 1) * rows)
            o_ref[...] = (acc[here, :] + dot(inner[here], dr_ref[...])).astype(BF)


def slot_kernel(plan, adapters, got_ref, *outs):
    seqs, halves = got_ref.shape[:2]
    marks = []
    for i in range(seqs):
        ids = got_ref[i, 0, 0, :, -PAD:].astype(F32)
        marks.append(
            [
                jnp.max(jnp.where(ids == float(e), 1.0, 0.0), axis=1, keepdims=True)
                for e in range(adapters)
            ]
        )
    for out_ref, parts in zip(outs, plan):
        for to, width, sources in parts:
            values = []
            for i in range(seqs):
                total = None
                for h, t, at in sources:
                    part = got_ref[i, h, t, :, at : at + width].astype(F32)
                    total = part if total is None else total + part
                values.append(total)
            for e in range(adapters):
                out_ref[e, :, to : to + width] = sum(
                    marks[i][e] * values[i] for i in range(seqs)
                )


def joint_terms_kernel(sides, me_ref, dq_ref, dkv_ref, *refs):
    extra, refs = (refs[: len(sides)], refs[len(sides) :])
    (cos_ref, sin_ref, jr_ref, x0, x1, x2, x3a, x3b, dj, inner_ref, tjr_ref, tjl_ref, keys) = refs
    me = me_ref[0]
    rows, wide = x0.shape
    d = wide - PAD
    half = rows // 2
    span = TP * half
    nk = dkv_ref.shape[1] // HEAD_DIM // 2
    query_width = dq_ref.shape[1]
    for side in (0, 1):
        here = slice(side * span, (side + 1) * span)
        total = dkv_ref[here, :]
        for ref, owner in zip(extra, sides):
            if owner == side:
                total = total + ref[...].astype(F32)
        for head in range(nk):
            e = total[:, head * HEAD_DIM : (head + 1) * HEAD_DIM]
            back = e * cos_ref[here, :] - pltpu.roll(e, HEAD_DIM // 2, 1) * sin_ref[here, :]
            keys[here, head * HEAD_DIM : (head + 1) * HEAD_DIM] = back.astype(BF)
        keys[here, nk * HEAD_DIM :] = total[:, nk * HEAD_DIM :].astype(BF)
    for r in range(TP):
        for source, target in place_rows(me, r, rows):
            to = slice(r * rows + source, r * rows + source + half)
            dj[to, :query_width] = dq_ref[pl.ds(target, half), :]
            dj[to, query_width:] = keys[pl.ds(target, half), :]
    term_r = jnp.zeros((PAD, dj.shape[1]), F32)
    term_l = jnp.zeros((PAD, d), F32)
    for r, x_refs in enumerate(((x0,), (x1,), (x2,), (x3a, x3b))):
        x = jnp.concatenate([ref[...] for ref in x_refs], axis=0)
        here = slice(r * rows, (r + 1) * rows)
        inner = dot_t(dj[here, :], jr_ref[...]).astype(BF)
        inner_ref[here, :] = inner
        term_r += t_dot(x[:, d:], dj[here, :])
        term_l += t_dot(inner, x[:, :d])
    tjr_ref[...] = term_r[:RANK]
    tjl_ref[...] = term_l[:RANK]


def joint_back_kernel(me_ref, *refs):
    pieces = refs[:-9]
    (dj, inner, jlt_ref, f0, f1, f2, f3, w_ref, sem) = refs[-9:]
    for copy in load_pieces(me_ref[1], pieces, w_ref, sem):
        copy.wait()
    rows = f0.shape[0]
    for r, f_ref in enumerate((f0, f1, f2, f3)):
        here = slice(r * rows, (r + 1) * rows)
        f_ref[...] = (dot_t(dj[here, :], w_ref[...]) + dot(inner[here, :], jlt_ref[...])).astype(BF)


def shape(dims, dtype=BF):
    return jax.ShapeDtypeStruct(dims, dtype)


def swap(value, r):
    return lax.ppermute(value, "t", [(i, i ^ r) for i in range(TP)])


def near_far(value):
    return (swap(value, 1), swap(value, 2))


def corners(near, far):
    half = near.shape[0] // 2
    return (swap(near[:half], 2), swap(far[half:], 1))


def sent(parts):
    return [parts[0]] + [swap(parts[r], r) for r in range(1, TP)]


def after(value, *others):
    return lax.optimization_barrier((value, others))[0]


def together(*values):
    return lax.optimization_barrier(values)


def flip(value, axis, bit):
    size = lax.axis_size(axis)
    return lax.ppermute(value, axis, [(i, i ^ bit) for i in range(size)])


def collect_first(value, seqs, halves):
    held = {0: value}
    for i in range(halves.bit_length() - 1):
        held[1 << i] = flip(value, "h", 1 << i)
    for i in range(1, seqs.bit_length() - 1):
        held[halves << i] = flip(value, "s", 1 << i)
    return held


def collect_rest(held, seqs, halves):
    held = dict(held)
    bits = [("h", 1 << i, 1 << i) for i in range(halves.bit_length() - 1)]
    bits += [("s", 1 << i, halves << i) for i in range(1, seqs.bit_length() - 1)]
    for axis, bit, offset in bits:
        for index in sorted(held):
            if index < offset and index | offset not in held:
                held[index | offset] = flip(held[index], axis, bit)
    return held


def norm_back(values, gain, incoming):
    factor = lax.rsqrt(jnp.mean(values * values, axis=-1, keepdims=True) + epsilon)
    scaled = incoming * gain
    return factor * scaled - values * (factor * factor * factor) * jnp.mean(
        scaled * values, axis=-1, keepdims=True
    )


def per_device(
    hidden,
    out_grad,
    norm_first,
    norm_second,
    joint_weight,
    out_weight,
    gate_weight,
    up_weight,
    down_weight,
    joint_left,
    joint_right,
    out_left,
    out_right,
    gate_left,
    gate_right,
    up_left,
    up_right,
    down_left,
    down_right,
    doc_lengths,
    adapter_ids,
):
    seqs = lax.axis_size("s")
    halves = lax.axis_size("h")
    groups = seqs * halves
    rows, d = hidden.shape[1:]
    half = rows // 2
    span = TP * half
    tokens = TP * rows
    length = rows * TP * halves
    strip = joint_weight.shape[0]
    ff = gate_weight.shape[1]
    own_ff = down_weight.shape[0]
    slice_ff = groups * own_ff
    wide = d + PAD
    nq = HEADS // TP
    nk = KV_HEADS // TP
    qw = nq * HEAD_DIM
    kw = nk * HEAD_DIM
    cols = qw + 2 * kw
    me = lax.axis_index("t")
    h = lax.axis_index("h")
    s_at = lax.axis_index("s")
    place = s_at * halves + h
    me_ref = jnp.stack([me, place]).astype(jnp.int32)
    slots, tile, ranges = key_plan(halves, span, length)

    adapter = adapter_ids[0]

    def pick(factor):
        return lax.dynamic_index_in_dim(factor, adapter, 0, keepdims=False)

    def pick_left(factor):
        return pick(jnp.swapaxes(factor, 1, 2))

    def padded(value, first):
        return jnp.pad(value, ((first, PAD - first - value.shape[0]), (0, 0)))

    q_end = HEADS * HEAD_DIM
    k_end = q_end + KV_HEADS * HEAD_DIM
    x_own = hidden[0]
    x32 = x_own.astype(F32)
    first = (
        x32 * lax.rsqrt(jnp.mean(x32 * x32, axis=-1, keepdims=True) + epsilon) * norm_first
    ).astype(BF)
    jlt_pad = padded(pick_left(joint_left), 0)
    first_aug = jnp.concatenate([first, dot_t(first, jlt_pad).astype(BF)], axis=1)

    whole_lanes = own_ff % HEAD_DIM == 0
    feed_shapes = [shape((2, strip, slice_ff))] * (TP if whole_lanes else 0)
    cut = pl.pallas_call(
        functools.partial(cut_kernel, own_ff),
        out_shape=[shape((strip, cols))] * TP + feed_shapes,
        in_specs=[SM] + [VM] * 3,
        out_specs=[VM] * (TP + len(feed_shapes)),
        compiler_params=params(24),
        cost_estimate=cost(0, 6 * MIB),
        name="cut",
    )(me_ref, joint_weight, gate_weight, up_weight)
    feed_parts = cut[TP:]
    if not whole_lanes:
        both = jnp.stack([gate_weight, up_weight]).reshape(2, strip, groups, TP, own_ff)
        feed_parts = [
            lax.dynamic_index_in_dim(both, me ^ r, 3, keepdims=False).reshape(2, strip, slice_ff)
            for r in range(TP)
        ]

    def natural(parts, out, *others):
        return pl.pallas_call(
            functools.partial(natural_kernel, TP),
            out_shape=out,
            in_specs=[SM] + [ANY] * (TP + len(others)),
            out_specs=ANY,
            scratch_shapes=[pltpu.SemaphoreType.DMA((TP,))],
            compiler_params=params(8),
            cost_estimate=cost(0, 4 * MIB),
            name="natural",
        )(me_ref, *parts, *others)

    def ff_slice(value):
        return lax.dynamic_index_in_dim(
            value.reshape(RANK, groups, TP, own_ff), me, 2, keepdims=False
        ).reshape(RANK, slice_ff)

    jr = pick(joint_right)
    jr_own = jnp.concatenate(
        [
            lax.dynamic_slice_in_dim(jr[:, :q_end], me * qw, qw, 1),
            lax.dynamic_slice_in_dim(jr[:, q_end:k_end], me * kw, kw, 1),
            lax.dynamic_slice_in_dim(jr[:, k_end:], me * kw, kw, 1),
        ],
        axis=1,
    )
    jr_pad = padded(jr_own, 0)
    olt = pick_left(out_left)
    orr = pick(out_right)
    lgu = jnp.pad(
        jnp.concatenate([pick_left(gate_left), pick_left(up_left)], axis=0),
        ((RANK, PAD - 3 * RANK), (0, 0)),
    )
    rg = padded(ff_slice(pick(gate_right)), RANK)
    ru = padded(ff_slice(pick(up_right)), 2 * RANK)
    dlt = padded(ff_slice(pick_left(down_left)), 0)

    index = jnp.arange(span, dtype=jnp.int32)

    def side_places(side, at):
        return (span * at if side == 0 else length - span * (at + 1)) + index

    ends = jnp.cumsum(doc_lengths[0])

    def marked(places):
        documents = jnp.sum((places[:, None] >= ends[None, :]).astype(jnp.int32), axis=1)
        return places + documents * (4 * length)

    own_places = jnp.concatenate([side_places(0, h), side_places(1, h)])
    own_marks = marked(own_places)
    slot_marks = []
    for shift, side, pairs in slots:
        valid = functools.reduce(jnp.logical_or, [h == target for _, target in pairs])
        slot_marks.append(jnp.where(valid, marked(side_places(side, h - shift)), 1 << 29))
    key_marks = jnp.concatenate(slot_marks + [own_marks])[None, :]
    query_marks = own_marks[:, None]
    inverse = rotary_base ** (-jnp.arange(HEAD_DIM // 2, dtype=F32) * 2.0 / HEAD_DIM)
    angles = own_places.astype(F32)[:, None] * inverse[None, :]
    cosine = jnp.concatenate([jnp.cos(angles)] * 2, axis=1)
    sine = jnp.sin(angles)
    sine = jnp.concatenate([-sine, sine], axis=1)

    dy = out_grad[0]
    dr_pad = padded(pick(down_right), 0)
    dy_aug = jnp.concatenate([dy, dot_t(dy, dr_pad).astype(BF)], axis=1)

    joint_sent, out_held = together(sent(cut[:TP]), collect_first(out_weight, seqs, halves))
    joint_cut = natural(joint_sent, shape((TP * strip, cols)))
    joint_w = lax.all_gather(joint_cut, ("s", "h"), axis=0, tiled=True)

    feed_parts, first_aug, out_held, _ = together(feed_parts, first_aug, out_held, joint_cut)
    first_got, (rg, ru, dlt, lgu, olt, orr, dr_pad, dy_aug) = together(
        near_far(first_aug), (rg, ru, dlt, lgu, olt, orr, dr_pad, dy_aug)
    )
    joint_w = after(joint_w, first_got)
    down_w = lax.all_gather(after(down_weight, joint_w), ("s", "h"), axis=0, tiled=True)
    feed_parts, out_held = after((feed_parts, out_held), first_got)
    first_ends, out_held, feed_sent = together(
        corners(*first_got), collect_rest(out_held, seqs, halves), sent(feed_parts)
    )
    held_groups = tuple(sorted(out_held))
    out_mine = jnp.concatenate([out_held[i] for i in held_groups], axis=0)
    firsts = [first_aug, *first_got, *first_ends]

    q, kv = pl.pallas_call(
        functools.partial(qkv_kernel, 1),
        out_shape=(shape((tokens, qw)), shape((tokens, 2 * kw))),
        in_specs=[SM] + [ANY] + [VM] * 8,
        out_specs=(VM, VM),
        scratch_shapes=[pltpu.VMEM((d, cols), BF), pltpu.SemaphoreType.DMA((1,))],
        compiler_params=params(48),
        cost_estimate=cost(2 * tokens * wide * cols, 10 * MIB),
        name="qkv",
    )(me_ref, joint_w, *firsts, jr_pad, cosine, sine)

    out_mine = after(out_mine, q)
    pieces, out_got, own_core = together(
        [
            lax.ppermute(kv[side * span : (side + 1) * span], "h", pairs)
            for shift, side, pairs in slots
        ],
        near_far(out_mine),
        flip(out_mine, "s", 1),
    )
    down_w, feed_sent = after((down_w, feed_sent), pieces)
    feed_cut = natural(feed_sent, shape((2, TP * strip, slice_ff)))
    feed_w = lax.all_gather(after(feed_cut, down_w)[None], ("s", "h"), axis=0, tiled=True)
    kv_all = jnp.concatenate(pieces + [kv], axis=0)
    key_rows = kv_all.shape[0]
    pairs_done = sum((high - low) * tile for low, high in ranges) * nq

    out_ends = corners(*after(out_got, pieces))
    mixed, lse = pl.pallas_call(
        functools.partial(attend_kernel, tile, ranges),
        out_shape=(shape((TP, rows, qw)), shape((tokens, nq), F32)),
        in_specs=[SM] + [VM] * 4,
        out_specs=(VM, VM),
        scratch_shapes=[pltpu.VMEM((tokens, qw), BF)],
        compiler_params=params(48),
        cost_estimate=cost(4 * pairs_done * HEAD_DIM, 6 * MIB, pairs_done),
        name="attend",
    )(me_ref, q, kv_all, query_marks, key_marks)

    mixed_sent = after(mixed, out_ends)
    mine, out_cores = together(
        sent(mixed_sent), [flip(block, "s", 1) for block in after(out_got, mixed)]
    )
    mine = jnp.stack(mine)
    end_cores = together(*[flip(block, "s", 1) for block in out_ends])
    out_blocks = [out_mine, *out_got, *out_ends, own_core, *out_cores, *end_cores]
    cut_at = len(held_groups) // 2
    layout = [(0, held_groups), (1, held_groups), (2, held_groups)]
    layout += [(3, held_groups[:cut_at]), (3, held_groups[cut_at:])]
    layout += [(r, tuple(i | halves for i in some)) for r, some in layout]
    out_w = pl.pallas_call(
        functools.partial(strips_kernel, tuple(layout), strip),
        out_shape=shape((d, d)),
        in_specs=[SM] + [ANY] * len(layout),
        out_specs=ANY,
        scratch_shapes=[pltpu.SemaphoreType.DMA((groups * TP,))],
        compiler_params=params(8),
        cost_estimate=cost(0, 16 * MIB),
        name="strips",
    )(me_ref, *out_blocks)

    second_aug, residual, out_inner = pl.pallas_call(
        out_kernel,
        grid_spec=pltpu.PrefetchScalarGridSpec(
            num_scalar_prefetch=1,
            grid=(TP,),
            in_specs=[
                pl.BlockSpec((1, rows, qw), lambda r, m: (r, 0, 0)),
                pl.BlockSpec((qw, d), lambda r, m: (m[0] ^ r, 0)),
                pl.BlockSpec((RANK, qw), lambda r, m: (0, m[0] ^ r)),
                pl.BlockSpec((RANK, d), lambda r, m: (0, 0)),
                pl.BlockSpec((rows, d), lambda r, m: (0, 0)),
                pl.BlockSpec((1, d), lambda r, m: (0, 0)),
                pl.BlockSpec((PAD, d), lambda r, m: (0, 0)),
            ],
            out_specs=[
                pl.BlockSpec((rows, wide), lambda r, m: (0, 0)),
                pl.BlockSpec((rows, d), lambda r, m: (0, 0)),
                pl.BlockSpec((rows, RANK), lambda r, m: (0, 0)),
            ],
            scratch_shapes=[pltpu.VMEM((rows, d), F32), pltpu.VMEM((rows, RANK), F32)],
        ),
        out_shape=(shape((rows, wide)), shape((rows, d), F32), shape((rows, RANK))),
        compiler_params=params(48, 1),
        cost_estimate=cost(2 * rows * d * d, 12 * MIB),
        name="out",
    )(me_ref, mine, out_w, olt, orr, x_own, norm_second[None], lgu)

    second_got = together(*near_far(second_aug))
    second_ends = corners(*second_got)
    dy_aug = after(dy_aug, second_got)
    dys = sent([dy_aug] * TP)
    seconds = [second_aug, *second_got, *second_ends]

    block = max(256, own_ff)
    steps = slice_ff // block
    fixed = lambda j: (0, 0)
    column = lambda j: (0, j)
    term_spec = pl.BlockSpec((RANK, block), column)
    low_spec = pl.BlockSpec((PAD, block), column)
    wide_spec = pl.BlockSpec((tokens, block), column)
    down_spec = pl.BlockSpec((block, d), lambda j: (j, 0))
    once = dict(pipeline_mode=pl.Buffered(1))
    kept = pl.BlockSpec((PAD, d), fixed, **once)
    weight_specs = [
        pl.BlockSpec((groups, 1, TP * strip, block), lambda j: (0, 0, 0, j)),
        pl.BlockSpec((groups, 1, TP * strip, block), lambda j: (0, 1, 0, j)),
    ]
    act, silu, slope = pl.pallas_call(
        gate_kernel,
        grid=(steps,),
        in_specs=[ANY] * 5 + weight_specs + [low_spec] * 2,
        out_specs=[wide_spec] * 3,
        scratch_shapes=[pltpu.VMEM((tokens, wide), BF), pltpu.SemaphoreType.DMA((5,))],
        out_shape=[shape((tokens, slice_ff))] * 3,
        compiler_params=params(56, 1),
        cost_estimate=cost(2 * tokens * d * slice_ff * 2, 32 * MIB),
        name="gate",
    )(*seconds, feed_w, feed_w, rg, ru)

    tall = rows + RANK
    back = pl.pallas_call(
        feed_back_kernel,
        grid=(steps,),
        in_specs=[SM]
        + [ANY] * 9
        + weight_specs
        + [down_spec]
        + [wide_spec] * 2
        + [low_spec] * 3
        + [kept],
        out_specs=[pl.BlockSpec((tall, d), fixed, **once)] * 4 + [term_spec] * 2,
        scratch_shapes=[
            pltpu.VMEM((tokens, wide), BF),
            pltpu.VMEM((tokens, wide), BF),
            pltpu.VMEM((tokens, d), F32),
            pltpu.VMEM((tokens, PAD), F32),
            pltpu.SemaphoreType.DMA((10,)),
        ],
        out_shape=[shape((tall, d))] * 4 + [shape((RANK, slice_ff), F32)] * 2,
        compiler_params=params(60, 1),
        cost_estimate=cost(2 * tokens * d * slice_ff * 3, 50 * MIB),
        name="feed_back",
    )(me_ref, *seconds, *dys, feed_w, feed_w, down_w, silu, slope, dlt, rg, ru, lgu)
    second_parts, (term_gr, term_ur) = (back[:4], back[4:])

    down = pl.pallas_call(
        down_kernel,
        grid=(steps,),
        in_specs=[ANY] * 4 + [down_spec, wide_spec, low_spec, kept],
        out_specs=[pl.BlockSpec((rows, d), fixed, **once)] * 4
        + [term_spec, pl.BlockSpec((RANK, d), fixed)],
        scratch_shapes=[
            pltpu.VMEM((tokens, wide), BF),
            pltpu.VMEM((tokens, d), F32),
            pltpu.VMEM((tokens, PAD), F32),
            pltpu.SemaphoreType.DMA((5,)),
        ],
        out_shape=[shape((rows, d))] * 4 + [shape((RANK, slice_ff), F32), shape((RANK, d), F32)],
        compiler_params=params(56, 1),
        cost_estimate=cost(2 * tokens * d * slice_ff, 24 * MIB),
        name="down",
    )(*dys, down_w, after(act, second_parts), dlt, dr_pad)
    out_parts, (term_dl, term_dr) = (down[:4], down[4:])

    adapters = joint_left.shape[0]
    bits = halves.bit_length() - 1
    turned = [sum(((i >> b) & 1) << (bits - 1 - b) for b in range(bits)) for i in range(halves)]
    share = slice_ff // halves

    def by_slice(at):
        parts = []
        for source in range(halves):
            first_column = turned[source] * share
            for t in range(TP):
                for g in range(share // own_ff):
                    group = first_column // own_ff + g
                    to = (group * TP + t) * own_ff
                    parts.append((to, own_ff, ((source, t, at + g * own_ff),)))
        return tuple(parts)

    def by_t(at, size, base=0, count=halves):
        return tuple(
            (base + t * size, size, tuple((i, t, at) for i in range(count))) for t in range(TP)
        )

    def slotted(got, plan, widths, name):
        return pl.pallas_call(
            functools.partial(slot_kernel, plan, adapters),
            out_shape=[shape((adapters, RANK, size), F32) for size in widths],
            in_specs=[VM],
            out_specs=[VM] * len(widths),
            compiler_params=params(48),
            cost_estimate=cost(adapters * seqs * RANK * sum(widths), 64 * adapters * sum(widths)),
            name=name,
        )(got)

    def over_h(value):
        at = 1
        while at < halves:
            count = value.shape[1] // 2
            upper = (h // at) % 2
            keep = lax.dynamic_slice_in_dim(value, upper * count, count, 1)
            give = lax.dynamic_slice_in_dim(value, (1 - upper) * count, count, 1)
            value = keep + flip(give.astype(BF), "h", at).astype(F32)
            at *= 2
        return value

    id_columns = jnp.full((RANK, PAD), adapter_ids[0], F32)
    width = d // TP

    second_got, out_parts = together(sent(second_parts), out_parts)
    second_terms = sum(part[rows:, : 2 * width].astype(F32) for part in second_got)

    dmix, delta_residual = pl.pallas_call(
        out_back_kernel,
        grid_spec=pltpu.PrefetchScalarGridSpec(
            num_scalar_prefetch=1,
            grid=(TP,),
            in_specs=[pl.BlockSpec((tall, d), lambda r, m: (0, 0))] * 4
            + [pl.BlockSpec((rows, d), lambda r, m: (0, 0))] * 2
            + [
                pl.BlockSpec((1, d), lambda r, m: (0, 0)),
                pl.BlockSpec((RANK, d), lambda r, m: (0, 0)),
                pl.BlockSpec((RANK, qw), lambda r, m: (0, m[0] ^ r)),
                pl.BlockSpec((rows, RANK), lambda r, m: (0, 0)),
                pl.BlockSpec((qw, d), lambda r, m: (m[0] ^ r, 0)),
                pl.BlockSpec((1, rows, qw), lambda r, m: (r, 0, 0)),
                pl.BlockSpec((RANK, d), lambda r, m: (0, 0)),
            ],
            out_specs=[
                pl.BlockSpec((1, rows + 3 * RANK, qw), lambda r, m: (r, 0, 0)),
                pl.BlockSpec((rows, d), lambda r, m: (0, 0)),
            ],
            scratch_shapes=[
                pltpu.VMEM((rows, d), BF),
                pltpu.VMEM((rows, RANK), BF),
                pltpu.VMEM((2 * RANK, d), F32),
            ],
        ),
        out_shape=(shape((TP, rows + 3 * RANK, qw)), shape((rows, d), F32)),
        compiler_params=params(48, 1),
        cost_estimate=cost(2 * rows * d * d, 16 * MIB),
        name="out_back",
    )(me_ref, *second_got, dy, residual, norm_second[None], orr, olt, out_inner, out_w, mine, term_dr)

    slice_terms = after(jnp.concatenate([term_gr, term_ur, term_dl], axis=0), dmix)
    deltas, slice_terms = together(sent(dmix), over_h(slice_terms))
    mixed_terms = sum(part[rows:].astype(F32) for part in deltas)
    early_in = jnp.concatenate(
        [slice_terms[i * RANK : (i + 1) * RANK] for i in range(3)]
        + [second_terms]
        + [mixed_terms[i * RANK : (i + 1) * RANK] for i in range(3)]
        + [id_columns],
        axis=1,
    ).astype(BF)
    deltas, early_in = together(deltas, early_in)
    early = lax.all_gather(early_in, ("s", "h", "t")).reshape(seqs, halves, TP, RANK, -1)

    dq, dkv, dslot = pl.pallas_call(
        functools.partial(attend_back_kernel, tile, ranges),
        out_shape=(
            shape((tokens, qw)),
            shape((tokens, 2 * kw), F32),
            shape((key_rows - tokens, 2 * kw)),
        ),
        in_specs=[SM] + [VM] * 12,
        out_specs=(VM, VM, VM),
        scratch_shapes=[
            pltpu.VMEM((tokens, qw), BF),
            pltpu.VMEM((tokens, qw), BF),
            pltpu.VMEM((key_rows, 2 * kw), F32),
        ],
        compiler_params=params(56),
        cost_estimate=cost(10 * pairs_done * HEAD_DIM, 12 * MIB, pairs_done),
        name="attend_back",
    )(me_ref, q, kv_all, query_marks, key_marks, lse, mixed, *deltas, cosine, sine)

    out_got = sent(after(out_parts, deltas))
    dslot = after(dslot, out_got[1:3])
    returned = [
        lax.ppermute(dslot[i * span : (i + 1) * span], "h", [(b, a) for a, b in pairs])
        for i, (shift, side, pairs) in enumerate(slots)
    ]
    layer_output = (
        residual
        + (out_got[0].astype(F32) + out_got[1].astype(F32))
        + (out_got[2].astype(F32) + out_got[3].astype(F32))
    ).astype(BF)[None]
    sides = tuple(side for _, side, _ in slots)
    dj, joint_deltas, term_jr, term_jl = pl.pallas_call(
        functools.partial(joint_terms_kernel, sides),
        out_shape=[
            shape((tokens, cols)),
            shape((tokens, PAD)),
            shape((RANK, cols), F32),
            shape((RANK, d), F32),
        ],
        in_specs=[SM] + [VM] * (2 + len(sides) + 8),
        out_specs=[VM] * 4,
        scratch_shapes=[pltpu.VMEM((tokens, 2 * kw), BF)],
        compiler_params=params(56),
        cost_estimate=cost(tokens * d * cols // 4, 12 * MIB),
        name="joint_terms",
    )(me_ref, dq, dkv, *returned, cosine, sine, jr_pad, *firsts)
    left_parts = [
        lax.dynamic_slice_in_dim(term_jl, (me ^ r) * width, width, 1).astype(BF) for r in range(TP)
    ]
    left_sent = sent(left_parts)
    first_parts = pl.pallas_call(
        joint_back_kernel,
        out_shape=[shape((rows, d))] * 4,
        in_specs=[SM] + [ANY] + [VM] * 3,
        out_specs=[VM] * 4,
        scratch_shapes=[pltpu.VMEM((d, cols), BF), pltpu.SemaphoreType.DMA((1,))],
        compiler_params=params(56),
        cost_estimate=cost(2 * tokens * d * cols, 16 * MIB),
        name="joint_back",
    )(me_ref, joint_w, dj, after(joint_deltas, out_got), jlt_pad)

    got = sent(first_parts)
    early = after(early, got[1:3])
    d_gr, d_ur, d_dl, d_gl, d_ul, d_dr, d_or, d_ol = slotted(
        early,
        tuple(by_slice(i * share) for i in range(3))
        + tuple(by_t(3 * share + i * width, width) for i in range(5)),
        (ff, ff, ff, d, d, d, d, d),
        "slots_early",
    )
    late = jnp.concatenate([sum(part.astype(F32) for part in left_sent), term_jr], axis=1)
    late = after(late, (got[1:3], d_gr))
    at = 1
    while at < halves:
        late = late + flip(late.astype(BF), "h", at).astype(F32)
        at *= 2
    late = jnp.concatenate([late, id_columns], axis=1).astype(BF)[None]
    at = 1
    while at < seqs:
        other = flip(late, "s", at)
        upper = (s_at // at) % 2 == 1
        late = jnp.concatenate(
            [jnp.where(upper, other, late), jnp.where(upper, late, other)], axis=0
        )
        at *= 2
    late_got = [late, swap(late, 1), swap(late, 2), swap(late, 3)]
    low = [jnp.where(me % 2 == 1, late_got[i ^ 1], late_got[i]) for i in range(TP)]
    late = jnp.stack([jnp.where(me >= 2, low[i ^ 2], low[i]) for i in range(TP)], axis=1)[:, None]
    delta_first = (got[0].astype(F32) + got[1].astype(F32)) + (
        got[2].astype(F32) + got[3].astype(F32)
    )
    input_delta = (delta_residual + norm_back(x32, norm_first, delta_first)).astype(BF)[None]
    d_jl, d_jr = slotted(
        late,
        (
            by_t(0, width, 0, 1),
            by_t(width, qw, 0, 1)
            + by_t(width + qw, kw, q_end, 1)
            + by_t(width + qw + kw, kw, k_end, 1),
        ),
        (d, HEADS * HEAD_DIM + 2 * KV_HEADS * HEAD_DIM),
        "slots_late",
    )

    def left(value):
        return jnp.swapaxes(value, 1, 2)

    return (
        layer_output,
        input_delta,
        left(d_jl),
        d_jr,
        left(d_ol),
        d_or,
        left(d_gl),
        d_gr,
        left(d_ul),
        d_ur,
        left(d_dl),
        d_dr,
    )


def solution(mesh):
    seqs, ctx = (mesh.shape["seq"], mesh.shape["ctx"])
    inner = Mesh(mesh.devices.reshape(seqs, ctx // TP, TP), ("s", "h", "t"))
    acts = P("s", ("h", "t"), None)
    weight = P(("s", "h", "t"), None)
    placed = (
        (acts, acts, P(), P())
        + (weight,) * 5
        + (P(),) * 10
        + (P("s", None), P("s"))
    )
    return jax.shard_map(
        per_device,
        mesh=inner,
        in_specs=placed,
        out_specs=(acts, acts) + (P(),) * 10,
        check_vma=False,
    )
```

```python
import functools

import jax
import jax.numpy as jnp
from jax import lax
from jax.experimental import pallas as pl
from jax.experimental.pallas import tpu as pltpu
from jax.sharding import Mesh, PartitionSpec as P

HEADS = 16
KV_HEADS = 8
HEAD_DIM = 128
WINDOW = 1024
FIRST_DOC = 1536
RANK = 16
PAD = 128
TP = 4

epsilon = 1e-06
rotary_base = 1000000.0
masked_score = -1e30

BF = jnp.bfloat16
F32 = jnp.float32
MIB = 1024 * 1024


def dot(left, right):
    return jnp.dot(left, right, preferred_element_type=F32)


def dot_t(left, right):
    return lax.dot_general(left, right, (((1,), (1,)), ((), ())), preferred_element_type=F32)


def t_dot(left, right):
    return lax.dot_general(left, right, (((0,), (0,)), ((), ())), preferred_element_type=F32)


def params(mib, grid=0):
    extra = {"dimension_semantics": ("arbitrary",) * grid} if grid else {}
    return pltpu.CompilerParams(vmem_limit_bytes=mib * MIB, **extra)


def cost(flops, nbytes, trans=0):
    return pl.CostEstimate(flops=int(flops), bytes_accessed=int(nbytes), transcendentals=int(trans))


VM = pl.BlockSpec(memory_space=pltpu.VMEM)
SM = pl.BlockSpec(memory_space=pltpu.SMEM)
ANY = pl.BlockSpec(memory_space=pl.ANY)


def half_range(side, h, span, length):
    start = span * h if side == 0 else length - span * (h + 1)
    return (start, start + span)


def may_see(q, k):
    grain = 64
    for q0 in range(q[0], q[1], grain):
        for k0 in range(k[0], k[1], grain):
            same = (q0 >= FIRST_DOC) == (k0 >= FIRST_DOC)
            if same and k0 < q0 + grain and q0 - (k0 + grain - 1) < WINDOW:
                return True
    return False


def key_plan(halves, span, length):
    slots = []
    for shift in list(range(halves - 1, 0, -1)) + list(range(-1, -halves, -1)):
        for side in (0, 1):
            pairs = []
            for h in range(halves):
                source = h - shift
                if not 0 <= source < halves:
                    continue
                wanted = half_range(side, source, span, length)
                if any(may_see(half_range(s, h, span, length), wanted) for s in (0, 1)):
                    pairs.append((source, h))
            if pairs:
                slots.append((shift, side, tuple(pairs)))
    tile = min(256, span)
    step = 128
    ranges = []
    for i in range(2 * span // tile):
        low, high = (1 << 30, 0)
        for h in range(halves):
            side, inside = divmod(i * tile, span)
            base = half_range(side, h, span, length)[0] + inside
            held = []
            for shift, key_side, pairs in slots:
                held.append(
                    half_range(key_side, h - shift, span, length) if (h - shift, h) in pairs else None
                )
            held += [half_range(s, h, span, length) for s in (0, 1)]
            for index, region in enumerate(held):
                if region is None:
                    continue
                for offset in range(0, span, step):
                    block = (region[0] + offset, region[0] + min(offset + step, span))
                    if may_see((base, base + tile), block):
                        low = min(low, index * span + offset)
                        high = max(high, index * span + offset + step)
        ranges.append((low, min(high, (len(slots) + 2) * span)))
    return (slots, tile, ranges)


def place_rows(me, r, rows):
    half = rows // 2
    other = me ^ r
    first = pl.multiple_of(other * half, half)
    second = pl.multiple_of(TP * half + (TP - 1 - other) * half, half)
    return ((0, first), (half, second))


def cut_kernel(wide, me_ref, joint_ref, gate_ref, up_ref, *outs):
    me = me_ref[0]
    joints, feeds = (outs[:TP], outs[TP:])
    cols = joints[0].shape[1]
    kw = KV_HEADS // TP * HEAD_DIM
    qw = cols - 2 * kw
    for r in range(TP):
        other = me ^ r
        start = 0
        base = 0
        for width, count in ((qw, TP), (kw, TP), (kw, TP)):
            joints[r][:, start : start + width] = joint_ref[
                :, pl.ds(pl.multiple_of(base + other * width, HEAD_DIM), width)
            ]
            start += width
            base += width * count
        for g in range(feeds[r].shape[2] // wide if feeds else 0):
            at = pl.ds(pl.multiple_of((g * TP + other) * wide, wide), wide)
            feeds[r][0, :, g * wide : (g + 1) * wide] = gate_ref[:, at]
            feeds[r][1, :, g * wide : (g + 1) * wide] = up_ref[:, at]


def natural_kernel(me_ref, r0, r1, r2, r3, out_ref):
    strip = r0.shape[-2]
    for r, ref in enumerate((r0, r1, r2, r3)):
        rows = pl.ds(pl.multiple_of((me_ref[0] ^ r) * strip, strip), strip)
        if len(ref.shape) == 2:
            out_ref[rows, :] = ref[...]
        else:
            out_ref[:, rows, :] = ref[...]


def strips_kernel(layout, strip, me_ref, *refs):
    out_ref, sem = refs[-2:]
    me, place = (me_ref[0], me_ref[1])
    copies = []
    for ref, (r, groups) in zip(refs, layout):
        for i, group in enumerate(groups):
            row = pl.multiple_of(((place ^ group) * TP + (me ^ r)) * strip, strip)
            copies.append(
                pltpu.make_async_copy(
                    ref.at[pl.ds(i * strip, strip), :],
                    out_ref.at[pl.ds(row, strip), :],
                    sem.at[len(copies)],
                )
            )
    for copy in copies:
        copy.start()
    for copy in copies:
        copy.wait()


def load_pieces(place, pieces, target, sem):
    strip = pieces[0].shape[0]
    if len(pieces) == 1:
        copies = [pltpu.make_async_copy(pieces[0], target, sem.at[0])]
        copies[0].start()
        return copies
    copies = []
    for r, ref in enumerate(pieces):
        rows = pl.ds(pl.multiple_of((place ^ r) * strip, strip), strip)
        copies.append(pltpu.make_async_copy(ref, target.at[rows, :], sem.at[r]))
    for copy in copies:
        copy.start()
    return copies


def qkv_kernel(count, me_ref, *refs):
    pieces = refs[:count]
    (x0, x1, x2, x3a, x3b, jr_ref, cos_ref, sin_ref) = refs[count : count + 8]
    (q_ref, kv_ref, w_ref, sem) = refs[-4:]
    me = me_ref[0]
    copies = load_pieces(me_ref[1], pieces, w_ref, sem)
    rows, wide = x0.shape
    d = wide - PAD
    half = rows // 2
    nq = q_ref.shape[1] // HEAD_DIM
    nk = kv_ref.shape[1] // HEAD_DIM // 2
    for copy in copies:
        copy.wait()
    for r, x_refs in enumerate(((x0,), (x1,), (x2,), (x3a, x3b))):
        x = jnp.concatenate([ref[...] for ref in x_refs], axis=0)
        joined = dot(x[:, :d], w_ref[...]) + dot(x[:, d:], jr_ref[...])
        for source, target in place_rows(me, r, rows):
            part = joined[source : source + half]
            cosine = cos_ref[pl.ds(target, half), :]
            sine = sin_ref[pl.ds(target, half), :]
            for head in range(nq + nk):
                u = part[:, head * HEAD_DIM : (head + 1) * HEAD_DIM]
                turned = (u * cosine + pltpu.roll(u, HEAD_DIM // 2, 1) * sine).astype(BF)
                if head < nq:
                    q_ref[pl.ds(target, half), head * HEAD_DIM : (head + 1) * HEAD_DIM] = turned
                else:
                    at = head - nq
                    kv_ref[pl.ds(target, half), at * HEAD_DIM : (at + 1) * HEAD_DIM] = turned
            kv_ref[pl.ds(target, half), nk * HEAD_DIM :] = part[:, (nq + nk) * HEAD_DIM :].astype(BF)


def head_columns(ref, rows, first, count):
    return jnp.concatenate(
        [ref[rows, (first + i) * HEAD_DIM : (first + i + 1) * HEAD_DIM] for i in range(count)], axis=0
    )


def bias_of(qpos_ref, kpos_ref, rows, low, high, group):
    distance = qpos_ref[rows, :] - kpos_ref[:, low:high]
    bias = jnp.where((distance >= 0) & (distance < WINDOW), 0.0, masked_score).astype(F32)
    return jnp.concatenate([bias] * group, axis=0)


def attend_kernel(tile, ranges, me_ref, q_ref, kv_ref, qpos_ref, kpos_ref, mixed_ref, lse_ref, held):
    me = me_ref[0]
    rows = mixed_ref.shape[1]
    half = rows // 2
    nk = kv_ref.shape[1] // HEAD_DIM // 2
    group = q_ref.shape[1] // HEAD_DIM // nk
    scale = HEAD_DIM ** (-0.5)
    for i, (low, high) in enumerate(ranges):
        here = slice(i * tile, (i + 1) * tile)
        bias = bias_of(qpos_ref, kpos_ref, here, low, high, group)
        for head in range(nk):
            q = head_columns(q_ref, here, head * group, group)
            k = kv_ref[low:high, head * HEAD_DIM : (head + 1) * HEAD_DIM]
            v = kv_ref[low:high, (nk + head) * HEAD_DIM : (nk + head + 1) * HEAD_DIM]
            scores = dot_t(q, k) * scale + bias
            largest = jnp.max(scores, axis=-1, keepdims=True)
            raised = jnp.exp(scores - largest)
            total = jnp.sum(raised, axis=-1, keepdims=True)
            out = dot((raised * (1.0 / total)).astype(BF), v).astype(BF)
            lse = largest + jnp.log(total)
            for g in range(group):
                at = head * group + g
                held[here, at * HEAD_DIM : (at + 1) * HEAD_DIM] = out[g * tile : (g + 1) * tile]
                lse_ref[here, at : at + 1] = lse[g * tile : (g + 1) * tile]
    for r in range(TP):
        for source, target in place_rows(me, r, rows):
            mixed_ref[r, source : source + half, :] = held[pl.ds(target, half), :]


def attend_back_kernel(
    tile,
    ranges,
    me_ref,
    q_ref,
    kv_ref,
    qpos_ref,
    kpos_ref,
    lse_ref,
    mixed_ref,
    d0,
    d1,
    d2,
    d3,
    cos_ref,
    sin_ref,
    dq_ref,
    dkv_ref,
    dslot_ref,
    held,
    given,
    total_ref,
):
    me = me_ref[0]
    rows = mixed_ref.shape[1]
    half = rows // 2
    nk = kv_ref.shape[1] // HEAD_DIM // 2
    group = q_ref.shape[1] // HEAD_DIM // nk
    scale = HEAD_DIM ** (-0.5)
    for r, d_ref in enumerate((d0, d1, d2, d3)):
        for source, target in place_rows(me, r, rows):
            held[pl.ds(target, half), :] = mixed_ref[r, source : source + half, :]
            given[pl.ds(target, half), :] = d_ref[source : source + half, :]
    total_ref[...] = jnp.zeros_like(total_ref)
    for i, (low, high) in enumerate(ranges):
        here = slice(i * tile, (i + 1) * tile)
        bias = bias_of(qpos_ref, kpos_ref, here, low, high, group)
        cosine = cos_ref[here, :]
        sine = sin_ref[here, :]
        for head in range(nk):
            key_columns = slice(head * HEAD_DIM, (head + 1) * HEAD_DIM)
            value_columns = slice((nk + head) * HEAD_DIM, (nk + head + 1) * HEAD_DIM)
            q = head_columns(q_ref, here, head * group, group)
            out = head_columns(held, here, head * group, group)
            delta = head_columns(given, here, head * group, group)
            lse = jnp.concatenate(
                [lse_ref[here, head * group + g : head * group + g + 1] for g in range(group)], axis=0
            )
            k = kv_ref[low:high, key_columns]
            v = kv_ref[low:high, value_columns]
            chances = jnp.exp(dot_t(q, k) * scale + bias - lse)
            inner = jnp.sum(out.astype(F32) * delta.astype(F32), axis=-1, keepdims=True)
            raw = (chances * (dot_t(delta, v) - inner) * scale).astype(BF)
            dq = dot(raw, k)
            for g in range(group):
                at = head * group + g
                e = dq[g * tile : (g + 1) * tile]
                back = e * cosine - pltpu.roll(e, HEAD_DIM // 2, 1) * sine
                dq_ref[here, at * HEAD_DIM : (at + 1) * HEAD_DIM] = back.astype(BF)
            total_ref[low:high, key_columns] += t_dot(raw, q)
            total_ref[low:high, value_columns] += t_dot(chances.astype(BF), delta)
    extra = dslot_ref.shape[0]
    dslot_ref[...] = total_ref[:extra, :].astype(BF)
    dkv_ref[...] = total_ref[extra:, :]


def out_kernel(
    me_ref, m_ref, w_ref, olt_ref, or_ref, x_ref, gain_ref, lgu_ref, aug_ref, res_ref, oi_ref, acc, inner
):
    r = pl.program_id(0)
    d = x_ref.shape[1]

    @pl.when(r == 0)
    def _():
        acc[...] = x_ref[...].astype(F32)
        inner[...] = jnp.zeros_like(inner)

    m = m_ref[0]
    acc[...] += dot(m, w_ref[...])
    inner[...] += dot_t(m, olt_ref[...])

    @pl.when(r == TP - 1)
    def _():
        low = inner[...].astype(BF)
        oi_ref[...] = low
        residual = acc[...] + dot(low, or_ref[...])
        res_ref[...] = residual
        factor = lax.rsqrt(jnp.mean(residual * residual, axis=-1, keepdims=True) + epsilon)
        second = (residual * factor * gain_ref[...]).astype(BF)
        aug_ref[:, :d] = second
        aug_ref[:, d:] = dot_t(second, lgu_ref[...]).astype(BF)


def out_back_kernel(
    me_ref,
    p0,
    p1,
    p2,
    p3,
    dy_ref,
    res_ref,
    gain_ref,
    or_ref,
    olt_ref,
    oi_ref,
    w_ref,
    m_ref,
    tdr_ref,
    dmix_ref,
    dres_ref,
    branch,
    inner,
    terms,
):
    r = pl.program_id(0)
    rows, d = dy_ref.shape
    width = d // TP

    @pl.when(r == 0)
    def _():
        gain = gain_ref[...]
        incoming = (p0[:rows].astype(F32) + p1[:rows].astype(F32)) + (
            p2[:rows].astype(F32) + p3[:rows].astype(F32)
        )
        v = res_ref[...]
        factor = lax.rsqrt(jnp.mean(v * v, axis=-1, keepdims=True) + epsilon)
        scaled = incoming * gain
        back = factor * scaled - v * (factor * factor * factor) * jnp.mean(
            scaled * v, axis=-1, keepdims=True
        )
        delta = dy_ref[...].astype(F32) + back
        dres_ref[...] = delta
        low = delta.astype(BF)
        branch[...] = low
        inner[...] = dot_t(low, or_ref[...]).astype(BF)
        terms[:RANK] = tdr_ref[...]
        terms[RANK:] = t_dot(oi_ref[...], low)

    dmix_ref[0, :rows] = (dot_t(branch[...], w_ref[...]) + dot(inner[...], olt_ref[...])).astype(BF)
    at = pl.ds(pl.multiple_of((me_ref[0] ^ r) * width, width), width)
    dmix_ref[0, rows : rows + 2 * RANK] = terms[:, at].astype(BF)
    dmix_ref[0, rows + 2 * RANK :] = t_dot(inner[...], m_ref[0]).astype(BF)


def load_rows(refs, stores, sem):
    copies = []
    for some, store in zip(refs, stores):
        at = 0
        for ref in some:
            copies.append(
                pltpu.make_async_copy(
                    ref, store.at[pl.ds(at, ref.shape[0]), :], sem.at[len(copies)]
                )
            )
            at += ref.shape[0]
    for copy in copies:
        copy.start()
    for copy in copies:
        copy.wait()


def gate_kernel(*refs):
    xs, refs = (refs[:5], refs[5:])
    (gate_ref, up_ref, rg_ref, ru_ref, act_ref, silu_ref, slope_ref, x_all, sem) = refs
    d = x_all.shape[1] - PAD

    @pl.when(pl.program_id(0) == 0)
    def _():
        load_rows((xs,), (x_all,), sem)

    block = gate_ref.shape[-1]
    gate_w = gate_ref[...].reshape(d, block)
    up_w = up_ref[...].reshape(d, block)
    count = x_all.shape[0]
    take = min(512, count)
    for start in range(0, count, take):
        here = slice(start, start + take)
        x = x_all[here, :d]
        xi = x_all[here, d:]
        gate = dot(x, gate_w) + dot(xi, rg_ref[...])
        up = dot(x, up_w) + dot(xi, ru_ref[...])
        sigmoid = jax.nn.sigmoid(gate)
        silu = gate * sigmoid
        act_ref[here, :] = (silu * up).astype(BF)
        silu_ref[here, :] = silu.astype(BF)
        slope_ref[here, :] = (up * sigmoid * (1.0 + gate * (1.0 - sigmoid))).astype(BF)


def feed_back_kernel(me_ref, *refs):
    xs, ys, refs = (refs[:5], refs[5:9], refs[9:])
    (gate_ref, up_ref, down_ref, silu_ref, slope_ref, dlt_ref, rg_ref, ru_ref, lgu_ref, *refs) = refs
    (s0, s1, s2, s3, tgr_ref, tur_ref, x_all, y_all, acc_second, acc_inner, sem) = refs
    me = me_ref[0]
    j = pl.program_id(0)
    d = acc_second.shape[1]
    rows = x_all.shape[0] // TP

    @pl.when(j == 0)
    def _():
        load_rows((xs, ys), (x_all, y_all), sem)
        acc_second[...] = jnp.zeros_like(acc_second)
        acc_inner[...] = jnp.zeros_like(acc_inner)

    block = gate_ref.shape[-1]
    gate_w = gate_ref[...].reshape(d, block)
    up_w = up_ref[...].reshape(d, block)
    down_w = down_ref[...]
    dlt, rg, ru = (dlt_ref[...], rg_ref[...], ru_ref[...])
    term_g = jnp.zeros((PAD, block), F32)
    term_u = jnp.zeros((PAD, block), F32)
    take = min(512, TP * rows)
    for start in range(0, TP * rows, take):
        here = slice(start, start + take)
        delta = dot_t(y_all[here, :d], down_w) + dot(y_all[here, d:], dlt)
        delta_gate = (delta * slope_ref[here, :].astype(F32)).astype(BF)
        delta_up = (delta * silu_ref[here, :].astype(F32)).astype(BF)
        acc_second[here, :] += dot_t(delta_gate, gate_w) + dot_t(delta_up, up_w)
        acc_inner[here, :] += dot_t(delta_gate, rg) + dot_t(delta_up, ru)
        tail = x_all[here, d:]
        term_g += t_dot(tail, delta_gate)
        term_u += t_dot(tail, delta_up)
    tgr_ref[...] = term_g[RANK : 2 * RANK]
    tur_ref[...] = term_u[2 * RANK : 3 * RANK]

    @pl.when(j == pl.num_programs(0) - 1)
    def _():
        inner = acc_inner[...].astype(BF)
        width = d // TP
        for r, s_ref in enumerate((s0, s1, s2, s3)):
            here = slice(r * rows, (r + 1) * rows)
            s_ref[:rows, :] = (acc_second[here, :] + dot(inner[here], lgu_ref[...])).astype(BF)
            at = pl.ds(pl.multiple_of((me ^ r) * width, width), width)
            term = t_dot(inner, x_all[:, at]).astype(BF)
            s_ref[rows:, :width] = term[RANK : 2 * RANK]
            s_ref[rows:, width : 2 * width] = term[2 * RANK : 3 * RANK]
            s_ref[rows:, 2 * width :] = jnp.zeros((RANK, d - 2 * width), BF)


def down_kernel(*refs):
    ys, refs = (refs[:4], refs[4:])
    (down_ref, act_ref, dlt_ref, dr_ref, o0, o1, o2, o3, tdl_ref, tdr_ref, *refs) = refs
    (y_all, acc, acc_inner, sem) = refs
    j = pl.program_id(0)
    rows = o0.shape[0]
    d = acc.shape[1]

    @pl.when(j == 0)
    def _():
        load_rows((ys,), (y_all,), sem)
        acc[...] = jnp.zeros_like(acc)
        acc_inner[...] = jnp.zeros_like(acc_inner)

    acc[...] += dot(act_ref[...], down_ref[...])
    acc_inner[...] += dot_t(act_ref[...], dlt_ref[...])
    tdl_ref[...] = t_dot(y_all[:, d:], act_ref[...])[:RANK]

    @pl.when(j == pl.num_programs(0) - 1)
    def _():
        inner = acc_inner[...].astype(BF)
        tdr_ref[...] = t_dot(inner, y_all[:, :d])[:RANK]
        for r, o_ref in enumerate((o0, o1, o2, o3)):
            here = slice(r * rows, (r + 1) * rows)
            o_ref[...] = (acc[here, :] + dot(inner[here], dr_ref[...])).astype(BF)


def slot_kernel(plan, adapters, got_ref, *outs):
    seqs, halves = got_ref.shape[:2]
    marks = []
    for i in range(seqs):
        ids = got_ref[i, 0, 0, :, -PAD:].astype(F32)
        marks.append(
            [
                jnp.max(jnp.where(ids == float(e), 1.0, 0.0), axis=1, keepdims=True)
                for e in range(adapters)
            ]
        )
    for out_ref, parts in zip(outs, plan):
        for to, width, sources in parts:
            values = []
            for i in range(seqs):
                total = None
                for h, t, at in sources:
                    part = got_ref[i, h, t, :, at : at + width].astype(F32)
                    total = part if total is None else total + part
                values.append(total)
            for e in range(adapters):
                out_ref[e, :, to : to + width] = sum(
                    marks[i][e] * values[i] for i in range(seqs)
                )


def joint_terms_kernel(sides, me_ref, dq_ref, dkv_ref, *refs):
    extra, refs = (refs[: len(sides)], refs[len(sides) :])
    (cos_ref, sin_ref, jr_ref, x0, x1, x2, x3a, x3b, dj, inner_ref, tjr_ref, tjl_ref, keys) = refs
    me = me_ref[0]
    rows, wide = x0.shape
    d = wide - PAD
    half = rows // 2
    span = TP * half
    nk = dkv_ref.shape[1] // HEAD_DIM // 2
    query_width = dq_ref.shape[1]
    for side in (0, 1):
        here = slice(side * span, (side + 1) * span)
        total = dkv_ref[here, :]
        for ref, owner in zip(extra, sides):
            if owner == side:
                total = total + ref[...].astype(F32)
        for head in range(nk):
            e = total[:, head * HEAD_DIM : (head + 1) * HEAD_DIM]
            back = e * cos_ref[here, :] - pltpu.roll(e, HEAD_DIM // 2, 1) * sin_ref[here, :]
            keys[here, head * HEAD_DIM : (head + 1) * HEAD_DIM] = back.astype(BF)
        keys[here, nk * HEAD_DIM :] = total[:, nk * HEAD_DIM :].astype(BF)
    for r in range(TP):
        for source, target in place_rows(me, r, rows):
            to = slice(r * rows + source, r * rows + source + half)
            dj[to, :query_width] = dq_ref[pl.ds(target, half), :]
            dj[to, query_width:] = keys[pl.ds(target, half), :]
    term_r = jnp.zeros((PAD, dj.shape[1]), F32)
    term_l = jnp.zeros((PAD, d), F32)
    for r, x_refs in enumerate(((x0,), (x1,), (x2,), (x3a, x3b))):
        x = jnp.concatenate([ref[...] for ref in x_refs], axis=0)
        here = slice(r * rows, (r + 1) * rows)
        inner = dot_t(dj[here, :], jr_ref[...]).astype(BF)
        inner_ref[here, :] = inner
        term_r += t_dot(x[:, d:], dj[here, :])
        term_l += t_dot(inner, x[:, :d])
    tjr_ref[...] = term_r[:RANK]
    tjl_ref[...] = term_l[:RANK]


def joint_back_kernel(me_ref, *refs):
    pieces = refs[:-9]
    (dj, inner, jlt_ref, f0, f1, f2, f3, w_ref, sem) = refs[-9:]
    for copy in load_pieces(me_ref[1], pieces, w_ref, sem):
        copy.wait()
    rows = f0.shape[0]
    for r, f_ref in enumerate((f0, f1, f2, f3)):
        here = slice(r * rows, (r + 1) * rows)
        f_ref[...] = (dot_t(dj[here, :], w_ref[...]) + dot(inner[here, :], jlt_ref[...])).astype(BF)


def shape(dims, dtype=BF):
    return jax.ShapeDtypeStruct(dims, dtype)


def swap(value, r):
    return lax.ppermute(value, "t", [(i, i ^ r) for i in range(TP)])


def near_far(value):
    return (swap(value, 1), swap(value, 2))


def corners(near, far):
    half = near.shape[0] // 2
    return (swap(near[:half], 2), swap(far[half:], 1))


def sent(parts):
    return [parts[0]] + [swap(parts[r], r) for r in range(1, TP)]


def after(value, *others):
    return lax.optimization_barrier((value, others))[0]


def together(*values):
    return lax.optimization_barrier(values)


def flip(value, axis, bit):
    size = lax.axis_size(axis)
    return lax.ppermute(value, axis, [(i, i ^ bit) for i in range(size)])


def collect_first(value, seqs, halves):
    held = {0: value}
    for i in range(halves.bit_length() - 1):
        held[1 << i] = flip(value, "h", 1 << i)
    for i in range(1, seqs.bit_length() - 1):
        held[halves << i] = flip(value, "s", 1 << i)
    return held


def collect_rest(held, seqs, halves):
    held = dict(held)
    bits = [("h", 1 << i, 1 << i) for i in range(halves.bit_length() - 1)]
    bits += [("s", 1 << i, halves << i) for i in range(1, seqs.bit_length() - 1)]
    for axis, bit, offset in bits:
        for index in sorted(held):
            if index < offset and index | offset not in held:
                held[index | offset] = flip(held[index], axis, bit)
    return held


def norm_back(values, gain, incoming):
    factor = lax.rsqrt(jnp.mean(values * values, axis=-1, keepdims=True) + epsilon)
    scaled = incoming * gain
    return factor * scaled - values * (factor * factor * factor) * jnp.mean(
        scaled * values, axis=-1, keepdims=True
    )


def per_device(
    hidden,
    out_grad,
    norm_first,
    norm_second,
    joint_weight,
    out_weight,
    gate_weight,
    up_weight,
    down_weight,
    joint_left,
    joint_right,
    out_left,
    out_right,
    gate_left,
    gate_right,
    up_left,
    up_right,
    down_left,
    down_right,
    doc_lengths,
    adapter_ids,
):
    seqs = lax.axis_size("s")
    halves = lax.axis_size("h")
    groups = seqs * halves
    rows, d = hidden.shape[1:]
    half = rows // 2
    span = TP * half
    tokens = TP * rows
    length = rows * TP * halves
    strip = joint_weight.shape[0]
    ff = gate_weight.shape[1]
    own_ff = down_weight.shape[0]
    slice_ff = groups * own_ff
    wide = d + PAD
    nq = HEADS // TP
    nk = KV_HEADS // TP
    qw = nq * HEAD_DIM
    kw = nk * HEAD_DIM
    cols = qw + 2 * kw
    me = lax.axis_index("t")
    h = lax.axis_index("h")
    s_at = lax.axis_index("s")
    place = s_at * halves + h
    me_ref = jnp.stack([me, place]).astype(jnp.int32)
    slots, tile, ranges = key_plan(halves, span, length)

    adapter = adapter_ids[0]

    def pick(factor):
        return lax.dynamic_index_in_dim(factor, adapter, 0, keepdims=False)

    def pick_left(factor):
        return pick(jnp.swapaxes(factor, 1, 2))

    def padded(value, first):
        return jnp.pad(value, ((first, PAD - first - value.shape[0]), (0, 0)))

    q_end = HEADS * HEAD_DIM
    k_end = q_end + KV_HEADS * HEAD_DIM
    x_own = hidden[0]
    x32 = x_own.astype(F32)
    first = (
        x32 * lax.rsqrt(jnp.mean(x32 * x32, axis=-1, keepdims=True) + epsilon) * norm_first
    ).astype(BF)
    jlt_pad = padded(pick_left(joint_left), 0)
    first_aug = jnp.concatenate([first, dot_t(first, jlt_pad).astype(BF)], axis=1)

    whole_lanes = own_ff % HEAD_DIM == 0
    feed_shapes = [shape((2, strip, slice_ff))] * (TP if whole_lanes else 0)
    cut = pl.pallas_call(
        functools.partial(cut_kernel, own_ff),
        out_shape=[shape((strip, cols))] * TP + feed_shapes,
        in_specs=[SM] + [VM] * 3,
        out_specs=[VM] * (TP + len(feed_shapes)),
        compiler_params=params(24),
        cost_estimate=cost(0, 6 * MIB),
        name="cut",
    )(me_ref, joint_weight, gate_weight, up_weight)
    feed_parts = cut[TP:]
    if not whole_lanes:
        both = jnp.stack([gate_weight, up_weight]).reshape(2, strip, groups, TP, own_ff)
        feed_parts = [
            lax.dynamic_index_in_dim(both, me ^ r, 3, keepdims=False).reshape(2, strip, slice_ff)
            for r in range(TP)
        ]

    def natural(parts, out):
        return pl.pallas_call(
            natural_kernel,
            out_shape=out,
            in_specs=[SM] + [VM] * TP,
            out_specs=VM,
            compiler_params=params(24),
            cost_estimate=cost(0, 4 * MIB),
            name="natural",
        )(me_ref, *parts)

    def ff_slice(value):
        return lax.dynamic_index_in_dim(
            value.reshape(RANK, groups, TP, own_ff), me, 2, keepdims=False
        ).reshape(RANK, slice_ff)

    jr = pick(joint_right)
    jr_own = jnp.concatenate(
        [
            lax.dynamic_slice_in_dim(jr[:, :q_end], me * qw, qw, 1),
            lax.dynamic_slice_in_dim(jr[:, q_end:k_end], me * kw, kw, 1),
            lax.dynamic_slice_in_dim(jr[:, k_end:], me * kw, kw, 1),
        ],
        axis=1,
    )
    jr_pad = padded(jr_own, 0)
    olt = pick_left(out_left)
    orr = pick(out_right)
    lgu = jnp.pad(
        jnp.concatenate([pick_left(gate_left), pick_left(up_left)], axis=0),
        ((RANK, PAD - 3 * RANK), (0, 0)),
    )
    rg = padded(ff_slice(pick(gate_right)), RANK)
    ru = padded(ff_slice(pick(up_right)), 2 * RANK)
    dlt = padded(ff_slice(pick_left(down_left)), 0)

    index = jnp.arange(span, dtype=jnp.int32)

    def side_places(side, at):
        return (span * at if side == 0 else length - span * (at + 1)) + index

    ends = jnp.cumsum(doc_lengths[0])

    def marked(places):
        documents = jnp.sum((places[:, None] >= ends[None, :]).astype(jnp.int32), axis=1)
        return places + documents * (4 * length)

    own_places = jnp.concatenate([side_places(0, h), side_places(1, h)])
    own_marks = marked(own_places)
    slot_marks = []
    for shift, side, pairs in slots:
        valid = functools.reduce(jnp.logical_or, [h == target for _, target in pairs])
        slot_marks.append(jnp.where(valid, marked(side_places(side, h - shift)), 1 << 29))
    key_marks = jnp.concatenate(slot_marks + [own_marks])[None, :]
    query_marks = own_marks[:, None]
    inverse = rotary_base ** (-jnp.arange(HEAD_DIM // 2, dtype=F32) * 2.0 / HEAD_DIM)
    angles = own_places.astype(F32)[:, None] * inverse[None, :]
    cosine = jnp.concatenate([jnp.cos(angles)] * 2, axis=1)
    sine = jnp.sin(angles)
    sine = jnp.concatenate([-sine, sine], axis=1)

    dy = out_grad[0]
    dr_pad = padded(pick(down_right), 0)
    dy_aug = jnp.concatenate([dy, dot_t(dy, dr_pad).astype(BF)], axis=1)

    joint_sent, out_held = together(sent(cut[:TP]), collect_first(out_weight, seqs, halves))
    joint_cut = natural(joint_sent, shape((TP * strip, cols)))
    joint_w = lax.all_gather(joint_cut, ("s", "h"), axis=0, tiled=True)

    feed_parts, first_aug, out_held, _ = together(feed_parts, first_aug, out_held, joint_cut)
    first_got, (rg, ru, dlt, lgu, olt, orr, dr_pad, dy_aug) = together(
        near_far(first_aug), (rg, ru, dlt, lgu, olt, orr, dr_pad, dy_aug)
    )
    joint_w = after(joint_w, first_got)
    down_w = lax.all_gather(after(down_weight, joint_w), ("s", "h"), axis=0, tiled=True)
    feed_parts, out_held = after((feed_parts, out_held), first_got)
    first_ends, out_held, feed_sent = together(
        corners(*first_got), collect_rest(out_held, seqs, halves), sent(feed_parts)
    )
    feed_cut = natural(feed_sent, shape((2, TP * strip, slice_ff)))
    held_groups = tuple(sorted(out_held))
    out_mine = jnp.concatenate([out_held[i] for i in held_groups], axis=0)
    firsts = [first_aug, *first_got, *first_ends]

    q, kv = pl.pallas_call(
        functools.partial(qkv_kernel, 1),
        out_shape=(shape((tokens, qw)), shape((tokens, 2 * kw))),
        in_specs=[SM] + [ANY] + [VM] * 8,
        out_specs=(VM, VM),
        scratch_shapes=[pltpu.VMEM((d, cols), BF), pltpu.SemaphoreType.DMA((1,))],
        compiler_params=params(48),
        cost_estimate=cost(2 * tokens * wide * cols, 10 * MIB),
        name="qkv",
    )(me_ref, joint_w, *firsts, jr_pad, cosine, sine)

    out_mine = after(out_mine, q)
    pieces, out_got, own_core = together(
        [
            lax.ppermute(kv[side * span : (side + 1) * span], "h", pairs)
            for shift, side, pairs in slots
        ],
        near_far(out_mine),
        flip(out_mine, "s", 1),
    )
    down_w, feed_cut = after((down_w, feed_cut), pieces)
    feed_w = lax.all_gather(after(feed_cut, down_w)[None], ("s", "h"), axis=0, tiled=True)
    kv_all = jnp.concatenate(pieces + [kv], axis=0)
    key_rows = kv_all.shape[0]
    pairs_done = sum((high - low) * tile for low, high in ranges) * nq

    out_ends = corners(*after(out_got, pieces))
    mixed, lse = pl.pallas_call(
        functools.partial(attend_kernel, tile, ranges),
        out_shape=(shape((TP, rows, qw)), shape((tokens, nq), F32)),
        in_specs=[SM] + [VM] * 4,
        out_specs=(VM, VM),
        scratch_shapes=[pltpu.VMEM((tokens, qw), BF)],
        compiler_params=params(48),
        cost_estimate=cost(4 * pairs_done * HEAD_DIM, 6 * MIB, pairs_done),
        name="attend",
    )(me_ref, q, kv_all, query_marks, key_marks)

    mixed_sent = after(mixed, out_ends)
    mine, out_cores = together(
        sent(mixed_sent), [flip(block, "s", 1) for block in after(out_got, mixed)]
    )
    mine = jnp.stack(mine)
    end_cores = together(*[flip(block, "s", 1) for block in out_ends])
    out_blocks = [out_mine, *out_got, *out_ends, own_core, *out_cores, *end_cores]
    cut_at = len(held_groups) // 2
    layout = [(0, held_groups), (1, held_groups), (2, held_groups)]
    layout += [(3, held_groups[:cut_at]), (3, held_groups[cut_at:])]
    layout += [(r, tuple(i | halves for i in some)) for r, some in layout]
    out_w = pl.pallas_call(
        functools.partial(strips_kernel, tuple(layout), strip),
        out_shape=shape((d, d)),
        in_specs=[SM] + [ANY] * len(layout),
        out_specs=ANY,
        scratch_shapes=[pltpu.SemaphoreType.DMA((groups * TP,))],
        compiler_params=params(8),
        cost_estimate=cost(0, 16 * MIB),
        name="strips",
    )(me_ref, *out_blocks)

    second_aug, residual, out_inner = pl.pallas_call(
        out_kernel,
        grid_spec=pltpu.PrefetchScalarGridSpec(
            num_scalar_prefetch=1,
            grid=(TP,),
            in_specs=[
                pl.BlockSpec((1, rows, qw), lambda r, m: (r, 0, 0)),
                pl.BlockSpec((qw, d), lambda r, m: (m[0] ^ r, 0)),
                pl.BlockSpec((RANK, qw), lambda r, m: (0, m[0] ^ r)),
                pl.BlockSpec((RANK, d), lambda r, m: (0, 0)),
                pl.BlockSpec((rows, d), lambda r, m: (0, 0)),
                pl.BlockSpec((1, d), lambda r, m: (0, 0)),
                pl.BlockSpec((PAD, d), lambda r, m: (0, 0)),
            ],
            out_specs=[
                pl.BlockSpec((rows, wide), lambda r, m: (0, 0)),
                pl.BlockSpec((rows, d), lambda r, m: (0, 0)),
                pl.BlockSpec((rows, RANK), lambda r, m: (0, 0)),
            ],
            scratch_shapes=[pltpu.VMEM((rows, d), F32), pltpu.VMEM((rows, RANK), F32)],
        ),
        out_shape=(shape((rows, wide)), shape((rows, d), F32), shape((rows, RANK))),
        compiler_params=params(48, 1),
        cost_estimate=cost(2 * rows * d * d, 12 * MIB),
        name="out",
    )(me_ref, mine, out_w, olt, orr, x_own, norm_second[None], lgu)

    second_got = together(*near_far(second_aug))
    second_ends = corners(*second_got)
    dy_aug = after(dy_aug, second_got)
    dys = sent([dy_aug] * TP)
    seconds = [second_aug, *second_got, *second_ends]

    block = max(256, own_ff)
    steps = slice_ff // block
    fixed = lambda j: (0, 0)
    column = lambda j: (0, j)
    term_spec = pl.BlockSpec((RANK, block), column)
    low_spec = pl.BlockSpec((PAD, block), column)
    wide_spec = pl.BlockSpec((tokens, block), column)
    down_spec = pl.BlockSpec((block, d), lambda j: (j, 0))
    once = dict(pipeline_mode=pl.Buffered(1))
    kept = pl.BlockSpec((PAD, d), fixed, **once)
    weight_specs = [
        pl.BlockSpec((groups, 1, TP * strip, block), lambda j: (0, 0, 0, j)),
        pl.BlockSpec((groups, 1, TP * strip, block), lambda j: (0, 1, 0, j)),
    ]
    act, silu, slope = pl.pallas_call(
        gate_kernel,
        grid=(steps,),
        in_specs=[ANY] * 5 + weight_specs + [low_spec] * 2,
        out_specs=[wide_spec] * 3,
        scratch_shapes=[pltpu.VMEM((tokens, wide), BF), pltpu.SemaphoreType.DMA((5,))],
        out_shape=[shape((tokens, slice_ff))] * 3,
        compiler_params=params(56, 1),
        cost_estimate=cost(2 * tokens * d * slice_ff * 2, 32 * MIB),
        name="gate",
    )(*seconds, feed_w, feed_w, rg, ru)

    tall = rows + RANK
    back = pl.pallas_call(
        feed_back_kernel,
        grid=(steps,),
        in_specs=[SM]
        + [ANY] * 9
        + weight_specs
        + [down_spec]
        + [wide_spec] * 2
        + [low_spec] * 3
        + [kept],
        out_specs=[pl.BlockSpec((tall, d), fixed, **once)] * 4 + [term_spec] * 2,
        scratch_shapes=[
            pltpu.VMEM((tokens, wide), BF),
            pltpu.VMEM((tokens, wide), BF),
            pltpu.VMEM((tokens, d), F32),
            pltpu.VMEM((tokens, PAD), F32),
            pltpu.SemaphoreType.DMA((10,)),
        ],
        out_shape=[shape((tall, d))] * 4 + [shape((RANK, slice_ff), F32)] * 2,
        compiler_params=params(60, 1),
        cost_estimate=cost(2 * tokens * d * slice_ff * 3, 50 * MIB),
        name="feed_back",
    )(me_ref, *seconds, *dys, feed_w, feed_w, down_w, silu, slope, dlt, rg, ru, lgu)
    second_parts, (term_gr, term_ur) = (back[:4], back[4:])

    down = pl.pallas_call(
        down_kernel,
        grid=(steps,),
        in_specs=[ANY] * 4 + [down_spec, wide_spec, low_spec, kept],
        out_specs=[pl.BlockSpec((rows, d), fixed, **once)] * 4
        + [term_spec, pl.BlockSpec((RANK, d), fixed)],
        scratch_shapes=[
            pltpu.VMEM((tokens, wide), BF),
            pltpu.VMEM((tokens, d), F32),
            pltpu.VMEM((tokens, PAD), F32),
            pltpu.SemaphoreType.DMA((5,)),
        ],
        out_shape=[shape((rows, d))] * 4 + [shape((RANK, slice_ff), F32), shape((RANK, d), F32)],
        compiler_params=params(56, 1),
        cost_estimate=cost(2 * tokens * d * slice_ff, 24 * MIB),
        name="down",
    )(*dys, down_w, after(act, second_parts), dlt, dr_pad)
    out_parts, (term_dl, term_dr) = (down[:4], down[4:])

    adapters = joint_left.shape[0]
    bits = halves.bit_length() - 1
    turned = [sum(((i >> b) & 1) << (bits - 1 - b) for b in range(bits)) for i in range(halves)]
    share = slice_ff // halves

    def by_slice(at):
        parts = []
        for source in range(halves):
            first_column = turned[source] * share
            for t in range(TP):
                for g in range(share // own_ff):
                    group = first_column // own_ff + g
                    to = (group * TP + t) * own_ff
                    parts.append((to, own_ff, ((source, t, at + g * own_ff),)))
        return tuple(parts)

    def by_t(at, size, base=0, count=halves):
        return tuple(
            (base + t * size, size, tuple((i, t, at) for i in range(count))) for t in range(TP)
        )

    def slotted(got, plan, widths, name):
        return pl.pallas_call(
            functools.partial(slot_kernel, plan, adapters),
            out_shape=[shape((adapters, RANK, size), F32) for size in widths],
            in_specs=[VM],
            out_specs=[VM] * len(widths),
            compiler_params=params(48),
            cost_estimate=cost(adapters * seqs * RANK * sum(widths), 64 * adapters * sum(widths)),
            name=name,
        )(got)

    def over_h(value):
        at = 1
        while at < halves:
            count = value.shape[1] // 2
            upper = (h // at) % 2
            keep = lax.dynamic_slice_in_dim(value, upper * count, count, 1)
            give = lax.dynamic_slice_in_dim(value, (1 - upper) * count, count, 1)
            value = keep + flip(give.astype(BF), "h", at).astype(F32)
            at *= 2
        return value

    id_columns = jnp.full((RANK, PAD), adapter_ids[0], F32)
    width = d // TP

    second_got, out_parts = together(sent(second_parts), out_parts)
    second_terms = sum(part[rows:, : 2 * width].astype(F32) for part in second_got)

    dmix, delta_residual = pl.pallas_call(
        out_back_kernel,
        grid_spec=pltpu.PrefetchScalarGridSpec(
            num_scalar_prefetch=1,
            grid=(TP,),
            in_specs=[pl.BlockSpec((tall, d), lambda r, m: (0, 0))] * 4
            + [pl.BlockSpec((rows, d), lambda r, m: (0, 0))] * 2
            + [
                pl.BlockSpec((1, d), lambda r, m: (0, 0)),
                pl.BlockSpec((RANK, d), lambda r, m: (0, 0)),
                pl.BlockSpec((RANK, qw), lambda r, m: (0, m[0] ^ r)),
                pl.BlockSpec((rows, RANK), lambda r, m: (0, 0)),
                pl.BlockSpec((qw, d), lambda r, m: (m[0] ^ r, 0)),
                pl.BlockSpec((1, rows, qw), lambda r, m: (r, 0, 0)),
                pl.BlockSpec((RANK, d), lambda r, m: (0, 0)),
            ],
            out_specs=[
                pl.BlockSpec((1, rows + 3 * RANK, qw), lambda r, m: (r, 0, 0)),
                pl.BlockSpec((rows, d), lambda r, m: (0, 0)),
            ],
            scratch_shapes=[
                pltpu.VMEM((rows, d), BF),
                pltpu.VMEM((rows, RANK), BF),
                pltpu.VMEM((2 * RANK, d), F32),
            ],
        ),
        out_shape=(shape((TP, rows + 3 * RANK, qw)), shape((rows, d), F32)),
        compiler_params=params(48, 1),
        cost_estimate=cost(2 * rows * d * d, 16 * MIB),
        name="out_back",
    )(me_ref, *second_got, dy, residual, norm_second[None], orr, olt, out_inner, out_w, mine, term_dr)

    slice_terms = after(jnp.concatenate([term_gr, term_ur, term_dl], axis=0), dmix)
    deltas, slice_terms = together(sent(dmix), over_h(slice_terms))
    mixed_terms = sum(part[rows:].astype(F32) for part in deltas)
    early_in = jnp.concatenate(
        [slice_terms[i * RANK : (i + 1) * RANK] for i in range(3)]
        + [second_terms]
        + [mixed_terms[i * RANK : (i + 1) * RANK] for i in range(3)]
        + [id_columns],
        axis=1,
    ).astype(BF)
    deltas, early_in = together(deltas, early_in)
    early = lax.all_gather(early_in, ("s", "h", "t")).reshape(seqs, halves, TP, RANK, -1)

    dq, dkv, dslot = pl.pallas_call(
        functools.partial(attend_back_kernel, tile, ranges),
        out_shape=(
            shape((tokens, qw)),
            shape((tokens, 2 * kw), F32),
            shape((key_rows - tokens, 2 * kw)),
        ),
        in_specs=[SM] + [VM] * 12,
        out_specs=(VM, VM, VM),
        scratch_shapes=[
            pltpu.VMEM((tokens, qw), BF),
            pltpu.VMEM((tokens, qw), BF),
            pltpu.VMEM((key_rows, 2 * kw), F32),
        ],
        compiler_params=params(56),
        cost_estimate=cost(10 * pairs_done * HEAD_DIM, 12 * MIB, pairs_done),
        name="attend_back",
    )(me_ref, q, kv_all, query_marks, key_marks, lse, mixed, *deltas, cosine, sine)

    out_got = sent(after(out_parts, deltas))
    dslot = after(dslot, out_got[1:3])
    returned = [
        lax.ppermute(dslot[i * span : (i + 1) * span], "h", [(b, a) for a, b in pairs])
        for i, (shift, side, pairs) in enumerate(slots)
    ]
    layer_output = (
        residual
        + (out_got[0].astype(F32) + out_got[1].astype(F32))
        + (out_got[2].astype(F32) + out_got[3].astype(F32))
    ).astype(BF)[None]
    sides = tuple(side for _, side, _ in slots)
    dj, joint_deltas, term_jr, term_jl = pl.pallas_call(
        functools.partial(joint_terms_kernel, sides),
        out_shape=[
            shape((tokens, cols)),
            shape((tokens, PAD)),
            shape((RANK, cols), F32),
            shape((RANK, d), F32),
        ],
        in_specs=[SM] + [VM] * (2 + len(sides) + 8),
        out_specs=[VM] * 4,
        scratch_shapes=[pltpu.VMEM((tokens, 2 * kw), BF)],
        compiler_params=params(56),
        cost_estimate=cost(tokens * d * cols // 4, 12 * MIB),
        name="joint_terms",
    )(me_ref, dq, dkv, *returned, cosine, sine, jr_pad, *firsts)
    left_parts = [
        lax.dynamic_slice_in_dim(term_jl, (me ^ r) * width, width, 1).astype(BF) for r in range(TP)
    ]
    left_sent = sent(left_parts)
    first_parts = pl.pallas_call(
        joint_back_kernel,
        out_shape=[shape((rows, d))] * 4,
        in_specs=[SM] + [ANY] + [VM] * 3,
        out_specs=[VM] * 4,
        scratch_shapes=[pltpu.VMEM((d, cols), BF), pltpu.SemaphoreType.DMA((1,))],
        compiler_params=params(56),
        cost_estimate=cost(2 * tokens * d * cols, 16 * MIB),
        name="joint_back",
    )(me_ref, joint_w, dj, after(joint_deltas, out_got), jlt_pad)

    got = sent(first_parts)
    early = after(early, got[1:3])
    d_gr, d_ur, d_dl, d_gl, d_ul, d_dr, d_or, d_ol = slotted(
        early,
        tuple(by_slice(i * share) for i in range(3))
        + tuple(by_t(3 * share + i * width, width) for i in range(5)),
        (ff, ff, ff, d, d, d, d, d),
        "slots_early",
    )
    late = jnp.concatenate([sum(part.astype(F32) for part in left_sent), term_jr], axis=1)
    late = after(late, (got[1:3], d_gr))
    at = 1
    while at < halves:
        late = late + flip(late.astype(BF), "h", at).astype(F32)
        at *= 2
    late = jnp.concatenate([late, id_columns], axis=1).astype(BF)[None]
    at = 1
    while at < seqs:
        other = flip(late, "s", at)
        upper = (s_at // at) % 2 == 1
        late = jnp.concatenate(
            [jnp.where(upper, other, late), jnp.where(upper, late, other)], axis=0
        )
        at *= 2
    late_got = [late, swap(late, 1), swap(late, 2), swap(late, 3)]
    low = [jnp.where(me % 2 == 1, late_got[i ^ 1], late_got[i]) for i in range(TP)]
    late = jnp.stack([jnp.where(me >= 2, low[i ^ 2], low[i]) for i in range(TP)], axis=1)[:, None]
    delta_first = (got[0].astype(F32) + got[1].astype(F32)) + (
        got[2].astype(F32) + got[3].astype(F32)
    )
    input_delta = (delta_residual + norm_back(x32, norm_first, delta_first)).astype(BF)[None]
    d_jl, d_jr = slotted(
        late,
        (
            by_t(0, width, 0, 1),
            by_t(width, qw, 0, 1)
            + by_t(width + qw, kw, q_end, 1)
            + by_t(width + qw + kw, kw, k_end, 1),
        ),
        (d, HEADS * HEAD_DIM + 2 * KV_HEADS * HEAD_DIM),
        "slots_late",
    )

    def left(value):
        return jnp.swapaxes(value, 1, 2)

    return (
        layer_output,
        input_delta,
        left(d_jl),
        d_jr,
        left(d_ol),
        d_or,
        left(d_gl),
        d_gr,
        left(d_ul),
        d_ur,
        left(d_dl),
        d_dr,
    )


def solution(mesh):
    seqs, ctx = (mesh.shape["seq"], mesh.shape["ctx"])
    inner = Mesh(mesh.devices.reshape(seqs, ctx // TP, TP), ("s", "h", "t"))
    acts = P("s", ("h", "t"), None)
    weight = P(("s", "h", "t"), None)
    placed = (
        (acts, acts, P(), P())
        + (weight,) * 5
        + (P(),) * 10
        + (P("s", None), P("s"))
    )
    return jax.shard_map(
        per_device,
        mesh=inner,
        in_specs=placed,
        out_specs=(acts, acts) + (P(),) * 10,
        check_vma=False,
    )
```
